32 devices in a mesh: row: 16 (over z, y, x), mem: 2 (over core).
Axes of the slice: x: 2, y: 2, z: 4, core: 2. Of those that a mesh axis runs over, the one named last changes fastest.
Arguments:
- inputs: bfloat16 [16384, 1024], P(('row', 'mem')), may hold values from -6 to 6
- memory: bfloat16 [8192, 1024], P(('row', 'mem')), may hold values from -6 to 6
- target_seg: int32 [16384], P(('row', 'mem')), may hold values from 0 to 7, as said below
- memory_seg: int32 [8192], P(('row', 'mem')), may hold values from 0 to 7, as said below
- self_query: bfloat16 [1024, 1024], replicated, may hold values from -0.1875 to 0.1875
- self_key: bfloat16 [1024, 1024], replicated, may hold values from -0.1875 to 0.1875
- self_value: bfloat16 [1024, 1024], replicated, may hold values from -0.1875 to 0.1875
- self_out: bfloat16 [1024, 1024], replicated, may hold values from -1.5 to 1.5
- cross_query: bfloat16 [1024, 1024], replicated, may hold values from -0.1875 to 0.1875
- cross_key: bfloat16 [1024, 1024], replicated, may hold values from -0.1875 to 0.1875
- cross_value: bfloat16 [1024, 1024], replicated, may hold values from -0.1875 to 0.1875
- cross_out: bfloat16 [1024, 1024], replicated, may hold values from -3 to 3
- expand_weight: bfloat16 [1024, 4096], replicated, may hold values from -0.1875 to 0.1875
- contract_weight: bfloat16 [4096, 1024], replicated, may hold values from -0.5 to 0.5
- norm_params: float32 [6, 1024], replicated, may hold values from -3 to 3, as said below
- out_grad: bfloat16 [16384, 1024], P(('row', 'mem')), may hold values from -6 to 6
Outputs:
- layer_out: bfloat16 [16384, 1024], P(('row', 'mem'))
- input_grad: bfloat16 [16384, 1024], P(('row', 'mem'))
- memory_grad: bfloat16 [8192, 1024], P(('row', 'mem'))
- self_query_grad: float32 [1024, 1024], P('row', 'mem')
- self_key_grad: float32 [1024, 1024], P('row', 'mem')
- self_value_grad: float32 [1024, 1024], P('row', 'mem')
- self_out_grad: float32 [1024, 1024], P('row', 'mem')
- cross_query_grad: float32 [1024, 1024], P('row', 'mem')
- cross_key_grad: float32 [1024, 1024], P('row', 'mem')
- cross_value_grad: float32 [1024, 1024], P('row', 'mem')
- cross_out_grad: float32 [1024, 1024], P('row', 'mem')
- expand_weight_grad: float32 [1024, 4096], P('row', 'mem')
- contract_weight_grad: float32 [4096, 1024], P('row', 'mem')
- norm_grad: float32 [6, 1024], P('mem', 'row')
The draws below stay inside these ranges and needn't reach their ends.
Inputs may be any that keep to these rules, and one draw needn't show every extreme that they name: `target_seg`: the rows of each device hold 4 whole target sequences one after another; ids count the sequences of the devices of one index of row from 0 upward in row order. `memory_seg`: within one index of row, memory ids never fall and every target sequence of that index has one memory row or more with its id; no memory sequence but the first of an index begins at a device's first memory row. `norm_params`: rows 0, 2, 4 are positive gains, rows 1, 3, 5 biases.
All inputs are finite; a program needn't handle non-finite values.
Results may differ from the reference program's by a relative error of at most 0.025.
Values may be sent and summed in bfloat16 or wider, within the bound.
No kernel may reach another device: no remote copies, remote signals or barrier semaphores. Data moves between devices by JAX's collectives and lax.ppermute only.
A program may use at most 256 MiB of HBM per device.

```python
from functools import partial
import jax
import jax.numpy as jnp
from jax import lax

D = 1024
HEADS = 16
HEAD_DIM = 64
FF = 4096
TOK_DEV = 512
MEM_DEV = 256
SEQ_DEV = 4
TOKENS = 16384
MTOKENS = 8192
N_MEM = 2


def draw_target_seg(key, part):
    key = jax.random.fold_in(key, 11)
    device_count = TOKENS // TOK_DEV
    cut_count = SEQ_DEV - 1
    raw_draw = jax.random.randint(key, (device_count, cut_count), 0, 32768)
    skewed = raw_draw * raw_draw // 32768
    places = 1 + skewed * (TOK_DEV - SEQ_DEV) // 32768
    places = jnp.sort(places, axis=1) + jnp.arange(cut_count, dtype=jnp.int32)[None, :]
    positions = jnp.arange(TOK_DEV, dtype=jnp.int32)
    local_ids = jnp.sum((positions[None, :, None] >= places[:, None, :]).astype(jnp.int32), -1)
    offsets = jnp.arange(device_count, dtype=jnp.int32) % N_MEM * SEQ_DEV
    return (local_ids + offsets[:, None]).reshape(-1).astype(jnp.int32)


def memory_order(key_row, candidate_count):
    return jax.random.permutation(key_row, candidate_count)


def draw_memory_seg(key, part):
    key = jax.random.fold_in(key, 23)
    pair_memory = N_MEM * MEM_DEV
    pair_count = MTOKENS // pair_memory
    cut_count = N_MEM * SEQ_DEV - 1
    candidate_count = pair_memory - N_MEM
    orders = jax.vmap(partial(memory_order, candidate_count=candidate_count))(jax.random.split(key, pair_count))
    chosen = jnp.sort(orders[:, :cut_count], axis=1).astype(jnp.int32)
    places = chosen + 1 + chosen // (MEM_DEV - 1)
    positions = jnp.arange(pair_memory, dtype=jnp.int32)
    segment_ids = jnp.sum((positions[None, :, None] >= places[:, None, :]).astype(jnp.int32), -1)
    return segment_ids.reshape(-1).astype(jnp.int32)


def draw_norm_params(key, part):
    key = jax.random.fold_in(key, 37)
    noise = jnp.clip(jax.random.normal(key, (6, D), jnp.float32), -5.0, 5.0)
    parity = jnp.arange(6, dtype=jnp.int32)[:, None] % 2
    return jnp.where(parity == 0, 1.0 + 0.15 * noise, 0.4 * noise).astype(jnp.float32)


def levels(stream_key, shape, cuts, low, top_value):
    level = 1.0
    for axis_at, parts in cuts:
        draws = jax.random.uniform(jax.random.fold_in(jax.random.fold_in(stream_key, 6), axis_at), (parts,), jnp.float32, low / len(cuts), top_value / len(cuts))
        level = level * jnp.repeat(jnp.exp(draws), shape[axis_at] // parts).reshape((-1,) + (1,) * (len(shape) - 1 - axis_at))
    return level


def normal_values(rng, extent, width, reach, cuts=(), held_as=jnp.bfloat16):
    values = width * jax.random.normal(rng, extent, jnp.float32)
    if cuts:
        values = values * levels(rng, extent, cuts, -0.22, 0.18)
    return jnp.clip(values, -reach, reach).astype(held_as)


def setup_inputs(seed: int = 0) -> dict:
    keys = jax.random.split(jax.random.key(seed), 17)
    inputs = normal_values(keys[0], (TOKENS, D), 1.0, 6.0, ((0, 32),))
    memory = normal_values(keys[1], (MTOKENS, D), 1.0, 6.0, ((0, 32),))
    target_seg = draw_target_seg(jax.random.fold_in(keys[16], 71), 0)
    memory_seg = draw_memory_seg(jax.random.fold_in(keys[16], 71), 0)
    self_query = normal_values(keys[4], (D, D), D ** -0.5, 0.1875)
    self_key = normal_values(keys[5], (D, D), D ** -0.5, 0.1875)
    self_value = normal_values(keys[6], (D, D), D ** -0.5, 0.1875)
    self_out = normal_values(keys[7], (D, D), (max(D // 64, 1)) ** -0.5, 1.5)
    cross_query = normal_values(keys[8], (D, D), D ** -0.5, 0.1875)
    cross_key = normal_values(keys[9], (D, D), D ** -0.5, 0.1875)
    cross_value = normal_values(keys[10], (D, D), D ** -0.5, 0.1875)
    cross_out = normal_values(keys[11], (D, D), (max(D // 256, 1)) ** -0.5, 3.0)
    expand_weight = normal_values(keys[12], (D, FF), D ** -0.5, 0.1875)
    contract_weight = normal_values(keys[13], (FF, D), (FF // 32) ** -0.5, 0.5)
    norm_params = draw_norm_params(jax.random.fold_in(keys[16], 71), 0)
    out_grad = normal_values(keys[15], (TOKENS, D), 1.0, 6.0, ((0, 32),))
    return dict(inputs=inputs, memory=memory, target_seg=target_seg, memory_seg=memory_seg, self_query=self_query, self_key=self_key, self_value=self_value, self_out=self_out, cross_query=cross_query, cross_key=cross_key, cross_value=cross_value, cross_out=cross_out, expand_weight=expand_weight, contract_weight=contract_weight, norm_params=norm_params, out_grad=out_grad)


ALPHA = 300.0 ** 0.25
SCALE = 0.125
NEG = -1e+30
EPS = 1e-05
HIGH = lax.Precision.HIGHEST

@jax.custom_vjp
def low(v):
    return lax.optimization_barrier(v.astype(jnp.bfloat16)).astype(jnp.float32)

@jax.custom_vjp
def low_back(v):
    return v

def low_keep(v):
    return (low(v), None)

def low_pass(kept, grad):
    return (grad,)

def back_keep(v):
    return (v, None)

def back_low(kept, grad):
    return (low(grad),)
low.defvjp(low_keep, low_pass)
low_back.defvjp(back_keep, back_low)

def layer_norm(tensor, gain_row, bias_row):
    middle = lax.optimization_barrier(jnp.mean(tensor, -1, keepdims=True))
    centred = tensor - middle
    spread = lax.optimization_barrier(jnp.mean(centred * centred, -1, keepdims=True))
    return centred * lax.rsqrt(spread + EPS) * gain_row + bias_row

def gelu_exact(tensor):
    return jax.nn.gelu(tensor, approximate=False)

def product(left_side, right_side):
    return jnp.dot(left_side, right_side, precision=HIGH, preferred_element_type=jnp.float32)

def rounded_product(left_side, right_side):
    return low_back(low(product(left_side, right_side)))

def attend(queries, key_rows, value_rows, query_seg, key_seg, causal):
    row_count = queries.shape[0]
    block_rows = min(512, row_count)
    block_count = row_count // block_rows
    query_blocks = queries.reshape(block_count, block_rows, HEADS, HEAD_DIM)
    seg_blocks = query_seg.reshape(block_count, block_rows)
    starts = jnp.arange(block_count, dtype=jnp.int32) * block_rows
    key_heads = key_rows.reshape(-1, HEADS, HEAD_DIM)
    value_heads = value_rows.reshape(-1, HEADS, HEAD_DIM)
    key_pos = jnp.arange(key_heads.shape[0], dtype=jnp.int32)

    def one_block(block_items):
        query_block, seg_block, start_row = block_items
        raw_scores = jnp.einsum('qhd,khd->hqk', query_block, key_heads, precision=HIGH)
        scores = low_back(raw_scores * SCALE)
        allowed = seg_block[:, None] == key_seg[None, :]
        if causal:
            row_pos = start_row + jnp.arange(block_rows, dtype=jnp.int32)
            allowed = allowed & (row_pos[:, None] >= key_pos[None, :])
        scores = jnp.where(allowed[None], scores, NEG)
        row_top = lax.optimization_barrier(jnp.max(scores, -1, keepdims=True))
        log_total = row_top + jnp.log(lax.optimization_barrier(jnp.sum(jnp.exp(scores - row_top), -1, keepdims=True)))
        prob_block = jnp.exp(scores - log_total)
        return jnp.einsum('hqk,khd->qhd', low(prob_block), value_heads, precision=HIGH)
    outputs = lax.map(jax.checkpoint(one_block), (query_blocks, seg_blocks, starts))
    return outputs.reshape(row_count, HEADS * HEAD_DIM)

def pair_layer(weight_values, norm_values, inputs, memory, target_seg, memory_seg):
    self_query, self_key, self_value, self_out, cross_query, cross_key, cross_value, cross_out, expand_weight, contract_weight = weight_values
    queries = rounded_product(inputs, self_query)
    key_rows = rounded_product(inputs, self_key)
    value_rows = rounded_product(inputs, self_value)
    attended = low_back(low(attend(queries, key_rows, value_rows, target_seg, target_seg, True)))
    first_sum = ALPHA * inputs + low_back(product(attended, self_out))
    hidden_one = layer_norm(first_sum, norm_values[0], norm_values[1])
    cross_queries = rounded_product(low(hidden_one), cross_query)
    memory_keys = rounded_product(memory, cross_key)
    memory_values = rounded_product(memory, cross_value)
    crossed = low_back(low(attend(cross_queries, memory_keys, memory_values, target_seg, memory_seg, False)))
    second_sum = ALPHA * hidden_one + low_back(product(crossed, cross_out))
    hidden_two = layer_norm(second_sum, norm_values[2], norm_values[3])
    pre_active = low_back(product(low(hidden_two), expand_weight))
    activated = low(gelu_exact(pre_active))
    third_sum = ALPHA * hidden_two + low_back(product(activated, contract_weight))
    return layer_norm(third_sum, norm_values[4], norm_values[5])

def reference(inputs, memory, target_seg, memory_seg, self_query, self_key, self_value, self_out, cross_query, cross_key, cross_value, cross_out, expand_weight, contract_weight, norm_params, out_grad):
    weights = tuple((weight.astype(jnp.float32) for weight in (self_query, self_key, self_value, self_out, cross_query, cross_key, cross_value, cross_out, expand_weight, contract_weight)))
    group_rows = N_MEM * TOK_DEV
    group_memory = N_MEM * MEM_DEV
    group_count = TOKENS // group_rows
    target_groups = target_seg.reshape(group_count, group_rows)
    memory_groups = memory_seg.reshape(group_count, group_memory)

    def forward(input_values, memory_values, weight_values, norm_values):

        def one_group(group_items):
            group_inputs, group_memory_rows, group_target, group_mem_seg = group_items
            return pair_layer(weight_values, norm_values, group_inputs, group_memory_rows, group_target, group_mem_seg)
        layered = lax.map(jax.checkpoint(one_group), (input_values.reshape(group_count, group_rows, D), memory_values.reshape(group_count, group_memory, D), target_groups, memory_groups))
        return layered.reshape(TOKENS, D)
    layer_value, pull_back = jax.vjp(forward, inputs.astype(jnp.float32), memory.astype(jnp.float32), weights, norm_params)
    input_back, memory_back, weight_backs, norm_back = pull_back(out_grad.astype(jnp.float32))
    return (layer_value.astype(jnp.bfloat16), input_back.astype(jnp.bfloat16), memory_back.astype(jnp.bfloat16), weight_backs[0], weight_backs[1], weight_backs[2], weight_backs[3], weight_backs[4], weight_backs[5], weight_backs[6], weight_backs[7], weight_backs[8], weight_backs[9], norm_back)
```

```python
from functools import partial

import jax
import jax.numpy as jnp
from jax import lax
from jax.sharding import PartitionSpec as P

HEADS = 16
HEAD_DIM = 64


ALPHA = 300.0**0.25
SCALE = 0.125
NEG = -1e30
EPS = 1e-05


def layer_norm(tensor, gain_row, bias_row):
    middle = jnp.mean(tensor, -1, keepdims=True)
    centred = tensor - middle
    spread = jnp.mean(centred * centred, -1, keepdims=True)
    return centred * lax.rsqrt(spread + EPS) * gain_row + bias_row


def gelu_exact(tensor):
    return jax.nn.gelu(tensor, approximate=False)


def project(left_side, right_side):
    return jnp.dot(left_side, right_side, preferred_element_type=jnp.float32)


def weight_grad(left_side, right_side):
    return jnp.einsum("rd,re->de", left_side, right_side, preferred_element_type=jnp.float32)


def back_project(grad_rows, weight):
    return jnp.einsum("re,de->rd", grad_rows, weight, preferred_element_type=jnp.float32)


def split_heads(tensor):
    return tensor.reshape(tensor.shape[0], HEADS, HEAD_DIM)


def join_heads(tensor):
    return tensor.reshape(tensor.shape[0], HEADS * HEAD_DIM)


def to_blocks(tensor, block_rows):
    return tensor.reshape((tensor.shape[0] // block_rows, block_rows) + tensor.shape[1:])


def masked_scores(query_block, key_heads, row_seg, key_seg, row_pos, key_pos):
    raw_scores = (
        jnp.einsum("qhd,khd->hqk", query_block, key_heads, preferred_element_type=jnp.float32)
        * SCALE
    )
    allowed = row_seg[:, None] == key_seg[None, :]
    if row_pos is not None:
        allowed = allowed & (row_pos[:, None] >= key_pos[None, :])
    return jnp.where(allowed[None], raw_scores, NEG)


def self_forward(queries, key_heads, value_heads, segments):
    row_count = queries.shape[0]
    positions = jnp.arange(row_count, dtype=jnp.int32)
    scores = masked_scores(queries, key_heads, segments, segments, positions, positions)
    row_top = jnp.max(scores, -1, keepdims=True)
    log_total = row_top + jnp.log(jnp.sum(jnp.exp(scores - row_top), -1, keepdims=True))
    prob_block = jnp.exp(scores - log_total).astype(jnp.bfloat16)
    outputs = jnp.einsum(
        "hqk,khd->qhd", prob_block, value_heads, preferred_element_type=jnp.float32
    )
    return (outputs, log_total)


def self_backward(queries, key_heads, value_heads, segments, log_totals, grad_heads):
    row_count = queries.shape[0]
    block_rows = min(512, row_count)
    positions = jnp.arange(row_count, dtype=jnp.int32)
    key_sum = jnp.zeros(key_heads.shape, jnp.float32)
    value_sum = jnp.zeros(value_heads.shape, jnp.float32)
    scores = masked_scores(queries, key_heads, segments, segments, positions, positions)
    prob_block = jnp.exp(scores - log_totals)
    grad_probs = jnp.einsum(
        "qhd,khd->hqk", grad_heads, value_heads, preferred_element_type=jnp.float32
    )
    row_delta = jnp.sum(prob_block * grad_probs, -1, keepdims=True)
    grad_scores = (prob_block * (grad_probs - row_delta)).astype(jnp.bfloat16)
    query_parts = (
        jnp.einsum("hqk,khd->qhd", grad_scores, key_heads, preferred_element_type=jnp.float32)
        * SCALE
    )
    key_sum = key_sum.at[:block_rows].add(
        jnp.einsum("hqk,qhd->khd", grad_scores, queries, preferred_element_type=jnp.float32) * SCALE
    )
    value_sum = value_sum.at[:block_rows].add(
        jnp.einsum(
            "hqk,qhd->khd",
            prob_block.astype(jnp.bfloat16),
            grad_heads,
            preferred_element_type=jnp.float32,
        )
    )
    return (query_parts, key_sum, value_sum)


def halving_orders(bit_count):
    plain = list(range(bit_count))
    third = max(bit_count // 3, 1)
    return [plain, plain[third:] + plain[:third], plain[2 * third :] + plain[: 2 * third]]


def swap_mem(tensor):
    return lax.ppermute(tensor, "mem", [(0, 1), (1, 0)])


def scatter_sum(blocks, order, row_count):
    bit_count = len(order)
    me = lax.axis_index("row")
    rest = blocks.shape[1:]
    current = blocks
    left = list(range(bit_count - 1, -1, -1))
    for bit in order:
        at = left.index(bit)
        high = 2**at
        low = 2 ** (len(left) - at - 1)
        view = current.reshape((high, 2, low) + rest)
        mine = (me >> bit) & 1
        keep = lax.dynamic_index_in_dim(view, mine, 1, keepdims=False).reshape((high * low,) + rest)
        send = lax.dynamic_index_in_dim(view, 1 - mine, 1, keepdims=False).reshape(
            (high * low,) + rest
        )
        pairs = [(i, i ^ (1 << bit)) for i in range(row_count)]
        got = lax.ppermute(send, "row", pairs)
        left.remove(bit)
        total = keep.astype(jnp.float32) + got.astype(jnp.float32)
        current = total.astype(jnp.bfloat16) if left else total
    return current[0]


def pair_half(wgrad):
    half = wgrad.shape[1] // 2
    core = lax.axis_index("mem")
    low = wgrad.astype(jnp.bfloat16)
    keep = lax.dynamic_slice_in_dim(low, core * half, half, 1)
    send = lax.dynamic_slice_in_dim(low, (1 - core) * half, half, 1)
    got = swap_mem(send)
    return (keep.astype(jnp.float32) + got.astype(jnp.float32)).astype(jnp.bfloat16)


def pair_norm(norm_wgrad, core):
    low = norm_wgrad.astype(jnp.bfloat16)
    keep = lax.dynamic_slice_in_dim(low, core * 3, 3, 0)
    got = swap_mem(lax.dynamic_slice_in_dim(low, (1 - core) * 3, 3, 0))
    return (keep.astype(jnp.float32) + got.astype(jnp.float32)).astype(jnp.bfloat16)


def cross_forward(queries, key_heads, value_heads, row_seg, key_seg):
    scores = masked_scores(queries, key_heads, row_seg, key_seg, None, None)
    row_top = jnp.max(scores, -1, keepdims=True)
    log_total = row_top + jnp.log(jnp.sum(jnp.exp(scores - row_top), -1, keepdims=True))
    prob_block = jnp.exp(scores - log_total).astype(jnp.bfloat16)
    outputs = jnp.einsum("hqk,khd->qhd", prob_block, value_heads, preferred_element_type=jnp.float32)
    return (outputs, log_total)


def cross_backward(queries, key_heads, value_heads, row_seg, key_seg, log_totals, grad_heads):
    scores = masked_scores(queries, key_heads, row_seg, key_seg, None, None)
    prob_block = jnp.exp(scores - log_totals)
    grad_probs = jnp.einsum("qhd,khd->hqk", grad_heads, value_heads, preferred_element_type=jnp.float32)
    row_delta = jnp.sum(prob_block * grad_probs, -1, keepdims=True)
    grad_scores = (prob_block * (grad_probs - row_delta)).astype(jnp.bfloat16)
    query_parts = jnp.einsum("hqk,khd->qhd", grad_scores, key_heads, preferred_element_type=jnp.float32) * SCALE
    key_sum = jnp.einsum("hqk,qhd->khd", grad_scores, queries, preferred_element_type=jnp.float32) * SCALE
    value_sum = jnp.einsum("hqk,qhd->khd", prob_block.astype(jnp.bfloat16), grad_heads, preferred_element_type=jnp.float32)
    return (query_parts, key_sum, value_sum)


def shards(
    row_count,
    inputs,
    memory,
    target_seg,
    memory_seg,
    self_query,
    self_key,
    self_value,
    self_out,
    cross_query,
    cross_key,
    cross_value,
    cross_out,
    expand_weight,
    contract_weight,
    norm_params,
    out_grad,
):
    inputs_wide = inputs.astype(jnp.float32)
    mem_rows = memory.shape[0]
    pair_memory = jnp.concatenate([memory, swap_mem(memory)])
    pair_seg = jnp.concatenate([memory_seg, swap_mem(memory_seg)])
    queries = split_heads(project(inputs, self_query).astype(jnp.bfloat16))
    key_rows = split_heads(project(inputs, self_key).astype(jnp.bfloat16))
    value_rows = split_heads(project(inputs, self_value).astype(jnp.bfloat16))
    attended, self_totals = self_forward(queries, key_rows, value_rows, target_seg)
    attended_low = join_heads(attended).astype(jnp.bfloat16)
    first_sum = ALPHA * inputs_wide + project(attended_low, self_out)
    hidden_one, norm_back_one = jax.vjp(layer_norm, first_sum, norm_params[0], norm_params[1])
    hidden_one_low = hidden_one.astype(jnp.bfloat16)
    cross_queries = project(hidden_one_low, cross_query).astype(jnp.bfloat16)
    key_heads = split_heads(project(pair_memory, cross_key).astype(jnp.bfloat16))
    value_heads = split_heads(project(pair_memory, cross_value).astype(jnp.bfloat16))
    query_heads = split_heads(cross_queries)
    crossed, cross_totals = cross_forward(query_heads, key_heads, value_heads, target_seg, pair_seg)
    cross_values = join_heads(crossed).astype(jnp.bfloat16)
    second_sum = ALPHA * hidden_one + project(cross_values, cross_out)
    hidden_two, norm_back_two = jax.vjp(layer_norm, second_sum, norm_params[2], norm_params[3])
    hidden_two_low = hidden_two.astype(jnp.bfloat16)
    pre_active = project(hidden_two_low, expand_weight)
    activated, gelu_back = jax.vjp(gelu_exact, pre_active)
    activated_low = activated.astype(jnp.bfloat16)
    third_sum = ALPHA * hidden_two + project(activated_low, contract_weight)
    layer_value, norm_back_three = jax.vjp(layer_norm, third_sum, norm_params[4], norm_params[5])
    layer_out = layer_value.astype(jnp.bfloat16)
    third_grad, gain_three, bias_three = norm_back_three(out_grad.astype(jnp.float32))
    branch_three = third_grad.astype(jnp.bfloat16)
    contract_back = weight_grad(activated_low, branch_three)
    (active_grad,) = gelu_back(back_project(branch_three, contract_weight))
    active_low = active_grad.astype(jnp.bfloat16)
    expand_back = weight_grad(hidden_two_low, active_low)
    hidden_two_grad = ALPHA * third_grad + back_project(active_low, expand_weight)
    second_grad, gain_two, bias_two = norm_back_two(hidden_two_grad)
    branch_two = second_grad.astype(jnp.bfloat16)
    cross_out_back = weight_grad(cross_values, branch_two)
    cross_grad = back_project(branch_two, cross_out).astype(jnp.bfloat16)
    query_parts, key_sum, value_sum = cross_backward(
        query_heads, key_heads, value_heads, target_seg, pair_seg, cross_totals, split_heads(cross_grad)
    )
    query_sum = join_heads(query_parts).astype(jnp.bfloat16)
    memory_key_back = join_heads(key_sum).astype(jnp.bfloat16)
    memory_value_back = join_heads(value_sum).astype(jnp.bfloat16)
    cross_query_wgrad = weight_grad(hidden_one_low, query_sum)
    cross_key_wgrad = weight_grad(pair_memory, memory_key_back)
    cross_value_wgrad = weight_grad(pair_memory, memory_value_back)
    memory_parts = back_project(memory_key_back, cross_key) + back_project(
        memory_value_back, cross_value
    )
    memory_grad = (
        memory_parts[:mem_rows]
        + swap_mem(memory_parts[mem_rows:].astype(jnp.bfloat16)).astype(jnp.float32)
    ).astype(jnp.bfloat16)
    hidden_one_grad = ALPHA * second_grad + back_project(query_sum, cross_query)
    first_grad, gain_one, bias_one = norm_back_one(hidden_one_grad)
    branch_one = first_grad.astype(jnp.bfloat16)
    self_out_wgrad = weight_grad(attended_low, branch_one)
    attended_grad = split_heads(back_project(branch_one, self_out).astype(jnp.bfloat16))
    query_heads_back, key_heads_back, value_heads_back = self_backward(
        queries, key_rows, value_rows, target_seg, self_totals, attended_grad
    )
    self_query_back = join_heads(query_heads_back).astype(jnp.bfloat16)
    self_key_back = join_heads(key_heads_back).astype(jnp.bfloat16)
    self_value_back = join_heads(value_heads_back).astype(jnp.bfloat16)
    self_query_wgrad = weight_grad(inputs, self_query_back)
    self_key_wgrad = weight_grad(inputs, self_key_back)
    self_value_wgrad = weight_grad(inputs, self_value_back)
    input_grad = (
        ALPHA * first_grad
        + back_project(self_query_back, self_query)
        + back_project(self_key_back, self_key)
        + back_project(self_value_back, self_value)
    ).astype(jnp.bfloat16)
    norm_wgrad = jnp.stack([gain_one, bias_one, gain_two, bias_two, gain_three, bias_three])
    orders = halving_orders(row_count.bit_length() - 1)
    small = (
        self_query_wgrad,
        self_key_wgrad,
        self_value_wgrad,
        self_out_wgrad,
        cross_query_wgrad,
        cross_key_wgrad,
        cross_value_wgrad,
        cross_out_back,
        expand_back,
        contract_back,
    )
    choice = (0, 1, 2, 0, 1, 2, 0, 1, 1, 0)
    summed = []
    for wgrad, which in zip(small, choice):
        half = pair_half(wgrad)
        blocks = half.reshape(row_count, half.shape[0] // row_count, half.shape[1])
        summed.append(scatter_sum(blocks, orders[which], row_count))
    core = lax.axis_index("mem")
    norm_half = pair_norm(norm_wgrad, core)
    norm_blocks = norm_half.reshape(3, row_count, norm_half.shape[1] // row_count).transpose(1, 0, 2)
    summed.append(scatter_sum(norm_blocks, orders[2], row_count))
    return (
        layer_out,
        input_grad,
        memory_grad,
        summed[0],
        summed[1],
        summed[2],
        summed[3],
        summed[4],
        summed[5],
        summed[6],
        summed[7],
        summed[8],
        summed[9],
        summed[10],
    )


def solution(mesh):
    in_specs = (
        P(("row", "mem"), None),
        P(("row", "mem"), None),
        P(("row", "mem")),
        P(("row", "mem")),
        P(),
        P(),
        P(),
        P(),
        P(),
        P(),
        P(),
        P(),
        P(),
        P(),
        P(),
        P(("row", "mem"), None),
    )
    out_specs = (
        P(("row", "mem"), None),
        P(("row", "mem"), None),
        P(("row", "mem"), None),
        P("row", "mem"),
        P("row", "mem"),
        P("row", "mem"),
        P("row", "mem"),
        P("row", "mem"),
        P("row", "mem"),
        P("row", "mem"),
        P("row", "mem"),
        P("row", "mem"),
        P("row", "mem"),
        P("mem", "row"),
    )
    return jax.shard_map(partial(shards, mesh.shape["row"]), mesh=mesh, in_specs=in_specs, out_specs=out_specs, check_vma=False)
```

```python
import math
from functools import partial

import jax
import jax.numpy as jnp
import numpy as np
from jax import lax
from jax.experimental import pallas as pl
from jax.experimental.pallas import tpu as pltpu
from jax.sharding import PartitionSpec as P

HEADS = 16
HEAD_DIM = 64
GROUP = 256
PAIR = 128

ALPHA = 300.0**0.25
SCALE = 0.125
NEG = -1e30
EPS = 1e-05

ERFC_SLOPE = 0.3
ERFC_TERMS = (
    0.16918800133874554,
    0.17071528857689505,
    0.14833875833407398,
    0.2149275739002705,
    -0.09465408961006916,
    0.5477246520897923,
    -0.5122819409407986,
    0.4855649934109654,
    -0.12952325668594952,
)

BF = jnp.bfloat16
F32 = jnp.float32
VMEM_LIMIT = 56 * 2**20


def mul(left, right, left_axis, right_axis):
    return lax.dot_general(
        left, right, (((left_axis,), (right_axis,)), ((), ())), preferred_element_type=F32
    )


def mul_nn(left, right):
    return mul(left, right, 1, 0)


def mul_nt(left, right):
    return mul(left, right, 1, 1)


def mul_tn(left, right):
    return mul(left, right, 0, 0)


def kernel_call(body, grid, in_specs, out_specs, out_shape, scratch, flops, moved, scalars=0):
    return pl.pallas_call(
        body,
        grid_spec=pltpu.PrefetchScalarGridSpec(
            num_scalar_prefetch=scalars,
            grid=grid,
            in_specs=in_specs,
            out_specs=out_specs,
            scratch_shapes=scratch,
        ),
        out_shape=out_shape,
        compiler_params=pltpu.CompilerParams(vmem_limit_bytes=VMEM_LIMIT),
        cost_estimate=pl.CostEstimate(
            flops=int(flops), bytes_accessed=int(moved), transcendentals=0
        ),
    )


def whole(shape):
    return pl.BlockSpec(shape, lambda *_: (0,) * len(shape))


def shape_of(shape, dtype):
    return jax.ShapeDtypeStruct(shape, dtype)


def by_rows(rows, step, body):
    def one(at, carry):
        body(pl.ds(pl.multiple_of(at * step, step), step))
        return carry

    lax.fori_loop(0, rows // step, one, 0)


def normalize(value):
    middle = jnp.mean(value, -1, keepdims=True)
    centred = value - middle
    spread = jnp.mean(centred * centred, -1, keepdims=True)
    inverse = lax.rsqrt(spread + EPS)
    return centred * inverse, inverse


def normalize_back(cotangent, normal, inverse, gain_row):
    scaled = cotangent * gain_row
    first = jnp.mean(scaled, -1, keepdims=True)
    second = jnp.mean(scaled * normal, -1, keepdims=True)
    grad = (scaled - first - normal * second) * inverse
    gain_term = jnp.sum(cotangent * normal, 0, keepdims=True)
    bias_term = jnp.sum(cotangent, 0, keepdims=True)
    return grad, gain_term, bias_term


def head_masks():
    lane = lax.broadcasted_iota(jnp.int32, (1, PAIR), 1)
    first = (lane < HEAD_DIM).astype(F32)
    return (first.astype(BF), (1.0 - first).astype(BF))


def head_masks_scaled():
    lane = lax.broadcasted_iota(jnp.int32, (1, PAIR), 1)
    first = (lane < HEAD_DIM).astype(F32)
    return ((first * SCALE).astype(BF), ((1.0 - first) * SCALE).astype(BF))


def fill_bias(bias, row_seg, key_seg, causal):
    rows, keys = bias.shape

    def block(at):
        allowed = row_seg[at, :] == key_seg[...]
        if causal:
            row_pos = at.start + lax.broadcasted_iota(jnp.int32, (64, keys), 0)
            key_pos = lax.broadcasted_iota(jnp.int32, (64, keys), 1)
            allowed = allowed & (row_pos >= key_pos)
        bias[at, :] = jnp.where(allowed, 0.0, NEG)

    by_rows(rows, 64, block)


def row_parts(rows, keys, causal):
    half = rows // 2
    if causal:
        return ((0, half, half), (half, half, rows))
    return ((0, half, keys), (half, half, keys))


def forward_body(causal, *refs):
    if causal:
        (row_seg, key_seg, source, w_query, w_key, w_value, w_out, norms) = refs[:8]
        rest = refs[8:]
        key_source = (source,)
    else:
        (row_seg, key_seg, source, normal_in, own, other) = refs[:6]
        (w_query, w_key, w_value, w_out, norms) = refs[6:11]
        rest = refs[11:]
        key_source = (own, other)
    (q_out, k_out, v_out, o_out, lse_out, normal_out, inverse_out, low_out) = rest[:8]
    bias, total = rest[8:10]
    step = pl.program_id(0)
    rows = source.shape[0]
    keys = bias.shape[1]

    @pl.when(step == 0)
    def _():
        fill_bias(bias, row_seg, key_seg, causal)
        total[...] = jnp.zeros_like(total)

    q_out[...] = mul_nn(source[...], w_query[...]).astype(BF)
    at = 0
    for part in key_source:
        size = part.shape[0]
        k_out[at : at + size, :] = mul_nn(part[...], w_key[...]).astype(BF)
        v_out[at : at + size, :] = mul_nn(part[...], w_value[...]).astype(BF)
        at += size
    scaled = head_masks_scaled()
    lane = lax.broadcasted_iota(jnp.int32, (1, PAIR), 1)
    for begin, size, seen in row_parts(rows, keys, causal):
        rows_at = slice(begin, begin + size)
        lse_block = jnp.zeros((size, PAIR), F32)
        for pair in range(GROUP // PAIR):
            lanes = slice(pair * PAIR, (pair + 1) * PAIR)
            query = q_out[rows_at, lanes]
            key = k_out[:seen, lanes]
            value = v_out[:seen, lanes]
            outs = []
            for head in range(2):
                scores = mul_nt(query * scaled[head], key) + bias[rows_at, :seen]
                top = jnp.max(scores, -1, keepdims=True)
                weights = jnp.exp(scores - top)
                weight_sum = jnp.sum(weights, -1, keepdims=True)
                outs.append(mul_nn(weights.astype(BF), value) * (1.0 / weight_sum))
                lse_block = jnp.where(
                    lane == pair * 2 + head, top + jnp.log(weight_sum), lse_block
                )
            o_out[rows_at, lanes] = jnp.where(lane < HEAD_DIM, outs[0], outs[1]).astype(BF)
        lse_out[rows_at, :] = lse_block
    total[...] += mul_nn(o_out[...], w_out[...])

    @pl.when(step == pl.num_programs(0) - 1)
    def _():
        def block(at):
            if causal:
                base = source[at, :].astype(F32)
                gain, shift = norms[0:1, :], norms[1:2, :]
            else:
                base = normal_in[at, :] * norms[0:1, :] + norms[1:2, :]
                gain, shift = norms[2:3, :], norms[3:4, :]
            normal, inverse = normalize(ALPHA * base + total[at, :])
            normal_out[at, :] = normal
            inverse_out[at, :] = inverse
            low_out[at, :] = (normal * gain + shift).astype(BF)

        by_rows(rows, 32, block)


def attention_forward(causal, row_seg, key_seg, source, extra, weights, norms):
    rows, width = source.shape
    keys = key_seg.shape[0]
    steps = width // GROUP
    columns = pl.BlockSpec((width, GROUP), lambda g: (0, g))
    in_specs = [whole((rows, 1)), whole((1, keys)), whole((rows, width))]
    operands = [row_seg.reshape(rows, 1), key_seg.reshape(1, keys), source]
    for item in extra:
        in_specs.append(whole(item.shape))
        operands.append(item)
    in_specs += [columns] * 3 + [pl.BlockSpec((GROUP, width), lambda g: (g, 0))]
    in_specs.append(whole(norms.shape))
    row_block = pl.BlockSpec((rows, GROUP), lambda g: (0, g))
    key_block = pl.BlockSpec((keys, GROUP), lambda g: (0, g))
    out_specs = [
        row_block,
        key_block,
        key_block,
        row_block,
        pl.BlockSpec((rows, PAIR), lambda g: (0, g)),
        whole((rows, width)),
        whole((rows, 1)),
        whole((rows, width)),
    ]
    out_shape = [
        shape_of((rows, width), BF),
        shape_of((keys, width), BF),
        shape_of((keys, width), BF),
        shape_of((rows, width), BF),
        shape_of((rows, PAIR * steps), F32),
        shape_of((rows, width), F32),
        shape_of((rows, 1), F32),
        shape_of((rows, width), BF),
    ]
    scratch = [pltpu.VMEM((rows, keys), F32), pltpu.VMEM((rows, width), F32)]
    flops = 2 * rows * width * width * 4 + 4 * rows * keys * width
    call = kernel_call(
        partial(forward_body, causal), (steps,), in_specs, out_specs, out_shape, scratch, flops, 20e6
    )
    return call(*operands, *weights, norms)


def gelu_parts(value):
    bell = jnp.exp(value * value * -0.5)
    short = 1.0 / (1.0 + (ERFC_SLOPE * 0.5**0.5) * jnp.abs(value))
    series = jnp.full_like(value, 0.5 * ERFC_TERMS[-1])
    for term in ERFC_TERMS[-2::-1]:
        series = series * short + 0.5 * term
    tail = bell * short * series
    share = jnp.where(value < 0, tail, 1.0 - tail)
    return value * share, share + value * (bell * (0.5 / np.pi) ** 0.5)


def expand_body(
    core, low, normal_in, w_expand, w_contract, norms, out_grad,
    active_out, slope_out, layer_out, grad_out, low_grad, send_grad, keep_grad, norm_out,
    total,
):
    step = pl.program_id(0)
    rows, width = low.shape

    @pl.when(step == 0)
    def _():
        total[...] = jnp.zeros_like(total)

    size = rows // 2
    for part in range(2):
        at = slice(part * size, (part + 1) * size)
        active, slope = gelu_parts(mul_nn(low[at, :], w_expand[...]))
        active_out[at, :] = active.astype(BF)
        slope_out[at, :] = slope.astype(BF)
    total[...] += mul_nn(active_out[...], w_contract[...])

    @pl.when(step == pl.num_programs(0) - 1)
    def _():
        norm_out[...] = jnp.zeros_like(norm_out)
        half = width // 2
        is_low = core[0] == 0

        def block(at):
            base = normal_in[at, :] * norms[2:3, :] + norms[3:4, :]
            normal, inverse = normalize(ALPHA * base + total[at, :])
            layer_out[at, :] = (normal * norms[4:5, :] + norms[5:6, :]).astype(BF)
            grad, gain_term, bias_term = normalize_back(
                out_grad[at, :].astype(F32), normal, inverse, norms[4:5, :]
            )
            norm_out[0:1, :] += gain_term
            norm_out[1:2, :] += bias_term
            grad_out[at, :] = grad
            low_grad[at, :] = grad.astype(BF)
            left, right = grad[:, :half], grad[:, half:]
            keep_grad[at, :] = jnp.where(is_low, left, right).astype(BF)
            send_grad[at, :] = jnp.where(is_low, right, left).astype(BF)

        by_rows(rows, 32, block)


def feed_forward(core, low, normal, w_expand, w_contract, norms, out_grad):
    rows, width = low.shape
    wide = w_expand.shape[1]
    chunk = 512
    steps = wide // chunk
    in_specs = [
        whole((rows, width)),
        whole((rows, width)),
        pl.BlockSpec((width, chunk), lambda c, _: (0, c)),
        pl.BlockSpec((chunk, width), lambda c, _: (c, 0)),
        whole(norms.shape),
        whole((rows, width)),
    ]
    wide_block = pl.BlockSpec((rows, chunk), lambda c, _: (0, c))
    out_specs = [wide_block, wide_block] + [whole((rows, width))] * 3
    out_specs += [whole((rows, width // 2))] * 2 + [whole((2, width))]
    out_shape = [
        shape_of((rows, wide), BF),
        shape_of((rows, wide), BF),
        shape_of((rows, width), BF),
        shape_of((rows, width), F32),
        shape_of((rows, width), BF),
        shape_of((rows, width // 2), BF),
        shape_of((rows, width // 2), BF),
        shape_of((2, width), F32),
    ]
    call = kernel_call(
        expand_body,
        (steps,),
        in_specs,
        out_specs,
        out_shape,
        [pltpu.VMEM((rows, width), F32)],
        4 * rows * width * wide,
        36e6,
        scalars=1,
    )
    return call(core, low, normal, w_expand, w_contract, norms, out_grad)


def send_first(step, steps, core):
    half = steps // 2
    later = step // half
    return jnp.where(later == 0, 1 - core[0], core[0]) * half + step % half


def contract_back_body(
    core, low_grad, w_contract, slope, w_expand, grad_in, normal_in, inverse_in, norms,
    send_wide, keep_wide, grad_out, low_out, send_low, keep_low, norm_out,
    total,
):
    step = pl.program_id(0)
    steps = pl.num_programs(0)
    rows, width = low_grad.shape

    @pl.when(step == 0)
    def _():
        total[...] = jnp.zeros_like(total)

    wide_grad = (mul_nt(low_grad[...], w_contract[...]) * slope[...].astype(F32)).astype(BF)

    @pl.when(step < steps // 2)
    def _():
        send_wide[...] = wide_grad

    @pl.when(step >= steps // 2)
    def _():
        keep_wide[...] = wide_grad

    total[...] += mul_nt(wide_grad, w_expand[...])

    @pl.when(step == steps - 1)
    def _():
        norm_out[...] = jnp.zeros_like(norm_out)
        half = width // 2
        is_low = core[0] == 0

        def block(at):
            grad, gain_term, bias_term = normalize_back(
                ALPHA * grad_in[at, :] + total[at, :],
                normal_in[at, :],
                inverse_in[at, :],
                norms[2:3, :],
            )
            norm_out[0:1, :] += gain_term
            norm_out[1:2, :] += bias_term
            grad_out[at, :] = grad
            low_out[at, :] = grad.astype(BF)
            left, right = grad[:, :half], grad[:, half:]
            keep_low[at, :] = jnp.where(is_low, left, right).astype(BF)
            send_low[at, :] = jnp.where(is_low, right, left).astype(BF)

        by_rows(rows, 32, block)


def feed_backward(core, low_grad, w_contract, slope, w_expand, grad, normal, inverse, norms):
    rows, width = low_grad.shape
    wide = w_expand.shape[1]
    chunk = 512
    steps = wide // chunk
    half = steps // 2
    in_specs = [
        whole((rows, width)),
        pl.BlockSpec((chunk, width), lambda s, core: (send_first(s, steps, core), 0)),
        pl.BlockSpec((rows, chunk), lambda s, core: (0, send_first(s, steps, core))),
        pl.BlockSpec((width, chunk), lambda s, core: (0, send_first(s, steps, core))),
        whole((rows, width)),
        whole((rows, width)),
        whole((rows, 1)),
        whole(norms.shape),
    ]
    out_specs = [
        pl.BlockSpec((rows, chunk), lambda s, _: (0, jnp.minimum(s, half - 1))),
        pl.BlockSpec((rows, chunk), lambda s, _: (0, jnp.maximum(s - half, 0))),
        whole((rows, width)),
        whole((rows, width)),
        whole((rows, width // 2)),
        whole((rows, width // 2)),
        whole((2, width)),
    ]
    out_shape = [
        shape_of((rows, wide // 2), BF),
        shape_of((rows, wide // 2), BF),
        shape_of((rows, width), F32),
        shape_of((rows, width), BF),
        shape_of((rows, width // 2), BF),
        shape_of((rows, width // 2), BF),
        shape_of((2, width), F32),
    ]
    call = kernel_call(
        contract_back_body,
        (steps,),
        in_specs,
        out_specs,
        out_shape,
        [pltpu.VMEM((rows, width), F32)],
        4 * rows * width * wide,
        32e6,
        scalars=1,
    )
    return call(core, low_grad, w_contract, slope, w_expand, grad, normal, inverse, norms)


def backward_body(causal, core, *refs):
    (row_seg, key_seg, low_grad, w_out, query_in, key_in, value_in, o_in, lse_in) = refs[:9]
    (w_query, w_key, w_value, grad_in) = refs[9:13]
    rest = refs[13:]
    if causal:
        (send_out, keep_out, input_out, bias, total) = rest
    else:
        (normal_in, inverse_in, norms) = rest[:3]
        (send_out, keep_out, grad_out, low_out, send_low, keep_low, norm_out) = rest[3:10]
        (mem_own, mem_send, bias, total, mem_total) = rest[10:]
    step = pl.program_id(0)
    steps = pl.num_programs(0)
    rows, width = low_grad.shape
    keys = bias.shape[1]

    @pl.when(step == 0)
    def _():
        fill_bias(bias, row_seg, key_seg, causal)
        total[...] = jnp.zeros_like(total)
        if not causal:
            mem_total[...] = jnp.zeros_like(mem_total)

    o_grad = mul_nt(low_grad[...], w_out[...]).astype(BF)
    plain = head_masks()
    scaled = head_masks_scaled()
    first_lanes = lax.broadcasted_iota(jnp.int32, (1, PAIR), 1) < HEAD_DIM
    query_grads, key_grads, value_grads = [], [], []
    for pair in range(GROUP // PAIR):
        lanes = slice(pair * PAIR, (pair + 1) * PAIR)
        key_all = key_in[:, lanes]
        value_all = value_in[:, lanes]
        key_grad = value_grad = None
        query_parts = []
        for begin, size, seen in row_parts(rows, keys, causal):
            rows_at = slice(begin, begin + size)
            query = query_in[rows_at, lanes]
            grad = o_grad[rows_at, lanes]
            product = grad.astype(F32) * o_in[rows_at, lanes].astype(F32)
            key = key_all[:seen]
            value = value_all[:seen]
            query_part = None
            for head in range(2):
                mine = first_lanes if head == 0 else jnp.logical_not(first_lanes)
                delta = jnp.sum(jnp.where(mine, product, 0.0), -1, keepdims=True)
                head_query = query * scaled[head]
                head_grad = grad * plain[head]
                lse = lse_in[rows_at, pair * 2 + head : pair * 2 + head + 1]
                prob = jnp.exp(mul_nt(head_query, key) + bias[rows_at, :seen] - lse)
                score_grad = (prob * (mul_nt(head_grad, value) - delta)).astype(BF)
                value_term = mul_tn(prob.astype(BF), head_grad)
                key_term = mul_tn(score_grad, head_query)
                query_term = mul_nn(score_grad, key * scaled[head])
                query_part = query_term if query_part is None else query_part + query_term
                if seen < keys:
                    zeros = jnp.zeros((keys - seen, PAIR), F32)
                    value_term = jnp.concatenate([value_term, zeros])
                    key_term = jnp.concatenate([key_term, zeros])
                value_grad = value_term if value_grad is None else value_grad + value_term
                key_grad = key_term if key_grad is None else key_grad + key_term
            query_parts.append(query_part)
        query_grads.append(jnp.concatenate(query_parts).astype(BF))
        key_grads.append(key_grad.astype(BF))
        value_grads.append(value_grad.astype(BF))
    query_grad = jnp.concatenate(query_grads, axis=1)
    key_grad = jnp.concatenate(key_grads, axis=1)
    value_grad = jnp.concatenate(value_grads, axis=1)

    @pl.when(step < steps // 2)
    def _():
        send_out[0], send_out[1], send_out[2] = query_grad, key_grad, value_grad

    @pl.when(step >= steps // 2)
    def _():
        keep_out[0], keep_out[1], keep_out[2] = query_grad, key_grad, value_grad

    if causal:
        joined = jnp.concatenate([query_grad, key_grad, value_grad], axis=1)
        weights = jnp.concatenate([w_query[...], w_key[...], w_value[...]], axis=1)
        total[...] += mul_nt(joined, weights)
    else:
        total[...] += mul_nt(query_grad, w_query[...])
        joined = jnp.concatenate([key_grad, value_grad], axis=1)
        weights = jnp.concatenate([w_key[...], w_value[...]], axis=1)
        mem_total[...] += mul_nt(joined, weights)

    @pl.when(step == steps - 1)
    def _():
        if causal:

            def block(at):
                input_out[at, :] = (ALPHA * grad_in[at, :] + total[at, :]).astype(BF)

            by_rows(rows, 64, block)
        else:
            own_rows = mem_own.shape[0]
            mem_own[...] = mem_total[:own_rows, :].astype(BF)
            mem_send[...] = mem_total[own_rows:, :].astype(BF)
            norm_out[...] = jnp.zeros_like(norm_out)
            half = width // 2
            is_low = core[0] == 0

            def block(at):
                grad, gain_term, bias_term = normalize_back(
                    ALPHA * grad_in[at, :] + total[at, :],
                    normal_in[at, :],
                    inverse_in[at, :],
                    norms[0:1, :],
                )
                norm_out[0:1, :] += gain_term
                norm_out[1:2, :] += bias_term
                grad_out[at, :] = grad
                low_out[at, :] = grad.astype(BF)
                left, right = grad[:, :half], grad[:, half:]
                keep_low[at, :] = jnp.where(is_low, left, right).astype(BF)
                send_low[at, :] = jnp.where(is_low, right, left).astype(BF)

            by_rows(rows, 32, block)


def attention_backward(causal, core, row_seg, key_seg, low_grad, w_out, saved, weights, grad, extra):
    rows, width = low_grad.shape
    keys = key_seg.shape[0]
    steps = width // GROUP
    half = steps // 2

    def block(shape, spread):
        def index(s, core):
            group = send_first(s, steps, core)
            return (group, 0) if spread == 0 else (0, group)

        return pl.BlockSpec(shape, index)

    row_block = block((rows, GROUP), 1)
    key_block = block((keys, GROUP), 1)
    columns = block((width, GROUP), 1)
    in_specs = [
        whole((rows, 1)),
        whole((1, keys)),
        whole((rows, width)),
        block((GROUP, width), 0),
        row_block,
        key_block,
        key_block,
        row_block,
        block((rows, PAIR), 1),
        columns,
        columns,
        columns,
        whole((rows, width)),
    ]
    in_specs += [whole(item.shape) for item in extra]
    out_specs = [
        pl.BlockSpec((3, rows, GROUP), lambda s, _: (0, 0, jnp.minimum(s, half - 1))),
        pl.BlockSpec((3, rows, GROUP), lambda s, _: (0, 0, jnp.maximum(s - half, 0))),
    ]
    out_shape = [shape_of((3, rows, width // 2), BF)] * 2
    scratch = [pltpu.VMEM((rows, keys), F32), pltpu.VMEM((rows, width), F32)]
    if causal:
        out_specs += [whole((rows, width))]
        out_shape += [shape_of((rows, width), BF)]
    else:
        out_specs += [whole((rows, width))] * 2 + [whole((rows, width // 2))] * 2
        out_specs += [whole((2, width))] + [whole((keys // 2, width))] * 2
        out_shape += [
            shape_of((rows, width), F32),
            shape_of((rows, width), BF),
            shape_of((rows, width // 2), BF),
            shape_of((rows, width // 2), BF),
            shape_of((2, width), F32),
            shape_of((keys // 2, width), BF),
            shape_of((keys // 2, width), BF),
        ]
        scratch += [pltpu.VMEM((keys, width), F32)]
    flops = 2 * rows * width * width * 4 + 10 * rows * keys * width
    call = kernel_call(
        partial(backward_body, causal),
        (steps,),
        in_specs,
        out_specs,
        out_shape,
        scratch,
        flops,
        24e6,
        scalars=1,
    )
    return call(
        core,
        row_seg.reshape(rows, 1),
        key_seg.reshape(1, keys),
        low_grad,
        w_out,
        *saved,
        *weights,
        grad,
        *extra,
    )


def swap_mem(tensor):
    return lax.ppermute(tensor, "mem", [(0, 1), (1, 0)])


def tie(value, *after):
    return lax.optimization_barrier((value, after))[0]


class Plan:
    def __init__(self, steps, row_count):
        self.steps = steps
        self.row_count = row_count
        bit_count = row_count.bit_length() - 1
        sizes = [2 ** (bit_count - 2) if step == "group" else 2 for step in steps]
        self.relative, self.fixed = [], []
        for k in range(row_count):
            mask = fixed = 0
            rest = row_count
            for step, size in zip(steps, sizes):
                rest //= size
                digit = k // rest % size
                if step == "group":
                    fixed = digit << 2
                else:
                    mask |= digit << step
            self.relative.append(mask)
            self.fixed.append(fixed)
        self.own_bits = sum(1 << step for step in steps if step != "group")
        self.groups = [list(range(low, row_count, 4)) for low in range(4)]

    def at_places(self, chip):
        own = chip & self.own_bits
        return (own ^ jnp.asarray(self.relative, jnp.int32)) | jnp.asarray(self.fixed, jnp.int32)

    def permute(self, tensor, bit):
        pairs = [(i, i ^ (1 << bit)) for i in range(self.row_count)]
        return lax.ppermute(tensor, "row", pairs)

    def group_sum(self, tensor):
        return lax.psum_scatter(
            tensor, "row", scatter_dimension=0, tiled=True, axis_index_groups=self.groups
        )


def group_sum_joined(plan, tensors):
    count = plan.row_count // 4
    lanes = math.gcd(*(tensor.shape[1] for tensor in tensors))
    pieces, sizes = [], []
    for tensor in tensors:
        blocks = tensor.reshape(count, -1, tensor.shape[1])
        sizes.append(blocks.shape[1:])
        pieces += [blocks[:, :, at : at + lanes] for at in range(0, blocks.shape[2], lanes)]
    joined = jnp.concatenate(pieces, axis=1)
    summed = plan.group_sum(joined)[0]
    outs, at = [], 0
    for rows, width in sizes:
        parts = []
        for _ in range(width // lanes):
            parts.append(summed[at : at + rows])
            at += rows
        outs.append(jnp.concatenate(parts, axis=1) if len(parts) > 1 else parts[0])
    return outs


class Chain:
    def __init__(self, plan, blocks):
        self.plan = plan
        self.left = list(plan.steps)
        self.got = None
        self.total = None
        if self.left[0] == "group":
            self.sent = blocks[0]
            self.left.pop(0)
            self.total = plan.group_sum(self.sent)
        else:
            self.keep, self.sent = blocks
            self.got = plan.permute(self.sent, self.left.pop(0))

    def sum_rows(self, rows):
        if self.got is None:
            return self.total[rows]
        return self.keep[rows].astype(F32) + self.got[rows].astype(F32)

    def merged(self):
        assert self.left.pop(0) == "group"
        return self.sum_rows(slice(None)).astype(BF)

    def advance(self):
        if self.left[0] == "group":
            self.sent = self.merged()
            self.total, self.got = self.plan.group_sum(self.sent), None
            return
        rows = (self.keep if self.got is not None else self.total).shape[0]
        sent = self.sum_rows(slice(rows // 2, None)).astype(BF)
        self.keep = self.sum_rows(slice(None, rows // 2)).astype(BF)
        self.sent = sent
        self.got = self.plan.permute(sent, self.left.pop(0))

    def result(self):
        assert not self.left
        return self.sum_rows(slice(None)).astype(F32)


def swap_mem(tensor):
    return lax.ppermute(tensor, "mem", [(0, 1), (1, 0)])


def weight_grads_body(spans, item_of_step, count, at_place, *refs):
    items = len(set(item_of_step))
    sources = refs[: 2 * items]
    own_grad, other_grad = refs[2 * items : 2 * items + 2]
    outs = refs[2 * items + 2 : -1]
    whole_grad = refs[-1]
    step = pl.program_id(0)
    _, block_rows, lanes = whole_grad.shape
    joined = max(16 // block_rows, 1)
    for item in range(items):
        steps = [at for at, which in enumerate(item_of_step) if which == item]

        @pl.when((step >= steps[0]) & (step <= steps[-1]))
        def _():
            own, other = sources[2 * item : 2 * item + 2]
            grad = mul_tn(own[...], own_grad[0]) + mul_tn(other[...], other_grad[0])
            whole_grad[...] = grad.reshape(count, block_rows, lanes)

    at_out = 0
    for number, (begin, chunks, halves) in enumerate(spans):
        targets = outs[at_out : at_out + (2 if halves else 1)]
        at_out += len(targets)

        @pl.when((step >= begin) & (step < begin + chunks))
        def _():
            size = count // len(targets)
            for part, out in enumerate(targets):
                for k in range(0, size, joined):
                    base = number * count + part * size + k
                    blocks = [whole_grad[at_place[base + i]] for i in range(joined)]
                    rows = slice(k * block_rows, (k + joined) * block_rows)
                    out[rows, :] = jnp.concatenate(blocks).astype(BF)


def weight_grads(chip, sources, item_of_step, own_grads, other_grads, chunk, outs):
    if own_grads.ndim == 2:
        own_grads, other_grads = own_grads[None], other_grads[None]
    tokens, width = sources[0][0].shape
    across = own_grads.shape[2] // chunk
    count = outs[0][1].row_count
    steps = len(item_of_step)
    grads_block = pl.BlockSpec((1, tokens, chunk), lambda i, _: (i // across, 0, i % across))
    in_specs = [whole((tokens, width))] * (2 * len(sources)) + [grads_block] * 2
    out_specs, out_shape, spans, parts = [], [], [], []
    begin = 0
    for chunks, plan in outs:
        halves = plan.steps[0] != "group"
        pieces = 2 if halves else 1

        def index(i, _, begin=begin, chunks=chunks):
            return (0, jnp.clip(i - begin, 0, chunks - 1))

        for _ in range(pieces):
            out_specs.append(pl.BlockSpec((width // pieces, chunk), index))
            out_shape.append(shape_of((width // pieces, chunk * chunks), BF))
        spans.append((begin, chunks, halves))
        parts.append(pieces)
        begin += chunks
    call = kernel_call(
        partial(weight_grads_body, spans, item_of_step, count),
        (steps,),
        in_specs,
        out_specs,
        out_shape,
        [pltpu.VMEM((count, width // count, chunk), F32)],
        4 * tokens * width * chunk * steps,
        4 * tokens * (width * len(sources) + chunk * steps) + 2 * width * chunk * steps,
        scalars=1,
    )
    at_place = jnp.concatenate([plan.at_places(chip) for _, plan in outs])
    flat = [item for pair in sources for item in pair]
    results = call(at_place, *flat, own_grads, other_grads)
    blocks, at = [], 0
    for pieces in parts:
        blocks.append(results[at : at + pieces])
        at += pieces
    return blocks


def shards(
    row_count,
    inputs,
    memory,
    target_seg,
    memory_seg,
    self_query,
    self_key,
    self_value,
    self_out,
    cross_query,
    cross_key,
    cross_value,
    cross_out,
    expand_weight,
    contract_weight,
    norm_params,
    out_grad,
):
    core = lax.axis_index("mem").astype(jnp.int32).reshape(1)
    chip = lax.axis_index("row").astype(jnp.int32)
    upper = list(range(2, row_count.bit_length() - 1))
    plan_x = Plan([0, 1, "group"], row_count)
    plan_y = Plan([1, 0, "group"], row_count)
    plan_z = Plan(["group", 0, 1], row_count)
    last_x = Plan([0, 1] + upper, row_count)
    last_y = Plan([1] + upper + [0], row_count)
    last_z = Plan(upper + [0, 1], row_count)

    other_inputs = swap_mem(inputs)
    other_memory = swap_mem(memory)
    pair_seg = jnp.concatenate([memory_seg, swap_mem(memory_seg)])

    self_saved = attention_forward(
        True,
        target_seg,
        target_seg,
        inputs,
        (),
        (self_query, self_key, self_value, self_out),
        norm_params,
    )
    self_o, normal_one, inverse_one, low_one = self_saved[3], *self_saved[5:]
    cross_saved = attention_forward(
        False,
        target_seg,
        pair_seg,
        low_one,
        (normal_one, memory, other_memory),
        (cross_query, cross_key, cross_value, cross_out),
        norm_params,
    )
    cross_o, normal_two, inverse_two, low_two = cross_saved[3], *cross_saved[5:]
    (active, slope, layer_out, grad_three, low_three, send_three, keep_three, norm_three) = (
        feed_forward(core, low_two, normal_two, expand_weight, contract_weight, norm_params, out_grad)
    )
    other_active = swap_mem(active)
    got_three = swap_mem(send_three)
    other_self_o = swap_mem(self_o)
    other_one = swap_mem(low_one)
    other_cross_o = swap_mem(cross_o)
    other_two = swap_mem(low_two)
    (send_wide, keep_wide, grad_two, low_grad_two, send_two, keep_two, norm_two) = feed_backward(
        core,
        low_three,
        contract_weight,
        slope,
        expand_weight,
        grad_three,
        normal_two,
        inverse_two,
        norm_params,
    )
    got_wide = swap_mem(send_wide)
    got_two = swap_mem(send_two)

    blocks = weight_grads(
        chip,
        [(tie(active, low_grad_two), other_active)],
        [0, 0],
        keep_three,
        got_three,
        256,
        [(1, plan_x), (1, plan_y)],
    )
    contract_x, contract_y = Chain(plan_x, blocks[0]), Chain(plan_y, blocks[1])
    blocks = weight_grads(
        chip,
        [(tie(low_two, contract_x.sent, contract_y.sent), other_two)],
        [0, 0, 0, 0],
        keep_wide,
        got_wide,
        512,
        [(2, plan_z), (2, plan_x)],
    )
    expand_z, expand_x = Chain(plan_z, blocks[0]), Chain(plan_x, blocks[1])
    blocks = weight_grads(
        chip,
        [(tie(cross_o, expand_z.sent, expand_x.sent), other_cross_o)],
        [0],
        keep_two,
        got_two,
        512,
        [(1, plan_y)],
    )
    cross_out_y = Chain(plan_y, blocks[0])

    (send_c, keep_c, grad_one, low_grad_one, send_one, keep_one, norm_one, mem_own, mem_send) = (
        attention_backward(
            False,
            core,
            target_seg,
            pair_seg,
            tie(low_grad_two, cross_out_y.sent),
            cross_out,
            (cross_saved[0], cross_saved[1], cross_saved[2], cross_o, cross_saved[4]),
            (cross_query, cross_key, cross_value),
            grad_two,
            (normal_one, inverse_one, norm_params),
        )
    )
    memory_grad = (mem_own.astype(F32) + swap_mem(mem_send).astype(F32)).astype(BF)
    got_c = swap_mem(send_c)
    got_one = swap_mem(send_one)

    contract_x.got, contract_y.got, expand_x.got = tie(
        (contract_x.got, contract_y.got, expand_x.got), low_grad_one
    )
    for chain in (contract_x, contract_y, expand_x):
        chain.advance()
    norm_grad = jnp.concatenate([norm_one, norm_two, norm_three])
    norm_grad = norm_grad.reshape(2, 3, norm_grad.shape[1])
    norm_half = norm_grad[core[0]] + swap_mem(norm_grad[1 - core[0]])
    pair_memory = jnp.concatenate([memory, other_memory])
    turned_memory = jnp.concatenate([other_memory, memory])
    blocks = weight_grads(
        chip,
        [
            (tie(low_one, contract_x.sent, contract_y.sent, expand_x.sent), other_one),
            (pair_memory, turned_memory),
        ],
        [0, 0, 1, 1, 1, 1],
        keep_c,
        got_c,
        256,
        [(3, plan_x), (3, plan_y)],
    )
    cross_x, cross_y = Chain(plan_x, blocks[0]), Chain(plan_y, blocks[1])
    blocks = weight_grads(
        chip,
        [(tie(self_o, cross_x.sent, cross_y.sent), other_self_o)],
        [0],
        keep_one,
        got_one,
        512,
        [(1, last_z)],
    )
    block_rows = self_o.shape[1] // row_count
    norm_blocks = norm_half.reshape(3, row_count, block_rows).transpose(1, 0, 2)
    norm_blocks = jnp.pad(norm_blocks, ((0, 0), (0, block_rows - 3), (0, PAIR - block_rows)))
    norm_blocks = jnp.take(norm_blocks, last_z.at_places(chip), axis=0).astype(BF)
    norm_blocks = norm_blocks.reshape(2, -1, PAIR)
    self_out_z = Chain(
        last_z, [jnp.concatenate([blocks[0][i], norm_blocks[i]], axis=1) for i in range(2)]
    )
    contract_x.got, contract_y.got, expand_x.got, cross_out_y.got = tie(
        (contract_x.got, contract_y.got, expand_x.got, cross_out_y.got), self_out_z.sent
    )
    cross_out_y.advance()
    merging = (contract_x, contract_y, expand_x)
    merged = [chain.merged() for chain in merging]
    merged_sums = group_sum_joined(plan_x, merged)

    send_s, keep_s, input_grad = attention_backward(
        True,
        core,
        target_seg,
        target_seg,
        tie(low_grad_one, cross_out_y.sent, merged),
        self_out,
        (self_saved[0], self_saved[1], self_saved[2], self_o, self_saved[4]),
        (self_query, self_key, self_value),
        grad_one,
        (),
    )
    got_s = swap_mem(send_s)
    cross_x.got, cross_y.got, self_out_z.got, cross_out_y.got = tie(
        (cross_x.got, cross_y.got, self_out_z.got, cross_out_y.got), input_grad
    )
    for chain in (cross_x, cross_y, self_out_z):
        chain.advance()
    blocks = weight_grads(
        chip,
        [(tie(inputs, cross_x.sent, cross_y.sent, self_out_z.sent), other_inputs)],
        [0, 0, 0],
        keep_s,
        got_s,
        512,
        [(1, last_x), (1, last_y), (1, last_z)],
    )
    self_x, self_y = Chain(last_x, blocks[0]), Chain(last_y, blocks[1])
    self_z = Chain(last_z, blocks[2])
    expand_z.total = tie(expand_z.total, self_x.sent, self_y.sent, self_z.sent)
    expand_z.advance()
    cross_out_merged = cross_out_y.merged()
    cross_merged = [cross_x.merged(), cross_y.merged(), cross_out_merged]
    cross_sums = group_sum_joined(plan_x, cross_merged)
    self_out_z.advance()
    self_x.advance(), self_y.advance(), self_z.advance()
    expand_z.advance()
    while self_x.left:
        for chain in (self_x, self_y, self_z, self_out_z):
            if chain.left:
                chain.advance()
    self_out_sum = self_out_z.result()
    own_lanes = self_out.shape[1] // 2
    cross_first, cross_second = cross_sums[0].astype(F32), cross_sums[1].astype(F32)
    chunk = 256
    return (
        layer_out,
        input_grad,
        memory_grad,
        self_x.result(),
        self_y.result(),
        self_z.result(),
        self_out_sum[:, :own_lanes],
        cross_first[:, : 2 * chunk],
        jnp.concatenate([cross_first[:, 2 * chunk :], cross_second[:, :chunk]], axis=1),
        cross_second[:, chunk:],
        cross_sums[2].astype(F32),
        jnp.concatenate([expand_z.result(), merged_sums[2].astype(F32)], axis=1),
        jnp.concatenate([merged_sums[0], merged_sums[1]], axis=1).astype(F32),
        self_out_sum[:3, own_lanes : own_lanes + block_rows],
    )


def solution(mesh):
    split_rows = P(("row", "mem"), None)
    split_ids = P(("row", "mem"))
    in_specs = (split_rows, split_rows, split_ids, split_ids) + (P(),) * 11 + (split_rows,)
    out_specs = (split_rows,) * 3 + (P("row", "mem"),) * 10 + (P("mem", "row"),)
    return jax.shard_map(
        partial(shards, mesh.shape["row"]),
        mesh=mesh,
        in_specs=in_specs,
        out_specs=out_specs,
        check_vma=False,
    )
```

```python
import math
from functools import partial

import jax
import jax.numpy as jnp
import numpy as np
from jax import lax
from jax.experimental import pallas as pl
from jax.experimental.pallas import tpu as pltpu
from jax.sharding import PartitionSpec as P

HEADS = 16
HEAD_DIM = 64
GROUP = 256
PAIR = 128

ALPHA = 300.0**0.25
SCALE = 0.125
NEG = -1e30
EPS = 1e-05

BF = jnp.bfloat16
F32 = jnp.float32
VMEM_LIMIT = 56 * 2**20


def mul(left, right, left_axis, right_axis):
    return lax.dot_general(
        left, right, (((left_axis,), (right_axis,)), ((), ())), preferred_element_type=F32
    )


def mul_nn(left, right):
    return mul(left, right, 1, 0)


def mul_nt(left, right):
    return mul(left, right, 1, 1)


def mul_tn(left, right):
    return mul(left, right, 0, 0)


def kernel_call(body, grid, in_specs, out_specs, out_shape, scratch, moved, scalars=0):
    return pl.pallas_call(
        body,
        grid_spec=pltpu.PrefetchScalarGridSpec(
            num_scalar_prefetch=scalars,
            grid=grid,
            in_specs=in_specs,
            out_specs=out_specs,
            scratch_shapes=scratch,
        ),
        out_shape=out_shape,
        compiler_params=pltpu.CompilerParams(vmem_limit_bytes=VMEM_LIMIT),
        cost_estimate=pl.CostEstimate(
            flops=1, bytes_accessed=int(moved * 2**20), transcendentals=0
        ),
    )


def whole(shape):
    return pl.BlockSpec(shape, lambda *_: (0,) * len(shape))


def shape_of(shape, dtype):
    return jax.ShapeDtypeStruct(shape, dtype)


def by_rows(rows, step, body):
    def one(at, carry):
        body(pl.ds(pl.multiple_of(at * step, step), step))
        return carry

    lax.fori_loop(0, rows // step, one, 0)


def normalize(value):
    middle = jnp.mean(value, -1, keepdims=True)
    centred = value - middle
    spread = jnp.mean(centred * centred, -1, keepdims=True)
    inverse = lax.rsqrt(spread + EPS)
    return centred * inverse, inverse


def normalize_back(cotangent, normal, inverse, gain_row):
    scaled = cotangent * gain_row
    first = jnp.mean(scaled, -1, keepdims=True)
    second = jnp.mean(scaled * normal, -1, keepdims=True)
    grad = (scaled - first - normal * second) * inverse
    gain_term = jnp.sum(cotangent * normal, 0, keepdims=True)
    bias_term = jnp.sum(cotangent, 0, keepdims=True)
    return grad, gain_term, bias_term


def head_masks():
    lane = lax.broadcasted_iota(jnp.int32, (1, PAIR), 1)
    first = (lane < HEAD_DIM).astype(F32)
    return (first.astype(BF), (1.0 - first).astype(BF))


def head_masks_scaled():
    lane = lax.broadcasted_iota(jnp.int32, (1, PAIR), 1)
    first = (lane < HEAD_DIM).astype(F32)
    return ((first * SCALE).astype(BF), ((1.0 - first) * SCALE).astype(BF))


def fill_bias(bias, row_seg, key_seg, causal):
    rows, keys = bias.shape

    def block(at):
        allowed = row_seg[at, :] == key_seg[...]
        if causal:
            row_pos = at.start + lax.broadcasted_iota(jnp.int32, (64, keys), 0)
            key_pos = lax.broadcasted_iota(jnp.int32, (64, keys), 1)
            allowed = allowed & (row_pos >= key_pos)
        bias[at, :] = jnp.where(allowed, 0.0, NEG)

    by_rows(rows, 64, block)


def row_parts(rows, keys, causal):
    half = rows // 2
    if causal:
        return ((0, half, half), (half, half, rows))
    return ((0, half, keys), (half, half, keys))


def forward_body(causal, *refs):
    if causal:
        (row_seg, key_seg, source, w_query, w_key, w_value, w_out, norms) = refs[:8]
        rest = refs[8:]
        key_source = (source,)
    else:
        (row_seg, key_seg, source, normal_in, own, other) = refs[:6]
        (w_query, w_key, w_value, w_out, norms) = refs[6:11]
        rest = refs[11:]
        key_source = (own, other)
    (q_out, k_out, v_out, o_out, lse_out, normal_out, inverse_out, low_out) = rest[:8]
    bias, total = rest[8:10]
    step = pl.program_id(0)
    rows = source.shape[0]
    keys = bias.shape[1]

    @pl.when(step == 0)
    def _():
        fill_bias(bias, row_seg, key_seg, causal)
        total[...] = jnp.zeros_like(total)

    q_out[...] = mul_nn(source[...], w_query[...]).astype(BF)
    at = 0
    for part in key_source:
        size = part.shape[0]
        k_out[at : at + size, :] = mul_nn(part[...], w_key[...]).astype(BF)
        v_out[at : at + size, :] = mul_nn(part[...], w_value[...]).astype(BF)
        at += size
    scaled = head_masks_scaled()
    lane = lax.broadcasted_iota(jnp.int32, (1, PAIR), 1)
    for begin, size, seen in row_parts(rows, keys, causal):
        rows_at = slice(begin, begin + size)
        scores = []
        for pair in range(GROUP // PAIR):
            lanes = slice(pair * PAIR, (pair + 1) * PAIR)
            query = q_out[rows_at, lanes]
            key = k_out[:seen, lanes]
            for head in range(2):
                scores.append(mul_nt(query * scaled[head], key) + bias[rows_at, :seen])
        lse_block = jnp.zeros((size, PAIR), F32)
        for pair in range(GROUP // PAIR):
            lanes = slice(pair * PAIR, (pair + 1) * PAIR)
            value = v_out[:seen, lanes]
            outs = []
            for head in range(2):
                score = scores[pair * 2 + head]
                top = jnp.max(score, -1, keepdims=True)
                weights = jnp.exp(score - top)
                weight_sum = jnp.sum(weights, -1, keepdims=True)
                outs.append(mul_nn(weights.astype(BF), value) * (1.0 / weight_sum))
                lse_block = jnp.where(
                    lane == pair * 2 + head, top + jnp.log(weight_sum), lse_block
                )
            o_out[rows_at, lanes] = jnp.where(lane < HEAD_DIM, outs[0], outs[1]).astype(BF)
        lse_out[rows_at, :] = lse_block
    total[...] += mul_nn(o_out[...], w_out[...])

    @pl.when(step == pl.num_programs(0) - 1)
    def _():
        def block(at):
            if causal:
                base = source[at, :].astype(F32)
                gain, shift = norms[0:1, :], norms[1:2, :]
            else:
                base = normal_in[at, :] * norms[0:1, :] + norms[1:2, :]
                gain, shift = norms[2:3, :], norms[3:4, :]
            normal, inverse = normalize(ALPHA * base + total[at, :])
            normal_out[at, :] = normal
            inverse_out[at, :] = inverse
            low_out[at, :] = (normal * gain + shift).astype(BF)

        by_rows(rows, 128, block)


def attention_forward(causal, row_seg, key_seg, source, extra, weights, norms):
    rows, width = source.shape
    keys = key_seg.shape[0]
    steps = width // GROUP
    columns = pl.BlockSpec((width, GROUP), lambda g: (0, g))
    in_specs = [whole((rows, 1)), whole((1, keys)), whole((rows, width))]
    operands = [row_seg.reshape(rows, 1), key_seg.reshape(1, keys), source]
    for item in extra:
        in_specs.append(whole(item.shape))
        operands.append(item)
    in_specs += [columns] * 3 + [pl.BlockSpec((GROUP, width), lambda g: (g, 0))]
    in_specs.append(whole(norms.shape))
    row_block = pl.BlockSpec((rows, GROUP), lambda g: (0, g))
    key_block = pl.BlockSpec((keys, GROUP), lambda g: (0, g))
    out_specs = [
        row_block,
        key_block,
        key_block,
        row_block,
        pl.BlockSpec((rows, PAIR), lambda g: (0, g)),
        whole((rows, width)),
        whole((rows, 1)),
        whole((rows, width)),
    ]
    out_shape = [
        shape_of((rows, width), BF),
        shape_of((keys, width), BF),
        shape_of((keys, width), BF),
        shape_of((rows, width), BF),
        shape_of((rows, PAIR * steps), F32),
        shape_of((rows, width), F32),
        shape_of((rows, 1), F32),
        shape_of((rows, width), BF),
    ]
    scratch = [pltpu.VMEM((rows, keys), F32), pltpu.VMEM((rows, width), F32)]
    call = kernel_call(
        partial(forward_body, causal), (steps,), in_specs, out_specs, out_shape, scratch, 30
    )
    return call(*operands, *weights, norms)


def gelu_parts(value):
    share = 0.5 + 0.5 * lax.erf(value * 0.5**0.5)
    bell = jnp.exp(value * value * -0.5) * (0.5 / np.pi) ** 0.5
    return value * share, share + value * bell


def expand_body(
    core, low, normal_in, w_expand, w_contract, norms, out_grad,
    active_out, slope_out, layer_out, grad_out, low_grad, send_grad, keep_grad, norm_out,
    total,
):
    step = pl.program_id(0)
    rows, width = low.shape

    @pl.when(step == 0)
    def _():
        total[...] = jnp.zeros_like(total)

    size = rows // 2
    spans = [slice(part * size, (part + 1) * size) for part in range(2)]
    values = [mul_nn(low[at, :], w_expand[...]) for at in spans]
    for at, value in zip(spans, values):
        active, slope = gelu_parts(value)
        active = active.astype(BF)
        active_out[at, :] = active
        slope_out[at, :] = slope.astype(BF)
        total[at, :] += mul_nn(active, w_contract[...])

    @pl.when(step == pl.num_programs(0) - 1)
    def _():
        norm_out[...] = jnp.zeros_like(norm_out)
        half = width // 2
        is_low = core[0] == 0

        def block(at):
            base = normal_in[at, :] * norms[2:3, :] + norms[3:4, :]
            normal, inverse = normalize(ALPHA * base + total[at, :])
            layer_out[at, :] = (normal * norms[4:5, :] + norms[5:6, :]).astype(BF)
            grad, gain_term, bias_term = normalize_back(
                out_grad[at, :].astype(F32), normal, inverse, norms[4:5, :]
            )
            norm_out[0:1, :] += gain_term
            norm_out[1:2, :] += bias_term
            grad_out[at, :] = grad
            low_grad[at, :] = grad.astype(BF)
            left, right = grad[:, :half], grad[:, half:]
            keep_grad[at, :] = jnp.where(is_low, left, right).astype(BF)
            send_grad[at, :] = jnp.where(is_low, right, left).astype(BF)

        by_rows(rows, 128, block)


def feed_forward(core, low, normal, w_expand, w_contract, norms, out_grad):
    rows, width = low.shape
    wide = w_expand.shape[1]
    chunk = 512
    steps = wide // chunk
    in_specs = [
        whole((rows, width)),
        whole((rows, width)),
        pl.BlockSpec((width, chunk), lambda c, _: (0, c)),
        pl.BlockSpec((chunk, width), lambda c, _: (c, 0)),
        whole(norms.shape),
        whole((rows, width)),
    ]
    wide_block = pl.BlockSpec((rows, chunk), lambda c, _: (0, c))
    out_specs = [wide_block, wide_block] + [whole((rows, width))] * 3
    out_specs += [whole((rows, width // 2))] * 2 + [whole((2, width))]
    out_shape = [
        shape_of((rows, wide), BF),
        shape_of((rows, wide), BF),
        shape_of((rows, width), BF),
        shape_of((rows, width), F32),
        shape_of((rows, width), BF),
        shape_of((rows, width // 2), BF),
        shape_of((rows, width // 2), BF),
        shape_of((2, width), F32),
    ]
    call = kernel_call(
        expand_body,
        (steps,),
        in_specs,
        out_specs,
        out_shape,
        [pltpu.VMEM((rows, width), F32)],
        34,
        scalars=1,
    )
    return call(core, low, normal, w_expand, w_contract, norms, out_grad)


def send_first(step, steps, core):
    half = steps // 2
    later = step // half
    return jnp.where(later == 0, 1 - core[0], core[0]) * half + step % half


def contract_back_body(last, core, *refs):
    low_grad, w_contract, slope, w_expand = refs[:4]
    if last:
        (total_in, grad_in, normal_in, inverse_in, norms) = refs[4:9]
        (wide_out, grad_out, low_out, send_low, keep_low, norm_out, total) = refs[9:]
    else:
        wide_out, total = refs[4:]
    step = pl.program_id(0)
    rows, width = low_grad.shape

    @pl.when(step == 0)
    def _():
        total[...] = total_in[...] if last else jnp.zeros_like(total)

    size = rows // 2
    spans = [slice(part * size, (part + 1) * size) for part in range(2)]
    values = [mul_nt(low_grad[at, :], w_contract[...]) for at in spans]
    for at, value in zip(spans, values):
        wide_grad = (value * slope[at, :].astype(F32)).astype(BF)
        wide_out[at, :] = wide_grad
        total[at, :] += mul_nt(wide_grad, w_expand[...])

    if not last:
        return

    @pl.when(step == pl.num_programs(0) - 1)
    def _():
        norm_out[...] = jnp.zeros_like(norm_out)
        half = width // 2
        is_low = core[0] == 0

        def block(at):
            grad, gain_term, bias_term = normalize_back(
                ALPHA * grad_in[at, :] + total[at, :],
                normal_in[at, :],
                inverse_in[at, :],
                norms[2:3, :],
            )
            norm_out[0:1, :] += gain_term
            norm_out[1:2, :] += bias_term
            grad_out[at, :] = grad
            low_out[at, :] = grad.astype(BF)
            left, right = grad[:, :half], grad[:, half:]
            keep_low[at, :] = jnp.where(is_low, left, right).astype(BF)
            send_low[at, :] = jnp.where(is_low, right, left).astype(BF)

        by_rows(rows, 128, block)


def feed_backward(last, core, low_grad, w_contract, slope, w_expand, *rest):
    rows, width = low_grad.shape
    wide = w_expand.shape[1]
    chunk = 512
    steps = wide // chunk // 2

    def at(s, core):
        return (core[0] if last else 1 - core[0]) * steps + s

    in_specs = [
        whole((rows, width)),
        pl.BlockSpec((chunk, width), lambda s, core: (at(s, core), 0)),
        pl.BlockSpec((rows, chunk), lambda s, core: (0, at(s, core))),
        pl.BlockSpec((width, chunk), lambda s, core: (0, at(s, core))),
    ] + [whole(item.shape) for item in rest]
    out_specs = [pl.BlockSpec((rows, chunk), lambda s, _: (0, s)), whole((rows, width))]
    out_shape = [shape_of((rows, wide // 2), BF), shape_of((rows, width), F32)]
    scratch = []
    if last:
        out_specs += [whole((rows, width))] + [whole((rows, width // 2))] * 2 + [whole((2, width))]
        out_shape += [
            shape_of((rows, width), BF),
            shape_of((rows, width // 2), BF),
            shape_of((rows, width // 2), BF),
            shape_of((2, width), F32),
        ]
        scratch = [pltpu.VMEM((rows, width), F32)]
    call = kernel_call(
        partial(contract_back_body, last),
        (steps,),
        in_specs,
        out_specs,
        out_shape,
        scratch,
        18,
        scalars=1,
    )
    return call(core, low_grad, w_contract, slope, w_expand, *rest)


def add_rows(parts):
    first, last = parts
    rows = first.shape[0]
    if rows == last.shape[0]:
        return first + last
    return jnp.concatenate([first + last[:rows], last[rows:]])


def backward_body(causal, core, *refs):
    (row_seg, key_seg, low_grad, w_out, query_in, key_in, value_in, o_in, lse_in) = refs[:9]
    (w_query, w_key, w_value, grad_in) = refs[9:13]
    rest = refs[13:]
    if causal:
        (send_out, keep_out, input_out, bias, total) = rest
    else:
        (normal_in, inverse_in, norms) = rest[:3]
        (send_out, keep_out, grad_out, low_out, send_low, keep_low, norm_out) = rest[3:10]
        (mem_own, mem_send, bias, total, mem_total) = rest[10:]
    step = pl.program_id(0)
    steps = pl.num_programs(0)
    rows, width = low_grad.shape
    keys = bias.shape[1]

    @pl.when(step == 0)
    def _():
        fill_bias(bias, row_seg, key_seg, causal)
        total[...] = jnp.zeros_like(total)
        if not causal:
            mem_total[...] = jnp.zeros_like(mem_total)

    o_grad = mul_nt(low_grad[...], w_out[...]).astype(BF)
    plain = head_masks()
    scaled = head_masks_scaled()
    first_lanes = lax.broadcasted_iota(jnp.int32, (1, PAIR), 1) < HEAD_DIM
    query_grads, key_grads, value_grads = [], [], []
    for pair in range(GROUP // PAIR):
        lanes = slice(pair * PAIR, (pair + 1) * PAIR)
        started = []
        for begin, size, seen in row_parts(rows, keys, causal):
            rows_at = slice(begin, begin + size)
            query = query_in[rows_at, lanes]
            grad = o_grad[rows_at, lanes]
            key = key_in[:seen, lanes]
            value = value_in[:seen, lanes]
            product = grad.astype(F32) * o_in[rows_at, lanes].astype(F32)
            head_queries = [query * scaled[head] for head in range(2)]
            head_grads = [grad * plain[head] for head in range(2)]
            scores = [mul_nt(item, key) for item in head_queries]
            prob_grads = [mul_nt(item, value) for item in head_grads]
            started.append(
                (rows_at, seen, key, product, head_queries, head_grads, scores, prob_grads)
            )
        query_parts, key_parts, value_parts = [], [], []
        for rows_at, seen, key, product, head_queries, head_grads, scores, prob_grads in started:
            probs, score_grads = [], []
            for head in range(2):
                mine = first_lanes if head == 0 else jnp.logical_not(first_lanes)
                delta = jnp.sum(jnp.where(mine, product, 0.0), -1, keepdims=True)
                lse = lse_in[rows_at, pair * 2 + head : pair * 2 + head + 1]
                prob = jnp.exp(scores[head] + bias[rows_at, :seen] - lse)
                score_grads.append((prob * (prob_grads[head] - delta)).astype(BF))
                probs.append(prob.astype(BF))
            value_parts.append(mul_tn(jnp.concatenate(probs), jnp.concatenate(head_grads)))
            stacked = jnp.concatenate(score_grads)
            key_parts.append(mul_tn(stacked, jnp.concatenate(head_queries)))
            wide = jnp.concatenate(score_grads, axis=1)
            head_keys = jnp.concatenate([key * scaled[0], key * scaled[1]])
            query_parts.append(mul_nn(wide, head_keys))
        query_grads.append(jnp.concatenate(query_parts).astype(BF))
        key_grads.append(add_rows(key_parts).astype(BF))
        value_grads.append(add_rows(value_parts).astype(BF))
    query_grad = jnp.concatenate(query_grads, axis=1)
    key_grad = jnp.concatenate(key_grads, axis=1)
    value_grad = jnp.concatenate(value_grads, axis=1)

    @pl.when(step < steps // 2)
    def _():
        send_out[0], send_out[1], send_out[2] = query_grad, key_grad, value_grad

    @pl.when(step >= steps // 2)
    def _():
        keep_out[0], keep_out[1], keep_out[2] = query_grad, key_grad, value_grad

    if causal:
        joined = jnp.concatenate([query_grad, key_grad, value_grad], axis=1)
        weights = jnp.concatenate([w_query[...], w_key[...], w_value[...]], axis=1)
        total[...] += mul_nt(joined, weights)
    else:
        total[...] += mul_nt(query_grad, w_query[...])
        joined = jnp.concatenate([key_grad, value_grad], axis=1)
        weights = jnp.concatenate([w_key[...], w_value[...]], axis=1)
        mem_total[...] += mul_nt(joined, weights)

    @pl.when(step == steps - 1)
    def _():
        if causal:

            def block(at):
                input_out[at, :] = (ALPHA * grad_in[at, :] + total[at, :]).astype(BF)

            by_rows(rows, 64, block)
        else:
            own_rows = mem_own.shape[0]
            mem_own[...] = mem_total[:own_rows, :].astype(BF)
            mem_send[...] = mem_total[own_rows:, :].astype(BF)
            norm_out[...] = jnp.zeros_like(norm_out)
            half = width // 2
            is_low = core[0] == 0

            def block(at):
                grad, gain_term, bias_term = normalize_back(
                    ALPHA * grad_in[at, :] + total[at, :],
                    normal_in[at, :],
                    inverse_in[at, :],
                    norms[0:1, :],
                )
                norm_out[0:1, :] += gain_term
                norm_out[1:2, :] += bias_term
                grad_out[at, :] = grad
                low_out[at, :] = grad.astype(BF)
                left, right = grad[:, :half], grad[:, half:]
                keep_low[at, :] = jnp.where(is_low, left, right).astype(BF)
                send_low[at, :] = jnp.where(is_low, right, left).astype(BF)

            by_rows(rows, 128, block)


def attention_backward(causal, core, row_seg, key_seg, low_grad, w_out, saved, weights, grad, extra):
    rows, width = low_grad.shape
    keys = key_seg.shape[0]
    steps = width // GROUP
    half = steps // 2

    def block(shape, spread):
        def index(s, core):
            group = send_first(s, steps, core)
            return (group, 0) if spread == 0 else (0, group)

        return pl.BlockSpec(shape, index)

    row_block = block((rows, GROUP), 1)
    key_block = block((keys, GROUP), 1)
    columns = block((width, GROUP), 1)
    in_specs = [
        whole((rows, 1)),
        whole((1, keys)),
        whole((rows, width)),
        block((GROUP, width), 0),
        row_block,
        key_block,
        key_block,
        row_block,
        block((rows, PAIR), 1),
        columns,
        columns,
        columns,
        whole((rows, width)),
    ]
    in_specs += [whole(item.shape) for item in extra]
    out_specs = [
        pl.BlockSpec((3, rows, GROUP), lambda s, _: (0, 0, jnp.minimum(s, half - 1))),
        pl.BlockSpec((3, rows, GROUP), lambda s, _: (0, 0, jnp.maximum(s - half, 0))),
    ]
    out_shape = [shape_of((3, rows, width // 2), BF)] * 2
    scratch = [pltpu.VMEM((rows, keys), F32), pltpu.VMEM((rows, width), F32)]
    if causal:
        out_specs += [whole((rows, width))]
        out_shape += [shape_of((rows, width), BF)]
    else:
        out_specs += [whole((rows, width))] * 2 + [whole((rows, width // 2))] * 2
        out_specs += [whole((2, width))] + [whole((keys // 2, width))] * 2
        out_shape += [
            shape_of((rows, width), F32),
            shape_of((rows, width), BF),
            shape_of((rows, width // 2), BF),
            shape_of((rows, width // 2), BF),
            shape_of((2, width), F32),
            shape_of((keys // 2, width), BF),
            shape_of((keys // 2, width), BF),
        ]
        scratch += [pltpu.VMEM((keys, width), F32)]
    call = kernel_call(
        partial(backward_body, causal),
        (steps,),
        in_specs,
        out_specs,
        out_shape,
        scratch,
        44,
        scalars=1,
    )
    return call(
        core,
        row_seg.reshape(rows, 1),
        key_seg.reshape(1, keys),
        low_grad,
        w_out,
        *saved,
        *weights,
        grad,
        *extra,
    )


def swap_mem(tensor):
    return lax.ppermute(tensor, "mem", [(0, 1), (1, 0)])


def tie(value, *after):
    return lax.optimization_barrier((value, after))[0]


def beside(outputs, arrays):
    return lax.optimization_barrier((outputs, arrays))


def during(outputs, *chains):
    outputs, terms = lax.optimization_barrier((outputs, [chain.terms for chain in chains]))
    for chain, items in zip(chains, terms):
        chain.terms = items
    return outputs


class Plan:
    def __init__(self, steps, row_count):
        self.steps = steps
        self.row_count = row_count
        sizes = [self.pieces(step) for step in steps]
        self.relative, self.fixed = [], []
        for k in range(row_count):
            mask = fixed = 0
            rest = row_count
            for step, size in zip(steps, sizes):
                rest //= size
                digit = k // rest % size
                if step == "group":
                    fixed = digit << 2
                elif step == "plane":
                    mask |= digit
                else:
                    mask |= digit << step
            self.relative.append(mask)
            self.fixed.append(fixed)
        self.groups = [list(range(low, row_count, 4)) for low in range(4)]

    def pieces(self, step):
        if step == "group":
            return self.row_count // 4
        return 4 if step == "plane" else 2

    def first_pieces(self):
        return 1 if self.steps[0] == "group" else self.pieces(self.steps[0])

    def at_places(self, chip):
        own = (chip & 3) if "group" in self.steps else chip
        return (own ^ jnp.asarray(self.relative, jnp.int32)) | jnp.asarray(self.fixed, jnp.int32)

    def permute(self, tensor, mask):
        pairs = [(i, i ^ mask) for i in range(self.row_count)]
        return lax.ppermute(tensor, "row", pairs)

    def group_sum(self, tensor):
        return lax.psum_scatter(
            tensor, "row", scatter_dimension=0, tiled=True, axis_index_groups=self.groups
        )


def group_sum_joined(plan, tensors):
    count = plan.row_count // 4
    lanes = math.gcd(*(tensor.shape[1] for tensor in tensors))
    pieces, sizes = [], []
    for tensor in tensors:
        blocks = tensor.reshape(count, -1, tensor.shape[1])
        sizes.append(blocks.shape[1:])
        pieces += [blocks[:, :, at : at + lanes] for at in range(0, blocks.shape[2], lanes)]
    joined = jnp.concatenate(pieces, axis=1)
    summed = plan.group_sum(joined)[0]
    outs, at = [], 0
    for rows, width in sizes:
        parts = []
        for _ in range(width // lanes):
            parts.append(summed[at : at + rows])
            at += rows
        outs.append(jnp.concatenate(parts, axis=1) if len(parts) > 1 else parts[0])
    return outs


class Chain:
    def __init__(self, plan, blocks):
        self.plan = plan
        self.left = list(plan.steps)
        self.launch(list(blocks))

    def launch(self, pieces):
        step = self.left.pop(0)
        if step == "group":
            self.sent = pieces
            self.terms = [self.plan.group_sum(pieces[0])]
            return
        self.sent = pieces[1:]
        masks = [1, 2, 3] if step == "plane" else [1 << step]
        got = [self.plan.permute(piece, mask) for piece, mask in zip(self.sent, masks)]
        self.terms = [pieces[0]] + got

    def hold(self, *after):
        got = self.terms[1:] if len(self.terms) > 1 else self.terms
        self.terms[-len(got) :] = tie(got, *after)

    def sum_rows(self, rows):
        total = self.terms[0][rows].astype(F32)
        for term in self.terms[1:]:
            total = total + term[rows].astype(F32)
        return total

    def merged(self):
        assert self.left.pop(0) == "group"
        return self.sum_rows(slice(None)).astype(BF)

    def advance(self):
        step = self.left[0]
        count = 1 if step == "group" else self.plan.pieces(step)
        rows = self.terms[0].shape[0] // count
        self.launch(
            [self.sum_rows(slice(k * rows, (k + 1) * rows)).astype(BF) for k in range(count)]
        )

    def result(self):
        assert not self.left
        return self.sum_rows(slice(None))


def swap_mem(tensor):
    return lax.ppermute(tensor, "mem", [(0, 1), (1, 0)])


def weight_grads_body(spans, sources_count, grads_count, step_table, count, at_place, *refs):
    sources = refs[: 2 * sources_count]
    grads = refs[2 * sources_count : 2 * (sources_count + grads_count)]
    outs = refs[2 * (sources_count + grads_count) : -1]
    whole_grad = refs[-1]
    step = pl.program_id(0)
    _, block_rows, lanes = whole_grad.shape
    joined = max(16 // block_rows, 1)
    for entry in sorted(set(step_table)):
        steps = [at for at, which in enumerate(step_table) if which == entry]

        @pl.when((step >= steps[0]) & (step <= steps[-1]))
        def _():
            own, other = sources[2 * entry[0] : 2 * entry[0] + 2]
            own_grad, other_grad = grads[2 * entry[1] : 2 * entry[1] + 2]
            grad = mul_tn(own[...], own_grad[0]) + mul_tn(other[...], other_grad[0])
            whole_grad[...] = grad.reshape(count, block_rows, lanes)

    at_out = 0
    for number, (begin, chunks, pieces) in enumerate(spans):
        targets = outs[at_out : at_out + pieces]
        at_out += pieces

        @pl.when((step >= begin) & (step < begin + chunks))
        def _():
            size = count // pieces
            for part, out in enumerate(targets):
                for k in range(0, size, joined):
                    base = number * count + part * size + k
                    blocks = [whole_grad[at_place[base + i]] for i in range(joined)]
                    rows = slice(k * block_rows, (k + joined) * block_rows)
                    out[rows, :] = jnp.concatenate(blocks).astype(BF)


def weight_grads(chip, sources, grads, step_table, chunk, outs, travelling=()):
    tokens, width = sources[0][0].shape
    count = outs[0][1].row_count
    steps = len(step_table)
    in_specs = [whole((tokens, width))] * (2 * len(sources))
    flat = [item for pair in sources for item in pair]
    for number, pair in enumerate(grads):
        pair = [item if item.ndim == 3 else item[None] for item in pair]
        flat += pair
        across = pair[0].shape[2] // chunk
        mine = [at for at, which in enumerate(step_table) if which[1] == number]

        def index(i, _, first=mine[0], last=mine[-1], across=across):
            at = jnp.clip(i, first, last) - first
            return (at // across, 0, at % across)

        in_specs += [pl.BlockSpec((1, tokens, chunk), index)] * 2
    out_specs, out_shape, spans = [], [], []
    begin = 0
    for chunks, plan in outs:
        pieces = plan.first_pieces()

        def index(i, _, begin=begin, chunks=chunks):
            return (0, jnp.clip(i - begin, 0, chunks - 1))

        for _ in range(pieces):
            out_specs.append(pl.BlockSpec((width // pieces, chunk), index))
            out_shape.append(shape_of((width // pieces, chunk * chunks), BF))
        spans.append((begin, chunks, pieces))
        begin += chunks
    call = kernel_call(
        partial(weight_grads_body, spans, len(sources), len(grads), step_table, count),
        (steps,),
        in_specs,
        out_specs,
        out_shape,
        [pltpu.VMEM((count, width // count, chunk), F32)],
        16,
        scalars=1,
    )
    at_place = jnp.concatenate([plan.at_places(chip) for _, plan in outs])
    results = during(call(at_place, *flat), *travelling)
    chains, at = [], 0
    for (_, plan), (_, _, pieces) in zip(outs, spans):
        chains.append(Chain(plan, results[at : at + pieces]))
        at += pieces
    return chains


def wide_grads_body(at_chunk, own, other, own_grad, other_grad, *outs):
    step = pl.program_id(0)
    chains = len(outs) // 2
    lanes = outs[0].shape[1]
    block_rows = outs[0].shape[0] * 2 * chains // at_chunk.shape[0]
    blocks = own.shape[1] // block_rows
    size = outs[0].shape[0] // block_rows
    grad = mul_tn(own[...], own_grad[...]) + mul_tn(other[...], other_grad[...])
    grad = grad.astype(BF)
    for block in range(blocks):
        for chain in range(chains):
            part = grad[block * block_rows : (block + 1) * block_rows]
            part = part[:, chain * lanes : (chain + 1) * lanes]
            place = at_chunk[2 * size * chain + step * blocks + block]
            for half in range(2):

                @pl.when((place >= half * size) & (place < (half + 1) * size))
                def _():
                    row = pl.multiple_of((place - half * size) * block_rows, block_rows)
                    outs[2 * chain + half][pl.ds(row, block_rows), :] = part


def wide_grads(chip, own, other, own_grad, other_grad, plans):
    tokens, width = own.shape
    lanes = own_grad.shape[1]
    chunk = 512
    source = pl.BlockSpec((tokens, chunk), lambda i, _: (0, i))
    out = (width // 2, lanes // len(plans))
    call = kernel_call(
        wide_grads_body,
        (width // chunk,),
        [source] * 2 + [whole((tokens, lanes))] * 2,
        [whole(out)] * (2 * len(plans)),
        [shape_of(out, BF)] * (2 * len(plans)),
        [],
        20,
        scalars=1,
    )
    place = jnp.concatenate([jnp.argsort(plan.at_places(chip)) for plan in plans])
    results = call(place.astype(jnp.int32), own, other, own_grad, other_grad)
    return [Chain(plan, results[2 * at : 2 * at + 2]) for at, plan in enumerate(plans)]


def shards(
    row_count,
    inputs,
    memory,
    target_seg,
    memory_seg,
    self_query,
    self_key,
    self_value,
    self_out,
    cross_query,
    cross_key,
    cross_value,
    cross_out,
    expand_weight,
    contract_weight,
    norm_params,
    out_grad,
):
    core = lax.axis_index("mem").astype(jnp.int32).reshape(1)
    chip = lax.axis_index("row").astype(jnp.int32)
    upper = list(range(2, row_count.bit_length() - 1))
    plan_x = Plan([0, 1, "group"], row_count)
    plan_y = Plan([1, 0, "group"], row_count)
    group_first = Plan(["group", 0, 1], row_count)
    last_x = Plan([0, 1] + upper, row_count)
    last_y = Plan([1, 0] + upper, row_count)

    other_inputs = swap_mem(inputs)
    other_memory = swap_mem(memory)
    pair_seg = jnp.concatenate([memory_seg, swap_mem(memory_seg)])

    self_saved = attention_forward(
        True,
        target_seg,
        target_seg,
        inputs,
        (),
        (self_query, self_key, self_value, self_out),
        norm_params,
    )
    self_o, normal_one, inverse_one, low_one = self_saved[3], *self_saved[5:]
    cross_saved = attention_forward(
        False,
        target_seg,
        pair_seg,
        low_one,
        (normal_one, memory, other_memory),
        (cross_query, cross_key, cross_value, cross_out),
        norm_params,
    )
    cross_saved, (other_inputs, other_self_o, other_one) = beside(
        cross_saved, (other_inputs, swap_mem(self_o), swap_mem(low_one))
    )
    cross_o, normal_two, inverse_two, low_two = cross_saved[3], *cross_saved[5:]
    outputs = feed_forward(
        core, low_two, normal_two, expand_weight, contract_weight, norm_params, out_grad
    )
    outputs, (other_cross_o, other_two) = beside(outputs, (swap_mem(cross_o), swap_mem(low_two)))
    (active, slope, layer_out, grad_three, low_three, send_three, keep_three, norm_three) = outputs
    outputs = feed_backward(False, core, low_three, contract_weight, slope, expand_weight)
    (send_wide, part_two), (other_active, got_three) = beside(
        outputs, (swap_mem(active), swap_mem(send_three))
    )

    contract_x, contract_y = wide_grads(
        chip, active, other_active, keep_three, got_three, [plan_x, plan_y]
    )
    outputs = feed_backward(
        True,
        core,
        tie(low_three, contract_x.sent, contract_y.sent),
        contract_weight,
        slope,
        expand_weight,
        part_two,
        grad_three,
        normal_two,
        inverse_two,
        norm_params,
    )
    outputs, got_wide = beside(outputs, swap_mem(send_wide))
    (keep_wide, grad_two, low_grad_two, send_two, keep_two, norm_two) = outputs
    expand, expand_x = weight_grads(
        chip,
        [(low_two, other_two)],
        [(keep_wide, got_wide)],
        [(0, 0)] * 4,
        512,
        [(2, group_first), (2, plan_x)],
        (contract_x, contract_y),
    )
    contract_x.advance()
    contract_y.advance()
    got_two = swap_mem(send_two)

    (send_c, keep_c, grad_one, low_grad_one, send_one, keep_one, norm_one, mem_own, mem_send) = (
        attention_backward(
            False,
            core,
            target_seg,
            pair_seg,
            tie(low_grad_two, expand.sent, expand_x.sent, contract_x.sent, contract_y.sent),
            cross_out,
            (cross_saved[0], cross_saved[1], cross_saved[2], cross_o, cross_saved[4]),
            (cross_query, cross_key, cross_value),
            grad_two,
            (normal_one, inverse_one, norm_params),
        )
    )
    (send_c, keep_c, grad_one, low_grad_one, send_one, keep_one, norm_one, mem_own, mem_send) = during(
        (send_c, keep_c, grad_one, low_grad_one, send_one, keep_one, norm_one, mem_own, mem_send),
        contract_x,
        contract_y,
        expand_x,
    )
    norm_grad = jnp.concatenate([norm_one, norm_two, norm_three])
    norm_grad = norm_grad.reshape(2, 3, norm_grad.shape[1])
    norm_half = norm_grad[core[0]] + swap_mem(norm_grad[1 - core[0]])
    got_c = swap_mem(send_c)
    got_one = swap_mem(send_one)
    merged = [chain.merged() for chain in (contract_x, contract_y)]
    contract_sums = group_sum_joined(plan_x, merged)
    expand_x.advance()
    memory_grad = (mem_own.astype(F32) + swap_mem(mem_send).astype(F32)).astype(BF)
    block_rows = inputs.shape[1] // row_count
    norm_blocks = norm_half.reshape(3, row_count, block_rows).transpose(1, 0, 2)
    norm_blocks = jnp.take(norm_blocks, last_y.at_places(chip), axis=0)
    norm_chain = Chain(last_y, norm_blocks.reshape((2, -1) + norm_blocks.shape[1:]).astype(BF))
    pair_memory = jnp.concatenate([memory, other_memory])
    turned_memory = jnp.concatenate([other_memory, memory])
    cross_x, cross_y = weight_grads(
        chip,
        [
            (tie(cross_o, merged, expand_x.sent, norm_chain.sent, memory_grad), other_cross_o),
            (low_one, other_one),
            (pair_memory, turned_memory),
            (self_o, other_self_o),
        ],
        [(keep_two, got_two), (keep_c, got_c), (keep_one, got_one)],
        [(0, 0)] * 2 + [(1, 1)] * 2 + [(2, 1)] * 4 + [(3, 2)] * 2,
        256,
        [(5, plan_x), (5, plan_y)],
        (expand_x, expand, norm_chain),
    )
    expand_x.advance()
    expand.advance()
    norm_chain.advance()

    send_s, keep_s, input_grad = attention_backward(
        True,
        core,
        target_seg,
        target_seg,
        tie(
            low_grad_one, cross_x.sent, cross_y.sent, expand.sent, expand_x.sent, norm_chain.sent
        ),
        self_out,
        (self_saved[0], self_saved[1], self_saved[2], self_o, self_saved[4]),
        (self_query, self_key, self_value),
        grad_one,
        (),
    )
    send_s, keep_s, input_grad = during(
        (send_s, keep_s, input_grad), cross_x, cross_y, expand, norm_chain
    )
    got_s = swap_mem(send_s)
    cross_x.advance()
    cross_y.advance()
    expand.advance()
    norm_chain.advance()
    self_chains = weight_grads(
        chip,
        [(tie(inputs, cross_x.sent, cross_y.sent, expand.sent, norm_chain.sent), other_inputs)],
        [(keep_s, got_s)],
        [(0, 0)] * 6,
        256,
        [(3, last_x), (3, last_y)],
        (cross_x, cross_y, expand, norm_chain),
    )
    started = [chain.sent for chain in self_chains]
    merged = [chain.merged() for chain in (cross_x, cross_y)]
    cross_sums = group_sum_joined(plan_x, merged)
    norm_chain.hold(merged)
    norm_chain.advance()
    for chain in self_chains:
        chain.hold(merged, norm_chain.sent)
    while self_chains[0].left:
        for chain in self_chains + [norm_chain]:
            if chain.left:
                chain.advance()
    own_lanes = self_out.shape[1] // 2
    self_sum = jnp.concatenate([chain.result() for chain in self_chains], axis=1)
    cross_sum = jnp.concatenate(cross_sums, axis=1).astype(F32)
    cross_parts = [cross_sum[:, at * own_lanes : (at + 1) * own_lanes] for at in range(5)]
    return (
        layer_out,
        input_grad,
        memory_grad,
        self_sum[:, :own_lanes],
        self_sum[:, own_lanes : 2 * own_lanes],
        self_sum[:, 2 * own_lanes :],
        cross_parts[4],
        cross_parts[1],
        cross_parts[2],
        cross_parts[3],
        cross_parts[0],
        jnp.concatenate([expand.result(), expand_x.result()], axis=1),
        jnp.concatenate(contract_sums, axis=1).astype(F32),
        norm_chain.result()[0],
    )


def solution(mesh):
    split_rows = P(("row", "mem"), None)
    split_ids = P(("row", "mem"))
    in_specs = (split_rows, split_rows, split_ids, split_ids) + (P(),) * 11 + (split_rows,)
    out_specs = (split_rows,) * 3 + (P("row", "mem"),) * 10 + (P("mem", "row"),)
    return jax.shard_map(
        partial(shards, mesh.shape["row"]),
        mesh=mesh,
        in_specs=in_specs,
        out_specs=out_specs,
        check_vma=False,
    )
```

```python
from functools import partial

import jax
import jax.numpy as jnp
import numpy as np
from jax import lax
from jax.experimental import pallas as pl
from jax.experimental.pallas import tpu as pltpu
from jax.sharding import PartitionSpec as P

HEADS = 16
HEAD_DIM = 64
GROUP = 256
PAIR = 128

ALPHA = 300.0**0.25
SCALE = 0.125
NEG = -1e30
EPS = 1e-05

BF = jnp.bfloat16
F32 = jnp.float32
VMEM_LIMIT = 56 * 2**20


def mul(left, right, left_axis, right_axis):
    return lax.dot_general(
        left, right, (((left_axis,), (right_axis,)), ((), ())), preferred_element_type=F32
    )


def mul_nn(left, right):
    return mul(left, right, 1, 0)


def mul_nt(left, right):
    return mul(left, right, 1, 1)


def mul_tn(left, right):
    return mul(left, right, 0, 0)


def kernel_call(body, grid, in_specs, out_specs, out_shape, scratch, moved, scalars=0):
    return pl.pallas_call(
        body,
        grid_spec=pltpu.PrefetchScalarGridSpec(
            num_scalar_prefetch=scalars,
            grid=grid,
            in_specs=in_specs,
            out_specs=out_specs,
            scratch_shapes=scratch,
        ),
        out_shape=out_shape,
        compiler_params=pltpu.CompilerParams(vmem_limit_bytes=VMEM_LIMIT),
        cost_estimate=pl.CostEstimate(
            flops=1, bytes_accessed=int(moved * 2**20), transcendentals=0
        ),
    )


def whole(shape):
    return pl.BlockSpec(shape, lambda *_: (0,) * len(shape))


def shape_of(shape, dtype):
    return jax.ShapeDtypeStruct(shape, dtype)


def by_rows(rows, step, body):
    def one(at, carry):
        body(pl.ds(pl.multiple_of(at * step, step), step))
        return carry

    lax.fori_loop(0, rows // step, one, 0)


def normalize(value):
    middle = jnp.mean(value, -1, keepdims=True)
    centred = value - middle
    spread = jnp.mean(centred * centred, -1, keepdims=True)
    inverse = lax.rsqrt(spread + EPS)
    return centred * inverse, inverse


def normalize_back(cotangent, normal, inverse, gain_row):
    scaled = cotangent * gain_row
    first = jnp.mean(scaled, -1, keepdims=True)
    second = jnp.mean(scaled * normal, -1, keepdims=True)
    grad = (scaled - first - normal * second) * inverse
    gain_term = jnp.sum(cotangent * normal, 0, keepdims=True)
    bias_term = jnp.sum(cotangent, 0, keepdims=True)
    return grad, gain_term, bias_term


def head_masks():
    lane = lax.broadcasted_iota(jnp.int32, (1, PAIR), 1)
    first = (lane < HEAD_DIM).astype(F32)
    return (first.astype(BF), (1.0 - first).astype(BF))


def head_masks_scaled():
    lane = lax.broadcasted_iota(jnp.int32, (1, PAIR), 1)
    first = (lane < HEAD_DIM).astype(F32)
    return ((first * SCALE).astype(BF), ((1.0 - first) * SCALE).astype(BF))


def fill_bias(bias, row_seg, key_seg, causal):
    rows, keys = bias.shape

    def block(at):
        allowed = row_seg[at, :] == key_seg[...]
        if causal:
            row_pos = at.start + lax.broadcasted_iota(jnp.int32, (64, keys), 0)
            key_pos = lax.broadcasted_iota(jnp.int32, (64, keys), 1)
            allowed = allowed & (row_pos >= key_pos)
        bias[at, :] = jnp.where(allowed, 0.0, NEG)

    by_rows(rows, 64, block)


def row_parts(rows, keys, causal):
    half = rows // 2
    if causal:
        return ((0, half, half), (half, half, rows))
    return ((0, half, keys), (half, half, keys))


def forward_body(causal, *refs):
    if causal:
        (row_seg, key_seg, source, w_query, w_key, w_value, w_out, norms) = refs[:8]
        rest = refs[8:]
        key_source = (source,)
    else:
        (row_seg, key_seg, source, normal_in, own, other) = refs[:6]
        (w_query, w_key, w_value, w_out, norms) = refs[6:11]
        rest = refs[11:]
        key_source = (own, other)
    (q_out, k_out, v_out, o_out, lse_out, normal_out, inverse_out, low_out) = rest[:8]
    bias, total = rest[8:10]
    step = pl.program_id(0)
    rows = source.shape[0]
    keys = bias.shape[1]

    @pl.when(step == 0)
    def _():
        fill_bias(bias, row_seg, key_seg, causal)
        total[...] = jnp.zeros_like(total)

    q_out[...] = mul_nn(source[...], w_query[...]).astype(BF)
    at = 0
    for part in key_source:
        size = part.shape[0]
        k_out[at : at + size, :] = mul_nn(part[...], w_key[...]).astype(BF)
        v_out[at : at + size, :] = mul_nn(part[...], w_value[...]).astype(BF)
        at += size
    scaled = head_masks_scaled()
    lane = lax.broadcasted_iota(jnp.int32, (1, PAIR), 1)
    for begin, size, seen in row_parts(rows, keys, causal):
        rows_at = slice(begin, begin + size)
        scores = []
        for pair in range(GROUP // PAIR):
            lanes = slice(pair * PAIR, (pair + 1) * PAIR)
            query = q_out[rows_at, lanes]
            key = k_out[:seen, lanes]
            for head in range(2):
                scores.append(mul_nt(query * scaled[head], key) + bias[rows_at, :seen])
        lse_block = jnp.zeros((size, PAIR), F32)
        for pair in range(GROUP // PAIR):
            lanes = slice(pair * PAIR, (pair + 1) * PAIR)
            value = v_out[:seen, lanes]
            outs = []
            for head in range(2):
                score = scores[pair * 2 + head]
                top = jnp.max(score, -1, keepdims=True)
                weights = jnp.exp(score - top)
                weight_sum = jnp.sum(weights, -1, keepdims=True)
                outs.append(mul_nn(weights.astype(BF), value) * (1.0 / weight_sum))
                lse_block = jnp.where(
                    lane == pair * 2 + head, top + jnp.log(weight_sum), lse_block
                )
            o_out[rows_at, lanes] = jnp.where(lane < HEAD_DIM, outs[0], outs[1]).astype(BF)
        lse_out[rows_at, :] = lse_block
    total[...] += mul_nn(o_out[...], w_out[...])

    @pl.when(step == pl.num_programs(0) - 1)
    def _():
        def block(at):
            if causal:
                base = source[at, :].astype(F32)
                gain, shift = norms[0:1, :], norms[1:2, :]
            else:
                base = normal_in[at, :] * norms[0:1, :] + norms[1:2, :]
                gain, shift = norms[2:3, :], norms[3:4, :]
            normal, inverse = normalize(ALPHA * base + total[at, :])
            normal_out[at, :] = normal
            inverse_out[at, :] = inverse
            low_out[at, :] = (normal * gain + shift).astype(BF)

        by_rows(rows, 128, block)


def attention_forward(causal, row_seg, key_seg, source, extra, weights, norms):
    rows, width = source.shape
    keys = key_seg.shape[0]
    steps = width // GROUP
    columns = pl.BlockSpec((width, GROUP), lambda g: (0, g))
    in_specs = [whole((rows, 1)), whole((1, keys)), whole((rows, width))]
    operands = [row_seg.reshape(rows, 1), key_seg.reshape(1, keys), source]
    for item in extra:
        in_specs.append(whole(item.shape))
        operands.append(item)
    in_specs += [columns] * 3 + [pl.BlockSpec((GROUP, width), lambda g: (g, 0))]
    in_specs.append(whole(norms.shape))
    row_block = pl.BlockSpec((rows, GROUP), lambda g: (0, g))
    key_block = pl.BlockSpec((keys, GROUP), lambda g: (0, g))
    out_specs = [
        row_block,
        key_block,
        key_block,
        row_block,
        pl.BlockSpec((rows, PAIR), lambda g: (0, g)),
        whole((rows, width)),
        whole((rows, 1)),
        whole((rows, width)),
    ]
    out_shape = [
        shape_of((rows, width), BF),
        shape_of((keys, width), BF),
        shape_of((keys, width), BF),
        shape_of((rows, width), BF),
        shape_of((rows, PAIR * steps), F32),
        shape_of((rows, width), F32),
        shape_of((rows, 1), F32),
        shape_of((rows, width), BF),
    ]
    scratch = [pltpu.VMEM((rows, keys), F32), pltpu.VMEM((rows, width), F32)]
    call = kernel_call(
        partial(forward_body, causal), (steps,), in_specs, out_specs, out_shape, scratch, 30
    )
    return call(*operands, *weights, norms)


def gelu_parts(value):
    share = 0.5 + 0.5 * lax.erf(value * 0.5**0.5)
    bell = jnp.exp(value * value * -0.5) * (0.5 / np.pi) ** 0.5
    return value * share, share + value * bell


def expand_body(
    core, low, normal_in, w_expand, w_contract, norms, out_grad,
    active_out, slope_out, layer_out, grad_out, low_grad, send_grad, keep_grad, norm_out,
    total,
):
    step = pl.program_id(0)
    rows, width = low.shape

    @pl.when(step == 0)
    def _():
        total[...] = jnp.zeros_like(total)

    size = rows // 2
    spans = [slice(part * size, (part + 1) * size) for part in range(2)]
    values = [mul_nn(low[at, :], w_expand[...]) for at in spans]
    for at, value in zip(spans, values):
        active, slope = gelu_parts(value)
        active = active.astype(BF)
        active_out[at, :] = active
        slope_out[at, :] = slope.astype(BF)
        total[at, :] += mul_nn(active, w_contract[...])

    @pl.when(step == pl.num_programs(0) - 1)
    def _():
        norm_out[...] = jnp.zeros_like(norm_out)
        half = width // 2
        is_low = core[0] == 0

        def block(at):
            base = normal_in[at, :] * norms[2:3, :] + norms[3:4, :]
            normal, inverse = normalize(ALPHA * base + total[at, :])
            layer_out[at, :] = (normal * norms[4:5, :] + norms[5:6, :]).astype(BF)
            grad, gain_term, bias_term = normalize_back(
                out_grad[at, :].astype(F32), normal, inverse, norms[4:5, :]
            )
            norm_out[0:1, :] += gain_term
            norm_out[1:2, :] += bias_term
            grad_out[at, :] = grad
            low_grad[at, :] = grad.astype(BF)
            left, right = grad[:, :half], grad[:, half:]
            keep_grad[at, :] = jnp.where(is_low, left, right).astype(BF)
            send_grad[at, :] = jnp.where(is_low, right, left).astype(BF)

        by_rows(rows, 128, block)


def feed_forward(core, low, normal, w_expand, w_contract, norms, out_grad):
    rows, width = low.shape
    wide = w_expand.shape[1]
    chunk = 512
    steps = wide // chunk
    in_specs = [
        whole((rows, width)),
        whole((rows, width)),
        pl.BlockSpec((width, chunk), lambda c, _: (0, c)),
        pl.BlockSpec((chunk, width), lambda c, _: (c, 0)),
        whole(norms.shape),
        whole((rows, width)),
    ]
    wide_block = pl.BlockSpec((rows, chunk), lambda c, _: (0, c))
    out_specs = [wide_block, wide_block] + [whole((rows, width))] * 3
    out_specs += [whole((rows, width // 2))] * 2 + [whole((2, width))]
    out_shape = [
        shape_of((rows, wide), BF),
        shape_of((rows, wide), BF),
        shape_of((rows, width), BF),
        shape_of((rows, width), F32),
        shape_of((rows, width), BF),
        shape_of((rows, width // 2), BF),
        shape_of((rows, width // 2), BF),
        shape_of((2, width), F32),
    ]
    call = kernel_call(
        expand_body,
        (steps,),
        in_specs,
        out_specs,
        out_shape,
        [pltpu.VMEM((rows, width), F32)],
        34,
        scalars=1,
    )
    return call(core, low, normal, w_expand, w_contract, norms, out_grad)


def send_first(step, steps, core):
    half = steps // 2
    later = step // half
    return jnp.where(later == 0, 1 - core[0], core[0]) * half + step % half


def contract_back_body(last, core, *refs):
    low_grad, w_contract, slope, w_expand = refs[:4]
    if last:
        (total_in, grad_in, normal_in, inverse_in, norms) = refs[4:9]
        (wide_out, grad_out, low_out, send_low, keep_low, norm_out, total) = refs[9:]
    else:
        wide_out, total = refs[4:]
    step = pl.program_id(0)
    rows, width = low_grad.shape

    @pl.when(step == 0)
    def _():
        total[...] = total_in[...] if last else jnp.zeros_like(total)

    size = rows // 2
    spans = [slice(part * size, (part + 1) * size) for part in range(2)]
    values = [mul_nt(low_grad[at, :], w_contract[...]) for at in spans]
    for at, value in zip(spans, values):
        wide_grad = (value * slope[at, :].astype(F32)).astype(BF)
        wide_out[at, :] = wide_grad
        total[at, :] += mul_nt(wide_grad, w_expand[...])

    if not last:
        return

    @pl.when(step == pl.num_programs(0) - 1)
    def _():
        norm_out[...] = jnp.zeros_like(norm_out)
        half = width // 2
        is_low = core[0] == 0

        def block(at):
            grad, gain_term, bias_term = normalize_back(
                ALPHA * grad_in[at, :] + total[at, :],
                normal_in[at, :],
                inverse_in[at, :],
                norms[2:3, :],
            )
            norm_out[0:1, :] += gain_term
            norm_out[1:2, :] += bias_term
            grad_out[at, :] = grad
            low_out[at, :] = grad.astype(BF)
            left, right = grad[:, :half], grad[:, half:]
            keep_low[at, :] = jnp.where(is_low, left, right).astype(BF)
            send_low[at, :] = jnp.where(is_low, right, left).astype(BF)

        by_rows(rows, 128, block)


def feed_backward(last, core, low_grad, w_contract, slope, w_expand, *rest):
    rows, width = low_grad.shape
    wide = w_expand.shape[1]
    chunk = 512
    steps = wide // chunk // 2

    def at(s, core):
        return (core[0] if last else 1 - core[0]) * steps + s

    in_specs = [
        whole((rows, width)),
        pl.BlockSpec((chunk, width), lambda s, core: (at(s, core), 0)),
        pl.BlockSpec((rows, chunk), lambda s, core: (0, at(s, core))),
        pl.BlockSpec((width, chunk), lambda s, core: (0, at(s, core))),
    ] + [whole(item.shape) for item in rest]
    out_specs = [pl.BlockSpec((rows, chunk), lambda s, _: (0, s)), whole((rows, width))]
    out_shape = [shape_of((rows, wide // 2), BF), shape_of((rows, width), F32)]
    scratch = []
    if last:
        out_specs += [whole((rows, width))] + [whole((rows, width // 2))] * 2 + [whole((2, width))]
        out_shape += [
            shape_of((rows, width), BF),
            shape_of((rows, width // 2), BF),
            shape_of((rows, width // 2), BF),
            shape_of((2, width), F32),
        ]
        scratch = [pltpu.VMEM((rows, width), F32)]
    call = kernel_call(
        partial(contract_back_body, last),
        (steps,),
        in_specs,
        out_specs,
        out_shape,
        scratch,
        18,
        scalars=1,
    )
    return call(core, low_grad, w_contract, slope, w_expand, *rest)


def add_rows(parts):
    first, last = parts
    rows = first.shape[0]
    if rows == last.shape[0]:
        return first + last
    return jnp.concatenate([first + last[:rows], last[rows:]])


def backward_body(causal, core, *refs):
    (row_seg, key_seg, low_grad, w_out, query_in, key_in, value_in, o_in, lse_in) = refs[:9]
    if causal:
        (send_out, keep_out, bias) = refs[9:]
    else:
        (w_query, grad_in, normal_in, inverse_in, norms) = refs[9:14]
        (send_out, keep_out, grad_out, low_out, send_low, keep_low, norm_out) = refs[14:21]
        (bias, total) = refs[21:]
    step = pl.program_id(0)
    steps = pl.num_programs(0)
    rows, width = low_grad.shape
    keys = bias.shape[1]

    @pl.when(step == 0)
    def _():
        fill_bias(bias, row_seg, key_seg, causal)
        if not causal:
            total[...] = jnp.zeros_like(total)

    o_grad = mul_nt(low_grad[...], w_out[...]).astype(BF)
    plain = head_masks()
    scaled = head_masks_scaled()
    first_lanes = lax.broadcasted_iota(jnp.int32, (1, PAIR), 1) < HEAD_DIM
    query_grads, key_grads, value_grads = [], [], []
    for pair in range(GROUP // PAIR):
        lanes = slice(pair * PAIR, (pair + 1) * PAIR)
        started = []
        for begin, size, seen in row_parts(rows, keys, causal):
            rows_at = slice(begin, begin + size)
            query = query_in[rows_at, lanes]
            grad = o_grad[rows_at, lanes]
            key = key_in[:seen, lanes]
            value = value_in[:seen, lanes]
            product = grad.astype(F32) * o_in[rows_at, lanes].astype(F32)
            head_queries = [query * scaled[head] for head in range(2)]
            head_grads = [grad * plain[head] for head in range(2)]
            scores = [mul_nt(item, key) for item in head_queries]
            prob_grads = [mul_nt(item, value) for item in head_grads]
            started.append(
                (rows_at, seen, key, product, head_queries, head_grads, scores, prob_grads)
            )
        query_parts, key_parts, value_parts = [], [], []
        for rows_at, seen, key, product, head_queries, head_grads, scores, prob_grads in started:
            probs, score_grads = [], []
            for head in range(2):
                mine = first_lanes if head == 0 else jnp.logical_not(first_lanes)
                delta = jnp.sum(jnp.where(mine, product, 0.0), -1, keepdims=True)
                lse = lse_in[rows_at, pair * 2 + head : pair * 2 + head + 1]
                prob = jnp.exp(scores[head] + bias[rows_at, :seen] - lse)
                score_grads.append((prob * (prob_grads[head] - delta)).astype(BF))
                probs.append(prob.astype(BF))
            value_parts.append(mul_tn(jnp.concatenate(probs), jnp.concatenate(head_grads)))
            stacked = jnp.concatenate(score_grads)
            key_parts.append(mul_tn(stacked, jnp.concatenate(head_queries)))
            wide = jnp.concatenate(score_grads, axis=1)
            head_keys = jnp.concatenate([key * scaled[0], key * scaled[1]])
            query_parts.append(mul_nn(wide, head_keys))
        query_grads.append(jnp.concatenate(query_parts).astype(BF))
        key_grads.append(add_rows(key_parts).astype(BF))
        value_grads.append(add_rows(value_parts).astype(BF))
    query_grad = jnp.concatenate(query_grads, axis=1)
    key_grad = jnp.concatenate(key_grads, axis=1)
    value_grad = jnp.concatenate(value_grads, axis=1)

    @pl.when(step < steps // 2)
    def _():
        send_out[0], send_out[1], send_out[2] = query_grad, key_grad, value_grad

    @pl.when(step >= steps // 2)
    def _():
        keep_out[0], keep_out[1], keep_out[2] = query_grad, key_grad, value_grad

    if causal:
        return
    total[...] += mul_nt(query_grad, w_query[...])

    @pl.when(step == steps - 1)
    def _():
        norm_out[...] = jnp.zeros_like(norm_out)
        half = width // 2
        is_low = core[0] == 0

        def block(at):
            grad, gain_term, bias_term = normalize_back(
                ALPHA * grad_in[at, :] + total[at, :],
                normal_in[at, :],
                inverse_in[at, :],
                norms[0:1, :],
            )
            norm_out[0:1, :] += gain_term
            norm_out[1:2, :] += bias_term
            grad_out[at, :] = grad
            low_out[at, :] = grad.astype(BF)
            left, right = grad[:, :half], grad[:, half:]
            keep_low[at, :] = jnp.where(is_low, left, right).astype(BF)
            send_low[at, :] = jnp.where(is_low, right, left).astype(BF)

        by_rows(rows, 128, block)


def project_back_body(items, core, send, keep, *refs):
    weights = refs[: len(items)]
    rest = refs[len(items) :]
    total = rest[-1]
    step = pl.program_id(0)
    steps = pl.num_programs(0)
    joined_weights = jnp.concatenate([weight[...] for weight in weights], axis=1)

    @pl.when(step == 0)
    def _():
        total[...] = jnp.zeros_like(total)

    for source, first in ((send, 0), (keep, steps // 2)):

        @pl.when((step >= first) & (step < first + steps // 2))
        def _():
            joined = jnp.concatenate([source[item] for item in items], axis=1)
            total[...] += mul_nt(joined, joined_weights)

    @pl.when(step == steps - 1)
    def _():
        if len(rest) == 3 and rest[0].dtype == F32:
            grad_in, out = rest[:2]

            def block(at):
                out[at, :] = (ALPHA * grad_in[at, :] + total[at, :]).astype(BF)

            by_rows(out.shape[0], 64, block)
        else:
            own, other = rest[:2]
            rows = own.shape[0]
            own[...] = total[:rows, :].astype(BF)
            other[...] = total[rows:, :].astype(BF)


def project_back(core, send, keep, items, weights, grad=None):
    count, rows, half = send.shape
    width = weights[0].shape[0]
    steps = 2 * half // GROUP
    in_specs = [
        pl.BlockSpec((count, rows, GROUP), lambda s, _: (0, 0, jnp.minimum(s, steps // 2 - 1))),
        pl.BlockSpec((count, rows, GROUP), lambda s, _: (0, 0, jnp.maximum(s - steps // 2, 0))),
    ]
    columns = pl.BlockSpec((width, GROUP), lambda s, core: (0, send_first(s, steps, core)))
    in_specs += [columns] * len(weights)
    extra = [] if grad is None else [grad]
    in_specs += [whole(item.shape) for item in extra]
    outs = [(rows, width)] if extra else [(rows // 2, width)] * 2
    call = kernel_call(
        partial(project_back_body, items),
        (steps,),
        in_specs,
        [whole(out) for out in outs],
        [shape_of(out, BF) for out in outs],
        [pltpu.VMEM((rows, width), F32)],
        0,
        scalars=1,
    )
    return call(core, send, keep, *weights, *extra)


def attention_backward(causal, core, row_seg, key_seg, low_grad, w_out, saved, extra):
    rows, width = low_grad.shape
    keys = key_seg.shape[0]
    steps = width // GROUP
    half = steps // 2

    def block(shape, spread):
        def index(s, core):
            group = send_first(s, steps, core)
            return (group, 0) if spread == 0 else (0, group)

        return pl.BlockSpec(shape, index)

    row_block = block((rows, GROUP), 1)
    key_block = block((keys, GROUP), 1)
    columns = block((width, GROUP), 1)
    in_specs = [
        whole((rows, 1)),
        whole((1, keys)),
        whole((rows, width)),
        block((GROUP, width), 0),
        row_block,
        key_block,
        key_block,
        row_block,
        block((rows, PAIR), 1),
    ]
    if not causal:
        in_specs += [columns]
    in_specs += [whole(item.shape) for item in extra[1:]]
    out_specs = [
        pl.BlockSpec((3, rows, GROUP), lambda s, _: (0, 0, jnp.minimum(s, half - 1))),
        pl.BlockSpec((3, rows, GROUP), lambda s, _: (0, 0, jnp.maximum(s - half, 0))),
    ]
    out_shape = [shape_of((3, rows, width // 2), BF)] * 2
    scratch = [pltpu.VMEM((rows, keys), F32)]
    if not causal:
        out_specs += [whole((rows, width))] * 2 + [whole((rows, width // 2))] * 2
        out_specs += [whole((2, width))]
        out_shape += [
            shape_of((rows, width), F32),
            shape_of((rows, width), BF),
            shape_of((rows, width // 2), BF),
            shape_of((rows, width // 2), BF),
            shape_of((2, width), F32),
        ]
        scratch += [pltpu.VMEM((rows, width), F32)]
    call = kernel_call(
        partial(backward_body, causal),
        (steps,),
        in_specs,
        out_specs,
        out_shape,
        scratch,
        44,
        scalars=1,
    )
    return call(
        core,
        row_seg.reshape(rows, 1),
        key_seg.reshape(1, keys),
        low_grad,
        w_out,
        *saved,
        *extra,
    )


def swap_mem(tensor):
    return lax.ppermute(tensor, "mem", [(0, 1), (1, 0)])


def tie(value, *after):
    return lax.optimization_barrier((value, after))[0]


def beside(outputs, arrays):
    return lax.optimization_barrier((outputs, arrays))


def during(outputs, *chains):
    outputs, terms = lax.optimization_barrier((outputs, [chain.terms for chain in chains]))
    for chain, items in zip(chains, terms):
        chain.terms = items
    return outputs


class Plan:
    def __init__(self, steps, row_count):
        self.steps = steps
        self.row_count = row_count
        sizes = [self.pieces(step) for step in steps]
        self.relative, self.fixed = [], []
        for k in range(row_count):
            mask = fixed = 0
            rest = row_count
            for step, size in zip(steps, sizes):
                rest //= size
                digit = k // rest % size
                if step == "group":
                    fixed = digit << 2
                elif step == "plane":
                    mask |= digit
                else:
                    mask |= digit << step
            self.relative.append(mask)
            self.fixed.append(fixed)
        self.groups = [list(range(low, row_count, 4)) for low in range(4)]

    def pieces(self, step):
        if step == "group":
            return self.row_count // 4
        return 4 if step == "plane" else 2

    def first_pieces(self):
        return 1 if self.steps[0] == "group" else self.pieces(self.steps[0])

    def block_at(self, chip, k):
        own = (chip & 3) if "group" in self.steps else chip
        return (own ^ self.relative[k]) | self.fixed[k]

    def place_of(self, chip, block):
        own = (chip & 3) if "group" in self.steps else chip
        apart = own ^ block
        place = 0
        for step in self.steps:
            size = self.pieces(step)
            if step == "group":
                digit = apart >> 2
            elif step == "plane":
                digit = apart & 3
            else:
                digit = (apart >> step) & 1
            place = place * size + digit
        return place

    def at_places(self, chip):
        own = (chip & 3) if "group" in self.steps else chip
        return (own ^ jnp.asarray(self.relative, jnp.int32)) | jnp.asarray(self.fixed, jnp.int32)

    def permute(self, tensor, mask):
        pairs = [(i, i ^ mask) for i in range(self.row_count)]
        return lax.ppermute(tensor, "row", pairs)

    def group_sum(self, tensor):
        return lax.psum_scatter(
            tensor, "row", scatter_dimension=0, tiled=True, axis_index_groups=self.groups
        )


def group_sum_joined(plan, tensors, lanes):
    count = plan.row_count // 4
    pieces, sizes = [], []
    for tensor in tensors:
        blocks = tensor.reshape(count, -1, tensor.shape[1])
        sizes.append(blocks.shape[1:])
        pieces += [blocks[:, :, at : at + lanes] for at in range(0, blocks.shape[2], lanes)]
    joined = jnp.concatenate(pieces, axis=1)
    return joined, sizes, plan.group_sum(joined)[0]


def parted(summed, sizes, lanes):
    outs, at = [], 0
    for rows, width in sizes:
        parts = []
        for _ in range(width // lanes):
            parts.append(summed[at : at + rows])
            at += rows
        outs.append(jnp.concatenate(parts, axis=1) if len(parts) > 1 else parts[0])
    return outs


class Chain:
    def __init__(self, plan, blocks):
        self.plan = plan
        self.left = list(plan.steps)
        self.launch(list(blocks))

    def launch(self, pieces):
        step = self.left.pop(0)
        if step == "group":
            self.sent = pieces
            self.terms = [self.plan.group_sum(pieces[0])]
            return
        self.sent = pieces[1:]
        masks = [1, 2, 3] if step == "plane" else [1 << step]
        got = [self.plan.permute(piece, mask) for piece, mask in zip(self.sent, masks)]
        self.terms = [pieces[0]] + got

    def hold(self, *after):
        got = self.terms[1:] if len(self.terms) > 1 else self.terms
        self.terms[-len(got) :] = tie(got, *after)

    def sum_rows(self, rows):
        total = self.terms[0][rows].astype(F32)
        for term in self.terms[1:]:
            total = total + term[rows].astype(F32)
        return total

    def merged(self):
        assert self.left.pop(0) == "group"
        return self.sum_rows(slice(None)).astype(BF)

    def advance(self):
        step = self.left[0]
        count = 1 if step == "group" else self.plan.pieces(step)
        rows = self.terms[0].shape[0] // count
        self.launch(
            [self.sum_rows(slice(k * rows, (k + 1) * rows)).astype(BF) for k in range(count)]
        )

    def result(self):
        assert not self.left
        return self.sum_rows(slice(None))


def joined_chain(chains, plan):
    half = chains[0].terms[0].shape[0] // 2
    blocks = []
    for rows in (slice(None, half), slice(half, None)):
        blocks.append(jnp.concatenate([chain.sum_rows(rows) for chain in chains], axis=1).astype(BF))
    return Chain(plan, blocks)


def swap_mem(tensor):
    return lax.ppermute(tensor, "mem", [(0, 1), (1, 0)])


def weight_grads_body(spans, sources_count, grads_count, step_table, count, chip, *refs):
    sources = refs[: 2 * sources_count]
    grads = refs[2 * sources_count : 2 * (sources_count + grads_count)]
    outs = refs[2 * (sources_count + grads_count) : -1]
    whole_grad = refs[-1]
    step = pl.program_id(0)
    _, block_rows, lanes = whole_grad.shape
    joined = max(16 // block_rows, 1)
    for entry in sorted(set(step_table)):
        steps = [at for at, which in enumerate(step_table) if which == entry]

        @pl.when((step >= steps[0]) & (step <= steps[-1]))
        def _():
            own, other = sources[2 * entry[0] : 2 * entry[0] + 2]
            own_grad, other_grad = grads[2 * entry[1] : 2 * entry[1] + 2]
            grad = mul_tn(own[...], own_grad[0]) + mul_tn(other[...], other_grad[0])
            whole_grad[...] = grad.reshape(count, block_rows, lanes)

    at_out = 0
    for begin, chunks, pieces, plan in spans:
        targets = outs[at_out : at_out + pieces]
        at_out += pieces

        @pl.when((step >= begin) & (step < begin + chunks))
        def _():
            size = count // pieces
            for part, out in enumerate(targets):
                for k in range(0, size, joined):
                    places = range(part * size + k, part * size + k + joined)
                    blocks = [whole_grad[plan.block_at(chip[0], place)] for place in places]
                    rows = slice(k * block_rows, (k + joined) * block_rows)
                    out[rows, :] = jnp.concatenate(blocks).astype(BF)


def weight_grads(chip, sources, grads, step_table, chunk, outs, travelling=()):
    tokens, width = sources[0][0].shape
    count = outs[0][1].row_count
    steps = len(step_table)
    in_specs = [whole((tokens, width))] * (2 * len(sources))
    flat = [item for pair in sources for item in pair]
    for number, pair in enumerate(grads):
        pair = [item if item.ndim == 3 else item[None] for item in pair]
        flat += pair
        across = pair[0].shape[2] // chunk
        mine = [at for at, which in enumerate(step_table) if which[1] == number]

        def index(i, _, first=mine[0], last=mine[-1], across=across):
            at = jnp.clip(i, first, last) - first
            return (at // across, 0, at % across)

        in_specs += [pl.BlockSpec((1, tokens, chunk), index)] * 2
    out_specs, out_shape, spans = [], [], []
    begin = 0
    for chunks, plan in outs:
        pieces = plan.first_pieces()

        def index(i, _, begin=begin, chunks=chunks):
            return (0, jnp.clip(i - begin, 0, chunks - 1))

        for _ in range(pieces):
            out_specs.append(pl.BlockSpec((width // pieces, chunk), index))
            out_shape.append(shape_of((width // pieces, chunk * chunks), BF))
        spans.append((begin, chunks, pieces, plan))
        begin += chunks
    call = kernel_call(
        partial(weight_grads_body, spans, len(sources), len(grads), step_table, count),
        (steps,),
        in_specs,
        out_specs,
        out_shape,
        [pltpu.VMEM((count, width // count, chunk), F32)],
        16,
        scalars=1,
    )
    results = during(call(chip.reshape(1), *flat), *travelling)
    chains, at = [], 0
    for _, _, pieces, plan in spans:
        chains.append(Chain(plan, results[at : at + pieces]))
        at += pieces
    return chains


def wide_grads_body(plans, chip, own, other, own_grad, other_grad, *outs):
    step = pl.program_id(0)
    chains = len(outs) // 2
    lanes = outs[0].shape[1]
    block_rows = outs[0].shape[0] * 2 // plans[0].row_count
    blocks = own.shape[1] // block_rows
    size = outs[0].shape[0] // block_rows
    grad = mul_tn(own[...], own_grad[...]) + mul_tn(other[...], other_grad[...])
    grad = grad.astype(BF)
    for block in range(blocks):
        for chain in range(chains):
            part = grad[block * block_rows : (block + 1) * block_rows]
            part = part[:, chain * lanes : (chain + 1) * lanes]
            place = plans[chain].place_of(chip[0], step * blocks + block)
            for half in range(2):

                @pl.when((place >= half * size) & (place < (half + 1) * size))
                def _():
                    row = pl.multiple_of((place - half * size) * block_rows, block_rows)
                    outs[2 * chain + half][pl.ds(row, block_rows), :] = part


def wide_grads(chip, own, other, own_grad, other_grad, plans):
    tokens, width = own.shape
    lanes = own_grad.shape[1]
    chunk = 512
    source = pl.BlockSpec((tokens, chunk), lambda i, _: (0, i))
    out = (width // 2, lanes // len(plans))
    call = kernel_call(
        partial(wide_grads_body, plans),
        (width // chunk,),
        [source] * 2 + [whole((tokens, lanes))] * 2,
        [whole(out)] * (2 * len(plans)),
        [shape_of(out, BF)] * (2 * len(plans)),
        [],
        20,
        scalars=1,
    )
    results = call(chip.reshape(1), own, other, own_grad, other_grad)
    return [Chain(plan, results[2 * at : 2 * at + 2]) for at, plan in enumerate(plans)]


def shards(
    row_count,
    inputs,
    memory,
    target_seg,
    memory_seg,
    self_query,
    self_key,
    self_value,
    self_out,
    cross_query,
    cross_key,
    cross_value,
    cross_out,
    expand_weight,
    contract_weight,
    norm_params,
    out_grad,
):
    core = lax.axis_index("mem").astype(jnp.int32).reshape(1)
    chip = lax.axis_index("row").astype(jnp.int32)
    upper = list(range(2, row_count.bit_length() - 1))
    plan_x = Plan([0, 1, "group"], row_count)
    plan_y = Plan([1, 0, "group"], row_count)
    group_first = Plan(["group", 0, 1], row_count)
    last_x = Plan([0, 1] + upper, row_count)
    last_y = Plan([1, 0] + upper, row_count)
    rest = Plan(upper, row_count)

    self_saved = attention_forward(
        True,
        target_seg,
        target_seg,
        inputs,
        (),
        (self_query, self_key, self_value, self_out),
        norm_params,
    )
    self_saved, (other_memory, other_seg) = beside(
        self_saved, (swap_mem(memory), swap_mem(memory_seg))
    )
    pair_seg = jnp.concatenate([memory_seg, other_seg])
    other_inputs = swap_mem(inputs)
    self_o, normal_one, inverse_one, low_one = self_saved[3], *self_saved[5:]
    cross_saved = attention_forward(
        False,
        target_seg,
        pair_seg,
        low_one,
        (normal_one, memory, other_memory),
        (cross_query, cross_key, cross_value, cross_out),
        norm_params,
    )
    cross_saved, (other_inputs, other_self_o, other_one) = beside(
        cross_saved, (other_inputs, swap_mem(self_o), swap_mem(low_one))
    )
    cross_o, normal_two, inverse_two, low_two = cross_saved[3], *cross_saved[5:]
    outputs = feed_forward(
        core, low_two, normal_two, expand_weight, contract_weight, norm_params, out_grad
    )
    outputs, (other_cross_o, other_two) = beside(outputs, (swap_mem(cross_o), swap_mem(low_two)))
    (active, slope, layer_out, grad_three, low_three, send_three, keep_three, norm_three) = outputs
    outputs = feed_backward(False, core, low_three, contract_weight, slope, expand_weight)
    (send_wide, part_two), (other_active, got_three) = beside(
        outputs, (swap_mem(active), swap_mem(send_three))
    )

    half = keep_three.shape[1]
    contract_x, contract_y = wide_grads(
        chip, active, other_active, keep_three, got_three, [plan_x, plan_y]
    )
    outputs = feed_backward(
        True,
        core,
        tie(low_three, contract_x.sent, contract_y.sent),
        contract_weight,
        slope,
        expand_weight,
        part_two,
        grad_three,
        normal_two,
        inverse_two,
        norm_params,
    )
    outputs, got_wide = beside(outputs, swap_mem(send_wide))
    (keep_wide, grad_two, low_grad_two, send_two, keep_two, norm_two) = outputs
    expand, expand_x = weight_grads(
        chip,
        [(low_two, other_two)],
        [(keep_wide, got_wide)],
        [(0, 0)] * 4,
        512,
        [(2, group_first), (2, plan_x)],
        (contract_x, contract_y),
    )
    contract_x.advance()
    contract_y.advance()
    got_two = swap_mem(send_two)

    outputs = attention_backward(
        False,
        core,
        target_seg,
        pair_seg,
        tie(low_grad_two, expand.sent, expand_x.sent, contract_x.sent, contract_y.sent),
        cross_out,
        (cross_saved[0], cross_saved[1], cross_saved[2], cross_o, cross_saved[4]),
        (cross_query, grad_two, normal_one, inverse_one, norm_params),
    )
    (send_c, keep_c, grad_one, low_grad_one, send_one, keep_one, norm_one) = during(
        outputs, contract_x, contract_y, expand_x
    )
    norm_grad = jnp.concatenate([norm_one, norm_two, norm_three])
    norm_grad = norm_grad.reshape(2, 3, norm_grad.shape[1])
    norm_half = norm_grad[core[0]] + swap_mem(norm_grad[1 - core[0]])
    got_c = swap_mem(send_c)
    got_one = swap_mem(send_one)
    contract_merged = [chain.merged() for chain in (contract_x, contract_y)]
    expand_x.advance()
    block_rows = inputs.shape[1] // row_count
    norm_blocks = norm_half.reshape(3, row_count, block_rows).transpose(1, 0, 2)
    norm_blocks = jnp.take(norm_blocks, last_y.at_places(chip), axis=0)
    norm_chain = Chain(last_y, norm_blocks.reshape((2, -1) + norm_blocks.shape[1:]).astype(BF))
    pair_memory = jnp.concatenate([memory, other_memory])
    turned_memory = jnp.concatenate([other_memory, memory])
    cross_x, cross_y = weight_grads(
        chip,
        [
            (tie(cross_o, contract_merged, expand_x.sent, norm_chain.sent), other_cross_o),
            (low_one, other_one),
            (pair_memory, turned_memory),
            (self_o, other_self_o),
        ],
        [(keep_two, got_two), (keep_c, got_c), (keep_one, got_one)],
        [(0, 0)] * 2 + [(1, 1)] * 2 + [(2, 1)] * 4 + [(3, 2)] * 2,
        256,
        [(5, last_x), (5, last_y)],
        (expand_x, expand, norm_chain),
    )
    merged = contract_merged + [expand_x.merged()]
    joined, forward_sizes, forward_sum = group_sum_joined(plan_x, merged, half // 2)
    expand.advance()
    norm_chain.advance()

    outputs = attention_backward(
        True,
        core,
        target_seg,
        target_seg,
        tie(
            low_grad_one, cross_x.sent, cross_y.sent, expand.sent, joined, norm_chain.sent
        ),
        self_out,
        (self_saved[0], self_saved[1], self_saved[2], self_o, self_saved[4]),
        (),
    )
    send_s, keep_s = during(outputs, cross_x, cross_y, expand, norm_chain)
    got_s = swap_mem(send_s)
    cross_x.advance()
    cross_y.advance()
    expand.advance()
    norm_chain.advance()
    self_chains = weight_grads(
        chip,
        [(tie(inputs, cross_x.sent, cross_y.sent, expand.sent, norm_chain.sent), other_inputs)],
        [(keep_s, got_s)],
        [(0, 0)] * 6,
        256,
        [(3, last_x), (3, last_y)],
        (cross_x, cross_y, expand),
    )
    started = [chain.sent for chain in self_chains]
    for chain in (cross_x, cross_y):
        chain.hold(started, forward_sum)
    cross_chain = joined_chain((cross_x, cross_y), rest)
    (input_grad,) = project_back(
        core,
        tie(send_s, cross_chain.sent),
        keep_s,
        (0, 1, 2),
        (self_query, self_key, self_value),
        grad_one,
    )
    for chain in self_chains + [cross_chain]:
        chain.hold(input_grad)
        chain.advance()
    mem_own, mem_send = project_back(
        core,
        tie(send_c, [chain.sent for chain in self_chains + [cross_chain]]),
        keep_c,
        (1, 2),
        (cross_key, cross_value),
    )
    for chain in self_chains + [cross_chain]:
        chain.hold(mem_own)
    self_chain = joined_chain(self_chains, rest)
    norm_chain.hold(self_chain.sent)
    norm_chain.advance()
    mem_send, forward_sum, expand.terms, cross_chain.terms = tie(
        (mem_send, forward_sum, expand.terms, cross_chain.terms), self_chain.sent
    )
    memory_grad = (mem_own.astype(F32) + swap_mem(mem_send).astype(F32)).astype(BF)
    forward_parts = [part.astype(F32) for part in parted(forward_sum, forward_sizes, half // 2)]
    contract_result = jnp.concatenate(forward_parts[:2], axis=1)
    expand_result = jnp.concatenate([expand.result(), forward_parts[2]], axis=1)
    self_chain.hold(contract_result, expand_result)
    for chain in (self_chain, cross_chain, norm_chain):
        while chain.left:
            chain.advance()
    self_sum, cross_sum = self_chain.result(), cross_chain.result()
    own_lanes = self_out.shape[1] // 2
    cross_parts = [cross_sum[:, at * own_lanes : (at + 1) * own_lanes] for at in range(5)]
    return (
        layer_out,
        input_grad,
        memory_grad,
        self_sum[:, :own_lanes],
        self_sum[:, own_lanes : 2 * own_lanes],
        self_sum[:, 2 * own_lanes :],
        cross_parts[4],
        cross_parts[1],
        cross_parts[2],
        cross_parts[3],
        cross_parts[0],
        expand_result,
        contract_result,
        norm_chain.result()[0],
    )


def solution(mesh):
    split_rows = P(("row", "mem"), None)
    split_ids = P(("row", "mem"))
    in_specs = (split_rows, split_rows, split_ids, split_ids) + (P(),) * 11 + (split_rows,)
    out_specs = (split_rows,) * 3 + (P("row", "mem"),) * 10 + (P("mem", "row"),)
    return jax.shard_map(
        partial(shards, mesh.shape["row"]),
        mesh=mesh,
        in_specs=in_specs,
        out_specs=out_specs,
        check_vma=False,
    )
```

```python
from functools import partial

import jax
import jax.numpy as jnp
import numpy as np
from jax import lax
from jax.experimental import pallas as pl
from jax.experimental.pallas import tpu as pltpu
from jax.sharding import PartitionSpec as P

HEADS = 16
HEAD_DIM = 64
GROUP = 256
PAIR = 128

ALPHA = 300.0**0.25
SCALE = 0.125
NEG = -1e30
EPS = 1e-05

BF = jnp.bfloat16
F32 = jnp.float32
VMEM_LIMIT = 56 * 2**20


def mul(left, right, left_axis, right_axis):
    return lax.dot_general(
        left, right, (((left_axis,), (right_axis,)), ((), ())), preferred_element_type=F32
    )


def mul_nn(left, right):
    return mul(left, right, 1, 0)


def mul_nt(left, right):
    return mul(left, right, 1, 1)


def mul_tn(left, right):
    return mul(left, right, 0, 0)


def kernel_call(body, grid, in_specs, out_specs, out_shape, scratch, moved, scalars=0):
    return pl.pallas_call(
        body,
        grid_spec=pltpu.PrefetchScalarGridSpec(
            num_scalar_prefetch=scalars,
            grid=grid,
            in_specs=in_specs,
            out_specs=out_specs,
            scratch_shapes=scratch,
        ),
        out_shape=out_shape,
        compiler_params=pltpu.CompilerParams(vmem_limit_bytes=VMEM_LIMIT),
        cost_estimate=pl.CostEstimate(
            flops=1, bytes_accessed=int(moved * 2**20), transcendentals=0
        ),
    )


def whole(shape):
    return pl.BlockSpec(shape, lambda *_: (0,) * len(shape))


def shape_of(shape, dtype):
    return jax.ShapeDtypeStruct(shape, dtype)


def gather_rows(pairs):
    for part, everything in pairs:
        size = part.shape[0]
        at = pl.multiple_of(pl.program_id(0) * size, size)
        everything[pl.ds(at, size), :] = part[...]


def by_rows(rows, step, body):
    def one(at, carry):
        body(pl.ds(pl.multiple_of(at * step, step), step))
        return carry

    lax.fori_loop(0, rows // step, one, 0)


def normalize(value):
    middle = jnp.mean(value, -1, keepdims=True)
    centred = value - middle
    spread = jnp.mean(centred * centred, -1, keepdims=True)
    inverse = lax.rsqrt(spread + EPS)
    return centred * inverse, inverse


def normalize_back(cotangent, normal, inverse, gain_row):
    scaled = cotangent * gain_row
    first = jnp.mean(scaled, -1, keepdims=True)
    second = jnp.mean(scaled * normal, -1, keepdims=True)
    grad = (scaled - first - normal * second) * inverse
    gain_term = jnp.sum(cotangent * normal, 0, keepdims=True)
    bias_term = jnp.sum(cotangent, 0, keepdims=True)
    return grad, gain_term, bias_term


def head_masks():
    lane = lax.broadcasted_iota(jnp.int32, (1, PAIR), 1)
    first = (lane < HEAD_DIM).astype(F32)
    return (first.astype(BF), (1.0 - first).astype(BF))


def head_masks_scaled():
    lane = lax.broadcasted_iota(jnp.int32, (1, PAIR), 1)
    first = (lane < HEAD_DIM).astype(F32)
    return ((first * SCALE).astype(BF), ((1.0 - first) * SCALE).astype(BF))


def fill_bias(bias, row_seg, key_seg, causal):
    rows, keys = bias.shape
    ids = jnp.broadcast_to(row_seg[...].astype(F32), (PAIR, rows)).T
    bias[:, :PAIR] = ids
    key_ids = key_seg[...].astype(F32)

    def block(at):
        allowed = bias[at, 0:1] == key_ids
        if causal:
            row_pos = at.start + lax.broadcasted_iota(jnp.int32, (64, keys), 0)
            key_pos = lax.broadcasted_iota(jnp.int32, (64, keys), 1)
            allowed = allowed & (row_pos >= key_pos)
        bias[at, :] = jnp.where(allowed, 0.0, NEG)

    by_rows(rows, 64, block)


def row_parts(rows, keys, causal):
    half = rows // 2
    if causal:
        return ((0, half, half), (half, half, rows))
    return ((0, half, keys), (half, half, keys))


def forward_body(causal, *refs):
    if causal:
        (row_seg, key_seg, source, w_query, w_key, w_value, w_out, norms) = refs[:8]
        rest = refs[8:]
        key_source = (source,)
    else:
        (row_seg, key_seg, source, normal_in, own, other) = refs[:6]
        (w_query, w_key, w_value, w_out, norms) = refs[6:11]
        rest = refs[11:]
        key_source = (own, other)
    (q_out, k_out, v_out, o_out, lse_out, normal_out, inverse_out, low_out) = rest[:8]
    bias, total = rest[8:10]
    step = pl.program_id(0)
    rows = source.shape[0]
    keys = bias.shape[1]

    @pl.when(step == 0)
    def _():
        fill_bias(bias, row_seg, key_seg, causal)
        total[...] = jnp.zeros_like(total)

    q_out[...] = mul_nn(source[...], w_query[...]).astype(BF)
    at = 0
    for part in key_source:
        size = part.shape[0]
        k_out[at : at + size, :] = mul_nn(part[...], w_key[...]).astype(BF)
        v_out[at : at + size, :] = mul_nn(part[...], w_value[...]).astype(BF)
        at += size
    scaled = head_masks_scaled()
    lane = lax.broadcasted_iota(jnp.int32, (1, PAIR), 1)
    for begin, size, seen in row_parts(rows, keys, causal):
        rows_at = slice(begin, begin + size)
        scores = []
        for pair in range(GROUP // PAIR):
            lanes = slice(pair * PAIR, (pair + 1) * PAIR)
            query = q_out[rows_at, lanes]
            key = k_out[:seen, lanes]
            for head in range(2):
                scores.append(mul_nt(query * scaled[head], key) + bias[rows_at, :seen])
        lse_block = jnp.zeros((size, PAIR), F32)
        for pair in range(GROUP // PAIR):
            lanes = slice(pair * PAIR, (pair + 1) * PAIR)
            value = v_out[:seen, lanes]
            outs = []
            for head in range(2):
                score = scores[pair * 2 + head]
                top = jnp.max(score, -1, keepdims=True)
                weights = jnp.exp(score - top)
                weight_sum = jnp.sum(weights, -1, keepdims=True)
                outs.append(mul_nn(weights.astype(BF), value) * (1.0 / weight_sum))
                lse_block = jnp.where(
                    lane == pair * 2 + head, top + jnp.log(weight_sum), lse_block
                )
            o_out[rows_at, lanes] = jnp.where(lane < HEAD_DIM, outs[0], outs[1]).astype(BF)
        lse_out[rows_at, :] = lse_block
    total[...] += mul_nn(o_out[...], w_out[...])

    @pl.when(step == pl.num_programs(0) - 1)
    def _():
        def block(at):
            if causal:
                base = source[at, :].astype(F32)
                gain, shift = norms[0:1, :], norms[1:2, :]
            else:
                base = normal_in[at, :] * norms[0:1, :] + norms[1:2, :]
                gain, shift = norms[2:3, :], norms[3:4, :]
            normal, inverse = normalize(ALPHA * base + total[at, :])
            normal_out[at, :] = normal
            inverse_out[at, :] = inverse
            low_out[at, :] = (normal * gain + shift).astype(BF)

        by_rows(rows, 128, block)


def attention_forward(causal, row_seg, key_seg, source, extra, weights, norms):
    rows, width = source.shape
    keys = key_seg.shape[0]
    steps = width // GROUP
    columns = pl.BlockSpec((width, GROUP), lambda g: (0, g))
    in_specs = [whole((1, rows)), whole((1, keys)), whole((rows, width))]
    operands = [row_seg.reshape(1, rows), key_seg.reshape(1, keys), source]
    for item in extra:
        in_specs.append(whole(item.shape))
        operands.append(item)
    in_specs += [columns] * 3 + [pl.BlockSpec((GROUP, width), lambda g: (g, 0))]
    in_specs.append(whole(norms.shape))
    row_block = pl.BlockSpec((rows, GROUP), lambda g: (0, g))
    key_block = pl.BlockSpec((keys, GROUP), lambda g: (0, g))
    out_specs = [
        row_block,
        key_block,
        key_block,
        row_block,
        pl.BlockSpec((rows, PAIR), lambda g: (0, g)),
        whole((rows, width)),
        whole((rows, 1)),
        whole((rows, width)),
    ]
    out_shape = [
        shape_of((rows, width), BF),
        shape_of((keys, width), BF),
        shape_of((keys, width), BF),
        shape_of((rows, width), BF),
        shape_of((rows, PAIR * steps), F32),
        shape_of((rows, width), F32),
        shape_of((rows, 1), F32),
        shape_of((rows, width), BF),
    ]
    scratch = [pltpu.VMEM((rows, keys), F32), pltpu.VMEM((rows, width), F32)]
    call = kernel_call(
        partial(forward_body, causal), (steps,), in_specs, out_specs, out_shape, scratch, 30
    )
    return call(*operands, *weights, norms)


def gelu_parts(value):
    share = 0.5 + 0.5 * lax.erf(value * 0.5**0.5)
    bell = jnp.exp(value * value * -0.5) * (0.5 / np.pi) ** 0.5
    return value * share, share + value * bell


def expand_body(
    core, low, normal_part, w_expand, w_contract, norms, cotangent_part,
    active_out, slope_out, layer_out, grad_out, low_grad, send_grad, keep_grad, norm_out,
    total, normal_in, out_grad,
):
    step = pl.program_id(0)
    gather_rows(((normal_part, normal_in), (cotangent_part, out_grad)))
    rows, width = low.shape

    @pl.when(step == 0)
    def _():
        total[...] = jnp.zeros_like(total)

    size = rows // 2
    spans = [slice(part * size, (part + 1) * size) for part in range(2)]
    values = [mul_nn(low[at, :], w_expand[...]) for at in spans]
    for at, value in zip(spans, values):
        active, slope = gelu_parts(value)
        active = active.astype(BF)
        active_out[at, :] = active
        slope_out[at, :] = slope.astype(BF)
        total[at, :] += mul_nn(active, w_contract[...])

    @pl.when(step == pl.num_programs(0) - 1)
    def _():
        norm_out[...] = jnp.zeros_like(norm_out)
        half = width // 2
        is_low = core[0] == 0

        def block(at):
            base = normal_in[at, :] * norms[2:3, :] + norms[3:4, :]
            normal, inverse = normalize(ALPHA * base + total[at, :])
            layer_out[at, :] = (normal * norms[4:5, :] + norms[5:6, :]).astype(BF)
            grad, gain_term, bias_term = normalize_back(
                out_grad[at, :].astype(F32), normal, inverse, norms[4:5, :]
            )
            norm_out[0:1, :] += gain_term
            norm_out[1:2, :] += bias_term
            grad_out[at, :] = grad
            low_grad[at, :] = grad.astype(BF)
            left, right = grad[:, :half], grad[:, half:]
            keep_grad[at, :] = jnp.where(is_low, left, right).astype(BF)
            send_grad[at, :] = jnp.where(is_low, right, left).astype(BF)

        by_rows(rows, 128, block)


def feed_forward(core, low, normal, w_expand, w_contract, norms, out_grad):
    rows, width = low.shape
    wide = w_expand.shape[1]
    chunk = 512
    steps = wide // chunk
    part = pl.BlockSpec((rows // steps, width), lambda c, _: (c, 0))
    in_specs = [
        whole((rows, width)),
        part,
        pl.BlockSpec((width, chunk), lambda c, _: (0, c)),
        pl.BlockSpec((chunk, width), lambda c, _: (c, 0)),
        whole(norms.shape),
        part,
    ]
    wide_block = pl.BlockSpec((rows, chunk), lambda c, _: (0, c))
    out_specs = [wide_block, wide_block] + [whole((rows, width))] * 3
    out_specs += [whole((rows, width // 2))] * 2 + [whole((2, width))]
    out_shape = [
        shape_of((rows, wide), BF),
        shape_of((rows, wide), BF),
        shape_of((rows, width), BF),
        shape_of((rows, width), F32),
        shape_of((rows, width), BF),
        shape_of((rows, width // 2), BF),
        shape_of((rows, width // 2), BF),
        shape_of((2, width), F32),
    ]
    call = kernel_call(
        expand_body,
        (steps,),
        in_specs,
        out_specs,
        out_shape,
        [pltpu.VMEM((rows, width), F32)] * 2 + [pltpu.VMEM((rows, width), BF)],
        34,
        scalars=1,
    )
    return call(core, low, normal, w_expand, w_contract, norms, out_grad)


def send_first(step, steps, core):
    half = steps // 2
    later = step // half
    return jnp.where(later == 0, 1 - core[0], core[0]) * half + step % half


def contract_back_body(last, core, *refs):
    low_grad, w_contract, slope, w_expand = refs[:4]
    if last:
        (total_in, grad_part, normal_part, inverse_in, norms) = refs[4:9]
        (wide_out, grad_out, low_out, send_low, keep_low, norm_out) = refs[9:15]
        (total, grad_in, normal_in) = refs[15:]
        gather_rows(((grad_part, grad_in), (normal_part, normal_in)))
    else:
        wide_out, total = refs[4:]
    step = pl.program_id(0)
    rows, width = low_grad.shape

    @pl.when(step == 0)
    def _():
        total[...] = total_in[...] if last else jnp.zeros_like(total)

    size = rows // 2
    spans = [slice(part * size, (part + 1) * size) for part in range(2)]
    values = [mul_nt(low_grad[at, :], w_contract[...]) for at in spans]
    for at, value in zip(spans, values):
        wide_grad = (value * slope[at, :].astype(F32)).astype(BF)
        wide_out[at, :] = wide_grad
        total[at, :] += mul_nt(wide_grad, w_expand[...])

    if not last:
        return

    @pl.when(step == pl.num_programs(0) - 1)
    def _():
        norm_out[...] = jnp.zeros_like(norm_out)
        half = width // 2
        is_low = core[0] == 0

        def block(at):
            grad, gain_term, bias_term = normalize_back(
                ALPHA * grad_in[at, :] + total[at, :],
                normal_in[at, :],
                inverse_in[at, :],
                norms[2:3, :],
            )
            norm_out[0:1, :] += gain_term
            norm_out[1:2, :] += bias_term
            grad_out[at, :] = grad
            low_out[at, :] = grad.astype(BF)
            left, right = grad[:, :half], grad[:, half:]
            keep_low[at, :] = jnp.where(is_low, left, right).astype(BF)
            send_low[at, :] = jnp.where(is_low, right, left).astype(BF)

        by_rows(rows, 128, block)


def feed_backward(last, core, low_grad, w_contract, slope, w_expand, *rest):
    rows, width = low_grad.shape
    wide = w_expand.shape[1]
    chunk = 512
    steps = wide // chunk // 2

    def at(s, core):
        return (core[0] if last else 1 - core[0]) * steps + s

    in_specs = [
        whole((rows, width)),
        pl.BlockSpec((chunk, width), lambda s, core: (at(s, core), 0)),
        pl.BlockSpec((rows, chunk), lambda s, core: (0, at(s, core))),
        pl.BlockSpec((width, chunk), lambda s, core: (0, at(s, core))),
    ] + [whole(item.shape) for item in rest]
    if last:
        in_specs[5:7] = [pl.BlockSpec((rows // steps, width), lambda s, _: (s, 0))] * 2
    out_specs = [pl.BlockSpec((rows, chunk), lambda s, _: (0, s)), whole((rows, width))]
    out_shape = [shape_of((rows, wide // 2), BF), shape_of((rows, width), F32)]
    scratch = []
    if last:
        out_specs += [whole((rows, width))] + [whole((rows, width // 2))] * 2 + [whole((2, width))]
        out_shape += [
            shape_of((rows, width), BF),
            shape_of((rows, width // 2), BF),
            shape_of((rows, width // 2), BF),
            shape_of((2, width), F32),
        ]
        scratch = [pltpu.VMEM((rows, width), F32)] * 3
    call = kernel_call(
        partial(contract_back_body, last),
        (steps,),
        in_specs,
        out_specs,
        out_shape,
        scratch,
        18,
        scalars=1,
    )
    return call(core, low_grad, w_contract, slope, w_expand, *rest)


def add_rows(parts):
    first, last = parts
    rows = first.shape[0]
    if rows == last.shape[0]:
        return first + last
    return jnp.concatenate([first + last[:rows], last[rows:]])


def backward_body(causal, core, *refs):
    (row_seg, key_seg, low_grad, w_out, query_in, key_in, value_in, o_in, lse_in) = refs[:9]
    if causal:
        (send_out, keep_out, bias) = refs[9:]
    else:
        (w_query, grad_part, normal_part, inverse_in, norms) = refs[9:14]
        (send_out, keep_out, grad_out, low_out, send_low, keep_low, norm_out) = refs[14:21]
        (bias, total, grad_in, normal_in) = refs[21:]
        gather_rows(((grad_part, grad_in), (normal_part, normal_in)))
    step = pl.program_id(0)
    steps = pl.num_programs(0)
    rows, width = low_grad.shape
    keys = bias.shape[1]

    @pl.when(step == 0)
    def _():
        fill_bias(bias, row_seg, key_seg, causal)
        if not causal:
            total[...] = jnp.zeros_like(total)

    o_grad = mul_nt(low_grad[...], w_out[...]).astype(BF)
    plain = head_masks()
    scaled = head_masks_scaled()
    first_lanes = lax.broadcasted_iota(jnp.int32, (1, PAIR), 1) < HEAD_DIM
    query_grads, key_grads, value_grads = [], [], []
    for pair in range(GROUP // PAIR):
        lanes = slice(pair * PAIR, (pair + 1) * PAIR)
        started = []
        for begin, size, seen in row_parts(rows, keys, causal):
            rows_at = slice(begin, begin + size)
            query = query_in[rows_at, lanes]
            grad = o_grad[rows_at, lanes]
            key = key_in[:seen, lanes]
            value = value_in[:seen, lanes]
            product = grad.astype(F32) * o_in[rows_at, lanes].astype(F32)
            head_queries = [query * scaled[head] for head in range(2)]
            head_grads = [grad * plain[head] for head in range(2)]
            scores = [mul_nt(item, key) for item in head_queries]
            prob_grads = [mul_nt(item, value) for item in head_grads]
            started.append(
                (rows_at, seen, key, product, head_queries, head_grads, scores, prob_grads)
            )
        query_parts, key_parts, value_parts = [], [], []
        for rows_at, seen, key, product, head_queries, head_grads, scores, prob_grads in started:
            probs, score_grads = [], []
            for head in range(2):
                mine = first_lanes if head == 0 else jnp.logical_not(first_lanes)
                delta = jnp.sum(jnp.where(mine, product, 0.0), -1, keepdims=True)
                lse = lse_in[rows_at, pair * 2 + head : pair * 2 + head + 1]
                prob = jnp.exp(scores[head] + bias[rows_at, :seen] - lse)
                score_grads.append((prob * (prob_grads[head] - delta)).astype(BF))
                probs.append(prob.astype(BF))
            value_parts.append(mul_tn(jnp.concatenate(probs), jnp.concatenate(head_grads)))
            stacked = jnp.concatenate(score_grads)
            key_parts.append(mul_tn(stacked, jnp.concatenate(head_queries)))
            wide = jnp.concatenate(score_grads, axis=1)
            head_keys = jnp.concatenate([key * scaled[0], key * scaled[1]])
            query_parts.append(mul_nn(wide, head_keys))
        query_grads.append(jnp.concatenate(query_parts).astype(BF))
        key_grads.append(add_rows(key_parts).astype(BF))
        value_grads.append(add_rows(value_parts).astype(BF))
    query_grad = jnp.concatenate(query_grads, axis=1)
    key_grad = jnp.concatenate(key_grads, axis=1)
    value_grad = jnp.concatenate(value_grads, axis=1)

    @pl.when(step < steps // 2)
    def _():
        send_out[0], send_out[1], send_out[2] = query_grad, key_grad, value_grad

    @pl.when(step >= steps // 2)
    def _():
        keep_out[0], keep_out[1], keep_out[2] = query_grad, key_grad, value_grad

    if causal:
        return
    total[...] += mul_nt(query_grad, w_query[...])

    @pl.when(step == steps - 1)
    def _():
        norm_out[...] = jnp.zeros_like(norm_out)
        half = width // 2
        is_low = core[0] == 0

        def block(at):
            grad, gain_term, bias_term = normalize_back(
                ALPHA * grad_in[at, :] + total[at, :],
                normal_in[at, :],
                inverse_in[at, :],
                norms[0:1, :],
            )
            norm_out[0:1, :] += gain_term
            norm_out[1:2, :] += bias_term
            grad_out[at, :] = grad
            low_out[at, :] = grad.astype(BF)
            left, right = grad[:, :half], grad[:, half:]
            keep_low[at, :] = jnp.where(is_low, left, right).astype(BF)
            send_low[at, :] = jnp.where(is_low, right, left).astype(BF)

        by_rows(rows, 128, block)


def project_back_body(items, core, send, keep, *refs):
    weights = refs[: len(items)]
    rest = refs[len(items) :]
    total = rest[-1]
    step = pl.program_id(0)
    steps = pl.num_programs(0)
    joined_weights = jnp.concatenate([weight[...] for weight in weights], axis=1)

    @pl.when(step == 0)
    def _():
        total[...] = jnp.zeros_like(total)

    for source, first in ((send, 0), (keep, steps // 2)):

        @pl.when((step >= first) & (step < first + steps // 2))
        def _():
            joined = jnp.concatenate([source[item] for item in items], axis=1)
            total[...] += mul_nt(joined, joined_weights)

    @pl.when(step == steps - 1)
    def _():
        if len(rest) == 3 and rest[0].dtype == F32:
            grad_in, out = rest[:2]

            def block(at):
                out[at, :] = (ALPHA * grad_in[at, :] + total[at, :]).astype(BF)

            by_rows(out.shape[0], 64, block)
        else:
            own, other = rest[:2]
            rows = own.shape[0]
            own[...] = total[:rows, :].astype(BF)
            other[...] = total[rows:, :].astype(BF)


def project_back(core, send, keep, items, weights, grad=None):
    count, rows, half = send.shape
    width = weights[0].shape[0]
    steps = 2 * half // GROUP
    in_specs = [
        pl.BlockSpec((count, rows, GROUP), lambda s, _: (0, 0, jnp.minimum(s, steps // 2 - 1))),
        pl.BlockSpec((count, rows, GROUP), lambda s, _: (0, 0, jnp.maximum(s - steps // 2, 0))),
    ]
    columns = pl.BlockSpec((width, GROUP), lambda s, core: (0, send_first(s, steps, core)))
    in_specs += [columns] * len(weights)
    extra = [] if grad is None else [grad]
    in_specs += [whole(item.shape) for item in extra]
    outs = [(rows, width)] if extra else [(rows // 2, width)] * 2
    call = kernel_call(
        partial(project_back_body, items),
        (steps,),
        in_specs,
        [whole(out) for out in outs],
        [shape_of(out, BF) for out in outs],
        [pltpu.VMEM((rows, width), F32)],
        0,
        scalars=1,
    )
    return call(core, send, keep, *weights, *extra)


def attention_backward(causal, core, row_seg, key_seg, low_grad, w_out, saved, extra):
    rows, width = low_grad.shape
    keys = key_seg.shape[0]
    steps = width // GROUP
    half = steps // 2

    def block(shape, spread):
        def index(s, core):
            group = send_first(s, steps, core)
            return (group, 0) if spread == 0 else (0, group)

        return pl.BlockSpec(shape, index)

    row_block = block((rows, GROUP), 1)
    key_block = block((keys, GROUP), 1)
    columns = block((width, GROUP), 1)
    in_specs = [
        whole((1, rows)),
        whole((1, keys)),
        whole((rows, width)),
        block((GROUP, width), 0),
        row_block,
        key_block,
        key_block,
        row_block,
        block((rows, PAIR), 1),
    ]
    if not causal:
        in_specs += [columns]
        in_specs += [pl.BlockSpec((rows // steps, width), lambda s, _: (s, 0))] * 2
    in_specs += [whole(item.shape) for item in extra[3:]]
    out_specs = [
        pl.BlockSpec((3, rows, GROUP), lambda s, _: (0, 0, jnp.minimum(s, half - 1))),
        pl.BlockSpec((3, rows, GROUP), lambda s, _: (0, 0, jnp.maximum(s - half, 0))),
    ]
    out_shape = [shape_of((3, rows, width // 2), BF)] * 2
    scratch = [pltpu.VMEM((rows, keys), F32)]
    if not causal:
        out_specs += [whole((rows, width))] * 2 + [whole((rows, width // 2))] * 2
        out_specs += [whole((2, width))]
        out_shape += [
            shape_of((rows, width), F32),
            shape_of((rows, width), BF),
            shape_of((rows, width // 2), BF),
            shape_of((rows, width // 2), BF),
            shape_of((2, width), F32),
        ]
        scratch += [pltpu.VMEM((rows, width), F32)] * 3
    call = kernel_call(
        partial(backward_body, causal),
        (steps,),
        in_specs,
        out_specs,
        out_shape,
        scratch,
        44,
        scalars=1,
    )
    return call(
        core,
        row_seg.reshape(1, rows),
        key_seg.reshape(1, keys),
        low_grad,
        w_out,
        *saved,
        *extra,
    )


def swap_mem(tensor):
    return lax.ppermute(tensor, "mem", [(0, 1), (1, 0)])


def tie(value, *after):
    return lax.optimization_barrier((value, after))[0]


def beside(outputs, arrays):
    return lax.optimization_barrier((outputs, arrays))


def during(outputs, *chains):
    outputs, terms = lax.optimization_barrier((outputs, [chain.terms for chain in chains]))
    for chain, items in zip(chains, terms):
        chain.terms = items
    return outputs


class Plan:
    def __init__(self, steps, row_count):
        self.steps = steps
        self.row_count = row_count
        sizes = [self.pieces(step) for step in steps]
        self.relative, self.fixed = [], []
        for k in range(row_count):
            mask = fixed = 0
            rest = row_count
            for step, size in zip(steps, sizes):
                rest //= size
                digit = k // rest % size
                if step == "group":
                    fixed = digit << 2
                elif step == "plane":
                    mask |= digit
                else:
                    mask |= digit << step
            self.relative.append(mask)
            self.fixed.append(fixed)
        self.groups = [list(range(low, row_count, 4)) for low in range(4)]

    def pieces(self, step):
        if step == "group":
            return self.row_count // 4
        return 4 if step == "plane" else 2

    def first_pieces(self):
        return 1 if self.steps[0] == "group" else self.pieces(self.steps[0])

    def block_at(self, chip, k):
        own = (chip & 3) if "group" in self.steps else chip
        return (own ^ self.relative[k]) | self.fixed[k]

    def place_of(self, chip, block):
        own = (chip & 3) if "group" in self.steps else chip
        apart = own ^ block
        place = 0
        for step in self.steps:
            size = self.pieces(step)
            if step == "group":
                digit = apart >> 2
            elif step == "plane":
                digit = apart & 3
            else:
                digit = (apart >> step) & 1
            place = place * size + digit
        return place

    def at_places(self, chip):
        own = (chip & 3) if "group" in self.steps else chip
        return (own ^ jnp.asarray(self.relative, jnp.int32)) | jnp.asarray(self.fixed, jnp.int32)

    def permute(self, tensor, mask):
        pairs = [(i, i ^ mask) for i in range(self.row_count)]
        return lax.ppermute(tensor, "row", pairs)

    def group_sum(self, tensor):
        return lax.psum_scatter(
            tensor, "row", scatter_dimension=0, tiled=True, axis_index_groups=self.groups
        )


def group_sum_joined(plan, tensors, lanes):
    count = plan.row_count // 4
    pieces, sizes = [], []
    for tensor in tensors:
        blocks = tensor.reshape(count, -1, tensor.shape[1])
        sizes.append(blocks.shape[1:])
        pieces += [blocks[:, :, at : at + lanes] for at in range(0, blocks.shape[2], lanes)]
    joined = jnp.concatenate(pieces, axis=1)
    return joined, sizes, plan.group_sum(joined)[0]


def parted(summed, sizes, lanes):
    outs, at = [], 0
    for rows, width in sizes:
        parts = []
        for _ in range(width // lanes):
            parts.append(summed[at : at + rows])
            at += rows
        outs.append(jnp.concatenate(parts, axis=1) if len(parts) > 1 else parts[0])
    return outs


class Chain:
    def __init__(self, plan, blocks):
        self.plan = plan
        self.left = list(plan.steps)
        self.launch(list(blocks))

    def launch(self, pieces):
        step = self.left.pop(0)
        if step == "group":
            self.sent = pieces
            self.terms = [self.plan.group_sum(pieces[0])]
            return
        self.sent = pieces[1:]
        masks = [1, 2, 3] if step == "plane" else [1 << step]
        got = [self.plan.permute(piece, mask) for piece, mask in zip(self.sent, masks)]
        self.terms = [pieces[0]] + got

    def hold(self, *after):
        got = self.terms[1:] if len(self.terms) > 1 else self.terms
        self.terms[-len(got) :] = tie(got, *after)

    def sum_rows(self, rows):
        total = self.terms[0][rows].astype(F32)
        for term in self.terms[1:]:
            total = total + term[rows].astype(F32)
        return total

    def merged(self):
        assert self.left.pop(0) == "group"
        return self.sum_rows(slice(None)).astype(BF)

    def advance(self):
        step = self.left[0]
        count = 1 if step == "group" else self.plan.pieces(step)
        rows = self.terms[0].shape[0] // count
        self.launch(
            [self.sum_rows(slice(k * rows, (k + 1) * rows)).astype(BF) for k in range(count)]
        )

    def result(self):
        assert not self.left
        return self.sum_rows(slice(None))


def joined_chain(chains, plan):
    half = chains[0].terms[0].shape[0] // 2
    blocks = []
    for rows in (slice(None, half), slice(half, None)):
        blocks.append(jnp.concatenate([chain.sum_rows(rows) for chain in chains], axis=1).astype(BF))
    return Chain(plan, blocks)


def swap_mem(tensor):
    return lax.ppermute(tensor, "mem", [(0, 1), (1, 0)])


def weight_grads_body(spans, sources_count, grads_count, step_table, count, chip, *refs):
    sources = refs[: 2 * sources_count]
    grads = refs[2 * sources_count : 2 * (sources_count + grads_count)]
    outs = refs[2 * (sources_count + grads_count) : -1]
    whole_grad = refs[-1]
    step = pl.program_id(0)
    _, block_rows, lanes = whole_grad.shape
    joined = max(16 // block_rows, 1)
    for entry in sorted(set(step_table)):
        steps = [at for at, which in enumerate(step_table) if which == entry]

        @pl.when((step >= steps[0]) & (step <= steps[-1]))
        def _():
            own, other = sources[2 * entry[0] : 2 * entry[0] + 2]
            own_grad, other_grad = grads[2 * entry[1] : 2 * entry[1] + 2]
            grad = mul_tn(own[...], own_grad[0]) + mul_tn(other[...], other_grad[0])
            whole_grad[...] = grad.reshape(count, block_rows, lanes)

    at_out = 0
    for begin, chunks, pieces, plan in spans:
        targets = outs[at_out : at_out + pieces]
        at_out += pieces

        @pl.when((step >= begin) & (step < begin + chunks))
        def _():
            size = count // pieces
            for part, out in enumerate(targets):
                for k in range(0, size, joined):
                    places = range(part * size + k, part * size + k + joined)
                    blocks = [whole_grad[plan.block_at(chip[0], place)] for place in places]
                    rows = slice(k * block_rows, (k + joined) * block_rows)
                    out[rows, :] = jnp.concatenate(blocks).astype(BF)


def weight_grads(chip, sources, grads, step_table, chunk, outs, travelling=()):
    tokens, width = sources[0][0].shape
    count = outs[0][1].row_count
    steps = len(step_table)
    in_specs = [whole((tokens, width))] * (2 * len(sources))
    flat = [item for pair in sources for item in pair]
    for number, pair in enumerate(grads):
        pair = [item if item.ndim == 3 else item[None] for item in pair]
        flat += pair
        across = pair[0].shape[2] // chunk
        mine = [at for at, which in enumerate(step_table) if which[1] == number]

        def index(i, _, first=mine[0], last=mine[-1], across=across):
            at = jnp.clip(i, first, last) - first
            return (at // across, 0, at % across)

        in_specs += [pl.BlockSpec((1, tokens, chunk), index)] * 2
    out_specs, out_shape, spans = [], [], []
    begin = 0
    for chunks, plan in outs:
        pieces = plan.first_pieces()

        def index(i, _, begin=begin, chunks=chunks):
            return (0, jnp.clip(i - begin, 0, chunks - 1))

        for _ in range(pieces):
            out_specs.append(pl.BlockSpec((width // pieces, chunk), index))
            out_shape.append(shape_of((width // pieces, chunk * chunks), BF))
        spans.append((begin, chunks, pieces, plan))
        begin += chunks
    call = kernel_call(
        partial(weight_grads_body, spans, len(sources), len(grads), step_table, count),
        (steps,),
        in_specs,
        out_specs,
        out_shape,
        [pltpu.VMEM((count, width // count, chunk), F32)],
        16,
        scalars=1,
    )
    results = during(call(chip.reshape(1), *flat), *travelling)
    chains, at = [], 0
    for _, _, pieces, plan in spans:
        chains.append(Chain(plan, results[at : at + pieces]))
        at += pieces
    return chains


def wide_grads_body(plans, chip, own, other, own_grad, other_grad, *outs):
    step = pl.program_id(0)
    chains = len(outs) // 2
    lanes = outs[0].shape[1]
    block_rows = outs[0].shape[0] * 2 // plans[0].row_count
    blocks = own.shape[1] // block_rows
    size = outs[0].shape[0] // block_rows
    grad = mul_tn(own[...], own_grad[...]) + mul_tn(other[...], other_grad[...])
    grad = grad.astype(BF)
    for block in range(blocks):
        for chain in range(chains):
            part = grad[block * block_rows : (block + 1) * block_rows]
            part = part[:, chain * lanes : (chain + 1) * lanes]
            place = plans[chain].place_of(chip[0], step * blocks + block)
            for half in range(2):

                @pl.when((place >= half * size) & (place < (half + 1) * size))
                def _():
                    row = pl.multiple_of((place - half * size) * block_rows, block_rows)
                    outs[2 * chain + half][pl.ds(row, block_rows), :] = part


def wide_grads(chip, own, other, own_grad, other_grad, plans):
    tokens, width = own.shape
    lanes = own_grad.shape[1]
    chunk = 512
    source = pl.BlockSpec((tokens, chunk), lambda i, _: (0, i))
    out = (width // 2, lanes // len(plans))
    call = kernel_call(
        partial(wide_grads_body, plans),
        (width // chunk,),
        [source] * 2 + [whole((tokens, lanes))] * 2,
        [whole(out)] * (2 * len(plans)),
        [shape_of(out, BF)] * (2 * len(plans)),
        [],
        20,
        scalars=1,
    )
    results = call(chip.reshape(1), own, other, own_grad, other_grad)
    return [Chain(plan, results[2 * at : 2 * at + 2]) for at, plan in enumerate(plans)]


def shards(
    row_count,
    inputs,
    memory,
    target_seg,
    memory_seg,
    self_query,
    self_key,
    self_value,
    self_out,
    cross_query,
    cross_key,
    cross_value,
    cross_out,
    expand_weight,
    contract_weight,
    norm_params,
    out_grad,
):
    core = lax.axis_index("mem").astype(jnp.int32).reshape(1)
    chip = lax.axis_index("row").astype(jnp.int32)
    upper = list(range(2, row_count.bit_length() - 1))
    plan_x = Plan([0, 1, "group"], row_count)
    plan_y = Plan([1, 0, "group"], row_count)
    group_first = Plan(["group", 0, 1], row_count)
    last_x = Plan([0, 1] + upper, row_count)
    last_y = Plan([1, 0] + upper, row_count)
    rest = Plan(upper, row_count)

    self_saved = attention_forward(
        True,
        target_seg,
        target_seg,
        inputs,
        (),
        (self_query, self_key, self_value, self_out),
        norm_params,
    )
    self_saved, (other_memory, other_seg) = beside(
        self_saved, (swap_mem(memory), swap_mem(memory_seg))
    )
    pair_seg = jnp.concatenate([memory_seg, other_seg])
    other_inputs = swap_mem(inputs)
    self_o, normal_one, inverse_one, low_one = self_saved[3], *self_saved[5:]
    cross_saved = attention_forward(
        False,
        target_seg,
        pair_seg,
        low_one,
        (normal_one, memory, other_memory),
        (cross_query, cross_key, cross_value, cross_out),
        norm_params,
    )
    cross_saved, (other_inputs, other_self_o, other_one) = beside(
        cross_saved, (other_inputs, swap_mem(self_o), swap_mem(low_one))
    )
    cross_o, normal_two, inverse_two, low_two = cross_saved[3], *cross_saved[5:]
    outputs = feed_forward(
        core, low_two, normal_two, expand_weight, contract_weight, norm_params, out_grad
    )
    outputs, (other_cross_o, other_two) = beside(outputs, (swap_mem(cross_o), swap_mem(low_two)))
    (active, slope, layer_out, grad_three, low_three, send_three, keep_three, norm_three) = outputs
    outputs = feed_backward(False, core, low_three, contract_weight, slope, expand_weight)
    (send_wide, part_two), (other_active, got_three) = beside(
        outputs, (swap_mem(active), swap_mem(send_three))
    )

    half = keep_three.shape[1]
    contract_x, contract_y = wide_grads(
        chip, active, other_active, keep_three, got_three, [plan_x, plan_y]
    )
    outputs = feed_backward(
        True,
        core,
        tie(low_three, contract_x.sent, contract_y.sent),
        contract_weight,
        slope,
        expand_weight,
        part_two,
        grad_three,
        normal_two,
        inverse_two,
        norm_params,
    )
    outputs, got_wide = beside(outputs, swap_mem(send_wide))
    (keep_wide, grad_two, low_grad_two, send_two, keep_two, norm_two) = outputs
    expand, expand_x = weight_grads(
        chip,
        [(low_two, other_two)],
        [(keep_wide, got_wide)],
        [(0, 0)] * 4,
        512,
        [(2, group_first), (2, plan_x)],
        (contract_x, contract_y),
    )
    contract_x.advance()
    contract_y.advance()
    got_two = swap_mem(send_two)

    outputs = attention_backward(
        False,
        core,
        target_seg,
        pair_seg,
        tie(low_grad_two, expand.sent, expand_x.sent, contract_x.sent, contract_y.sent),
        cross_out,
        (cross_saved[0], cross_saved[1], cross_saved[2], cross_o, cross_saved[4]),
        (cross_query, grad_two, normal_one, inverse_one, norm_params),
    )
    (send_c, keep_c, grad_one, low_grad_one, send_one, keep_one, norm_one) = during(
        outputs, contract_x, contract_y, expand_x
    )
    norm_grad = jnp.concatenate([norm_one, norm_two, norm_three])
    norm_grad = norm_grad.reshape(2, 3, norm_grad.shape[1])
    norm_half = norm_grad[core[0]] + swap_mem(norm_grad[1 - core[0]])
    got_c = swap_mem(send_c)
    got_one = swap_mem(send_one)
    contract_merged = [chain.merged() for chain in (contract_x, contract_y)]
    expand_x.advance()
    block_rows = inputs.shape[1] // row_count
    norm_blocks = norm_half.reshape(3, row_count, block_rows).transpose(1, 0, 2)
    norm_blocks = jnp.take(norm_blocks, last_y.at_places(chip), axis=0)
    norm_chain = Chain(last_y, norm_blocks.reshape((2, -1) + norm_blocks.shape[1:]).astype(BF))
    pair_memory = jnp.concatenate([memory, other_memory])
    turned_memory = jnp.concatenate([other_memory, memory])
    cross_x, cross_y = weight_grads(
        chip,
        [
            (tie(cross_o, contract_merged, expand_x.sent, norm_chain.sent), other_cross_o),
            (low_one, other_one),
            (pair_memory, turned_memory),
            (self_o, other_self_o),
        ],
        [(keep_two, got_two), (keep_c, got_c), (keep_one, got_one)],
        [(0, 0)] * 2 + [(1, 1)] * 2 + [(2, 1)] * 4 + [(3, 2)] * 2,
        256,
        [(5, last_x), (5, last_y)],
        (expand_x, expand, norm_chain),
    )
    merged = contract_merged + [expand_x.merged()]
    joined, forward_sizes, forward_sum = group_sum_joined(plan_x, merged, half // 2)
    expand.advance()
    norm_chain.advance()

    mem_own, mem_send = project_back(
        core, tie(send_c, cross_x.sent, cross_y.sent), keep_c, (1, 2), (cross_key, cross_value)
    )
    outputs = attention_backward(
        True,
        core,
        target_seg,
        target_seg,
        tie(low_grad_one, mem_own, expand.sent, joined, norm_chain.sent),
        self_out,
        (self_saved[0], self_saved[1], self_saved[2], self_o, self_saved[4]),
        (),
    )
    send_s, keep_s = during(outputs, cross_x, cross_y, expand, norm_chain)
    got_s = swap_mem(send_s)
    cross_x.advance()
    cross_y.advance()
    expand.advance()
    norm_chain.advance()
    self_chains = weight_grads(
        chip,
        [(tie(inputs, cross_x.sent, cross_y.sent, expand.sent, norm_chain.sent), other_inputs)],
        [(keep_s, got_s)],
        [(0, 0)] * 6,
        256,
        [(3, last_x), (3, last_y)],
        (cross_x, cross_y, expand),
    )
    started = [chain.sent for chain in self_chains]
    for chain in (cross_x, cross_y):
        chain.hold(started, forward_sum)
    cross_chain = joined_chain((cross_x, cross_y), rest)
    (input_grad,) = project_back(
        core,
        tie(send_s, cross_chain.sent),
        keep_s,
        (0, 1, 2),
        (self_query, self_key, self_value),
        grad_one,
    )
    for chain in self_chains + [cross_chain]:
        chain.hold(input_grad)
        chain.advance()
    self_chain = joined_chain(self_chains, rest)
    norm_chain.hold(self_chain.sent)
    norm_chain.advance()
    mem_send, forward_sum, expand.terms, cross_chain.terms = tie(
        (mem_send, forward_sum, expand.terms, cross_chain.terms), self_chain.sent
    )
    memory_grad = (mem_own.astype(F32) + swap_mem(mem_send).astype(F32)).astype(BF)
    forward_parts = [part.astype(F32) for part in parted(forward_sum, forward_sizes, half // 2)]
    contract_result = jnp.concatenate(forward_parts[:2], axis=1)
    expand_result = jnp.concatenate([expand.result(), forward_parts[2]], axis=1)
    self_chain.hold(contract_result, expand_result)
    for chain in (self_chain, cross_chain, norm_chain):
        while chain.left:
            chain.advance()
    self_sum, cross_sum = self_chain.result(), cross_chain.result()
    own_lanes = self_out.shape[1] // 2
    cross_parts = [cross_sum[:, at * own_lanes : (at + 1) * own_lanes] for at in range(5)]
    return (
        layer_out,
        input_grad,
        memory_grad,
        self_sum[:, :own_lanes],
        self_sum[:, own_lanes : 2 * own_lanes],
        self_sum[:, 2 * own_lanes :],
        cross_parts[4],
        cross_parts[1],
        cross_parts[2],
        cross_parts[3],
        cross_parts[0],
        expand_result,
        contract_result,
        norm_chain.result()[0],
    )


def solution(mesh):
    split_rows = P(("row", "mem"), None)
    split_ids = P(("row", "mem"))
    in_specs = (split_rows, split_rows, split_ids, split_ids) + (P(),) * 11 + (split_rows,)
    out_specs = (split_rows,) * 3 + (P("row", "mem"),) * 10 + (P("mem", "row"),)
    return jax.shard_map(
        partial(shards, mesh.shape["row"]),
        mesh=mesh,
        in_specs=in_specs,
        out_specs=out_specs,
        check_vma=False,
    )
```

```python
from functools import partial

import jax
import jax.numpy as jnp
import numpy as np
from jax import lax
from jax.experimental import pallas as pl
from jax.experimental.pallas import tpu as pltpu
from jax.sharding import PartitionSpec as P

HEADS = 16
HEAD_DIM = 64
GROUP = 256
PAIR = 128

ALPHA = 300.0**0.25
SCALE = 0.125
NEG = -1e30
EPS = 1e-05

BF = jnp.bfloat16
F32 = jnp.float32
VMEM_LIMIT = 56 * 2**20


def mul(left, right, left_axis, right_axis):
    return lax.dot_general(
        left, right, (((left_axis,), (right_axis,)), ((), ())), preferred_element_type=F32
    )


def mul_nn(left, right):
    return mul(left, right, 1, 0)


def mul_nt(left, right):
    return mul(left, right, 1, 1)


def mul_tn(left, right):
    return mul(left, right, 0, 0)


def kernel_call(body, grid, in_specs, out_specs, out_shape, scratch, moved, scalars=0, aliases=None):
    return pl.pallas_call(
        body,
        grid_spec=pltpu.PrefetchScalarGridSpec(
            num_scalar_prefetch=scalars,
            grid=grid,
            in_specs=in_specs,
            out_specs=out_specs,
            scratch_shapes=scratch,
        ),
        out_shape=out_shape,
        input_output_aliases=aliases or {},
        compiler_params=pltpu.CompilerParams(vmem_limit_bytes=VMEM_LIMIT),
        cost_estimate=pl.CostEstimate(
            flops=1, bytes_accessed=int(moved * 2**20), transcendentals=0
        ),
    )


def whole(shape):
    return pl.BlockSpec(shape, lambda *_: (0,) * len(shape))


def shape_of(shape, dtype):
    return jax.ShapeDtypeStruct(shape, dtype)


def gather_rows(pairs):
    for part, everything in pairs:
        size = part.shape[0]
        at = pl.multiple_of(pl.program_id(0) * size, size)
        everything[pl.ds(at, size), :] = part[...]


def by_rows(rows, step, body):
    def one(at, carry):
        body(pl.ds(pl.multiple_of(at * step, step), step))
        return carry

    lax.fori_loop(0, rows // step, one, 0)


def normalize(value):
    middle = jnp.mean(value, -1, keepdims=True)
    centred = value - middle
    spread = jnp.mean(centred * centred, -1, keepdims=True)
    inverse = lax.rsqrt(spread + EPS)
    return centred * inverse, inverse


def normalize_back(cotangent, normal, inverse, gain_row):
    scaled = cotangent * gain_row
    first = jnp.mean(scaled, -1, keepdims=True)
    second = jnp.mean(scaled * normal, -1, keepdims=True)
    grad = (scaled - first - normal * second) * inverse
    gain_term = jnp.sum(cotangent * normal, 0, keepdims=True)
    bias_term = jnp.sum(cotangent, 0, keepdims=True)
    return grad, gain_term, bias_term


def head_masks():
    lane = lax.broadcasted_iota(jnp.int32, (1, PAIR), 1)
    first = (lane < HEAD_DIM).astype(F32)
    return (first.astype(BF), (1.0 - first).astype(BF))


def head_masks_scaled():
    lane = lax.broadcasted_iota(jnp.int32, (1, PAIR), 1)
    first = (lane < HEAD_DIM).astype(F32)
    return ((first * SCALE).astype(BF), ((1.0 - first) * SCALE).astype(BF))


def fill_bias(bias, row_seg, key_seg, causal):
    rows, keys = bias.shape
    ids = jnp.broadcast_to(row_seg[...].astype(F32), (PAIR, rows)).T
    bias[:, :PAIR] = ids
    key_ids = key_seg[...].astype(F32)

    def block(at):
        allowed = bias[at, 0:1] == key_ids
        if causal:
            row_pos = at.start + lax.broadcasted_iota(jnp.int32, (64, keys), 0)
            key_pos = lax.broadcasted_iota(jnp.int32, (64, keys), 1)
            allowed = allowed & (row_pos >= key_pos)
        bias[at, :] = jnp.where(allowed, 0.0, NEG)

    by_rows(rows, 64, block)


def row_parts(rows, keys, causal):
    half = rows // 2
    if causal:
        return ((0, half, half), (half, half, rows))
    return ((0, half, keys), (half, half, keys))


def forward_body(causal, *refs):
    if causal:
        (row_seg, key_seg, source, w_query, w_key, w_value, w_out, norms) = refs[:8]
        rest = refs[8:]
        key_source = (source,)
    else:
        (row_seg, key_seg, source, normal_in, own, other) = refs[:6]
        (w_query, w_key, w_value, w_out, norms) = refs[6:11]
        rest = refs[11:]
        key_source = (own, other)
    (q_out, k_out, v_out, o_out, lse_out, normal_out, inverse_out, low_out) = rest[:8]
    bias, total = rest[8:10]
    step = pl.program_id(0)
    rows = source.shape[0]
    keys = bias.shape[1]

    @pl.when(step == 0)
    def _():
        fill_bias(bias, row_seg, key_seg, causal)
        total[...] = jnp.zeros_like(total)

    q_out[...] = mul_nn(source[...], w_query[...]).astype(BF)
    at = 0
    for part in key_source:
        size = part.shape[0]
        k_out[at : at + size, :] = mul_nn(part[...], w_key[...]).astype(BF)
        v_out[at : at + size, :] = mul_nn(part[...], w_value[...]).astype(BF)
        at += size
    scaled = head_masks_scaled()
    lane = lax.broadcasted_iota(jnp.int32, (1, PAIR), 1)
    for begin, size, seen in row_parts(rows, keys, causal):
        rows_at = slice(begin, begin + size)
        scores = []
        for pair in range(GROUP // PAIR):
            lanes = slice(pair * PAIR, (pair + 1) * PAIR)
            query = q_out[rows_at, lanes]
            key = k_out[:seen, lanes]
            for head in range(2):
                scores.append(mul_nt(query * scaled[head], key) + bias[rows_at, :seen])
        lse_block = jnp.zeros((size, PAIR), F32)
        for pair in range(GROUP // PAIR):
            lanes = slice(pair * PAIR, (pair + 1) * PAIR)
            value = v_out[:seen, lanes]
            outs = []
            for head in range(2):
                score = scores[pair * 2 + head]
                top = jnp.max(score, -1, keepdims=True)
                weights = jnp.exp(score - top)
                weight_sum = jnp.sum(weights, -1, keepdims=True)
                outs.append(mul_nn(weights.astype(BF), value) * (1.0 / weight_sum))
                lse_block = jnp.where(
                    lane == pair * 2 + head, top + jnp.log(weight_sum), lse_block
                )
            o_out[rows_at, lanes] = jnp.where(lane < HEAD_DIM, outs[0], outs[1]).astype(BF)
        lse_out[rows_at, :] = lse_block
    total[...] += mul_nn(o_out[...], w_out[...])

    @pl.when(step == pl.num_programs(0) - 1)
    def _():
        def block(at):
            if causal:
                base = source[at, :].astype(F32)
                gain, shift = norms[0:1, :], norms[1:2, :]
            else:
                base = normal_in[at, :] * norms[0:1, :] + norms[1:2, :]
                gain, shift = norms[2:3, :], norms[3:4, :]
            normal, inverse = normalize(ALPHA * base + total[at, :])
            normal_out[at, :] = normal
            inverse_out[at, :] = inverse
            low_out[at, :] = (normal * gain + shift).astype(BF)

        by_rows(rows, 128, block)


def attention_forward(causal, row_seg, key_seg, source, extra, weights, norms):
    rows, width = source.shape
    keys = key_seg.shape[0]
    steps = width // GROUP
    columns = pl.BlockSpec((width, GROUP), lambda g: (0, g))
    in_specs = [whole((1, rows)), whole((1, keys)), whole((rows, width))]
    operands = [row_seg.reshape(1, rows), key_seg.reshape(1, keys), source]
    for item in extra:
        in_specs.append(whole(item.shape))
        operands.append(item)
    in_specs += [columns] * 3 + [pl.BlockSpec((GROUP, width), lambda g: (g, 0))]
    in_specs.append(whole(norms.shape))
    row_block = pl.BlockSpec((rows, GROUP), lambda g: (0, g))
    key_block = pl.BlockSpec((keys, GROUP), lambda g: (0, g))
    out_specs = [
        row_block,
        key_block,
        key_block,
        row_block,
        pl.BlockSpec((rows, PAIR), lambda g: (0, g)),
        whole((rows, width)),
        whole((rows, 1)),
        whole((rows, width)),
    ]
    out_shape = [
        shape_of((rows, width), BF),
        shape_of((keys, width), BF),
        shape_of((keys, width), BF),
        shape_of((rows, width), BF),
        shape_of((rows, PAIR * steps), F32),
        shape_of((rows, width), F32),
        shape_of((rows, 1), F32),
        shape_of((rows, width), BF),
    ]
    scratch = [pltpu.VMEM((rows, keys), F32), pltpu.VMEM((rows, width), F32)]
    call = kernel_call(
        partial(forward_body, causal), (steps,), in_specs, out_specs, out_shape, scratch, 30
    )
    return call(*operands, *weights, norms)


def gelu_parts(value):
    share = 0.5 + 0.5 * lax.erf(value * 0.5**0.5)
    bell = jnp.exp(value * value * -0.5) * (0.5 / np.pi) ** 0.5
    return value * share, share + value * bell


def expand_body(
    core, low, normal_part, w_expand, w_contract, norms, cotangent_part,
    active_out, slope_out, layer_out, grad_out, low_grad, send_grad, keep_grad, norm_out,
    total, normal_in, out_grad,
):
    step = pl.program_id(0)
    gather_rows(((normal_part, normal_in), (cotangent_part, out_grad)))
    rows, width = low.shape

    @pl.when(step == 0)
    def _():
        total[...] = jnp.zeros_like(total)

    size = rows // 2
    spans = [slice(part * size, (part + 1) * size) for part in range(2)]
    values = [mul_nn(low[at, :], w_expand[...]) for at in spans]
    for at, value in zip(spans, values):
        active, slope = gelu_parts(value)
        active = active.astype(BF)
        active_out[at, :] = active
        slope_out[at, :] = slope.astype(BF)
        total[at, :] += mul_nn(active, w_contract[...])

    @pl.when(step == pl.num_programs(0) - 1)
    def _():
        norm_out[...] = jnp.zeros_like(norm_out)
        half = width // 2
        is_low = core[0] == 0

        def block(at):
            base = normal_in[at, :] * norms[2:3, :] + norms[3:4, :]
            normal, inverse = normalize(ALPHA * base + total[at, :])
            layer_out[at, :] = (normal * norms[4:5, :] + norms[5:6, :]).astype(BF)
            grad, gain_term, bias_term = normalize_back(
                out_grad[at, :].astype(F32), normal, inverse, norms[4:5, :]
            )
            norm_out[0:1, :] += gain_term
            norm_out[1:2, :] += bias_term
            grad_out[at, :] = grad
            low_grad[at, :] = grad.astype(BF)
            left, right = grad[:, :half], grad[:, half:]
            keep_grad[at, :] = jnp.where(is_low, left, right).astype(BF)
            send_grad[at, :] = jnp.where(is_low, right, left).astype(BF)

        by_rows(rows, 128, block)


def feed_forward(core, low, normal, w_expand, w_contract, norms, out_grad):
    rows, width = low.shape
    wide = w_expand.shape[1]
    chunk = 512
    steps = wide // chunk
    part = pl.BlockSpec((rows // steps, width), lambda c, _: (c, 0))
    in_specs = [
        whole((rows, width)),
        part,
        pl.BlockSpec((width, chunk), lambda c, _: (0, c)),
        pl.BlockSpec((chunk, width), lambda c, _: (c, 0)),
        whole(norms.shape),
        part,
    ]
    wide_block = pl.BlockSpec((rows, chunk), lambda c, _: (0, c))
    out_specs = [wide_block, wide_block] + [whole((rows, width))] * 3
    out_specs += [whole((rows, width // 2))] * 2 + [whole((2, width))]
    out_shape = [
        shape_of((rows, wide), BF),
        shape_of((rows, wide), BF),
        shape_of((rows, width), BF),
        shape_of((rows, width), F32),
        shape_of((rows, width), BF),
        shape_of((rows, width // 2), BF),
        shape_of((rows, width // 2), BF),
        shape_of((2, width), F32),
    ]
    call = kernel_call(
        expand_body,
        (steps,),
        in_specs,
        out_specs,
        out_shape,
        [pltpu.VMEM((rows, width), F32)] * 2 + [pltpu.VMEM((rows, width), BF)],
        34,
        scalars=1,
    )
    return call(core, low, normal, w_expand, w_contract, norms, out_grad)


def send_first(step, steps, core):
    half = steps // 2
    later = step // half
    return jnp.where(later == 0, 1 - core[0], core[0]) * half + step % half


def contract_back_body(last, core, *refs):
    low_grad, w_contract, slope, w_expand = refs[:4]
    if last:
        (total_in, grad_part, normal_part, inverse_in, norms) = refs[4:9]
        (wide_out, grad_out, low_out, send_low, keep_low, norm_out) = refs[9:15]
        (total, grad_in, normal_in) = refs[15:]
        gather_rows(((grad_part, grad_in), (normal_part, normal_in)))
    else:
        wide_out, total = refs[4:]
    step = pl.program_id(0)
    rows, width = low_grad.shape

    @pl.when(step == 0)
    def _():
        total[...] = total_in[...] if last else jnp.zeros_like(total)

    size = rows // 2
    spans = [slice(part * size, (part + 1) * size) for part in range(2)]
    values = [mul_nt(low_grad[at, :], w_contract[...]) for at in spans]
    for at, value in zip(spans, values):
        wide_grad = (value * slope[at, :].astype(F32)).astype(BF)
        wide_out[at, :] = wide_grad
        total[at, :] += mul_nt(wide_grad, w_expand[...])

    if not last:
        return

    @pl.when(step == pl.num_programs(0) - 1)
    def _():
        norm_out[...] = jnp.zeros_like(norm_out)
        half = width // 2
        is_low = core[0] == 0

        def block(at):
            grad, gain_term, bias_term = normalize_back(
                ALPHA * grad_in[at, :] + total[at, :],
                normal_in[at, :],
                inverse_in[at, :],
                norms[2:3, :],
            )
            norm_out[0:1, :] += gain_term
            norm_out[1:2, :] += bias_term
            grad_out[at, :] = grad
            low_out[at, :] = grad.astype(BF)
            left, right = grad[:, :half], grad[:, half:]
            keep_low[at, :] = jnp.where(is_low, left, right).astype(BF)
            send_low[at, :] = jnp.where(is_low, right, left).astype(BF)

        by_rows(rows, 128, block)


def feed_backward(last, core, low_grad, w_contract, slope, w_expand, *rest):
    rows, width = low_grad.shape
    wide = w_expand.shape[1]
    chunk = 512
    steps = wide // chunk // 2

    def at(s, core):
        return (core[0] if last else 1 - core[0]) * steps + s

    in_specs = [
        whole((rows, width)),
        pl.BlockSpec((chunk, width), lambda s, core: (at(s, core), 0)),
        pl.BlockSpec((rows, chunk), lambda s, core: (0, at(s, core))),
        pl.BlockSpec((width, chunk), lambda s, core: (0, at(s, core))),
    ] + [whole(item.shape) for item in rest]
    if last:
        in_specs[5:7] = [pl.BlockSpec((rows // steps, width), lambda s, _: (s, 0))] * 2
    out_specs = [pl.BlockSpec((rows, chunk), lambda s, _: (0, s)), whole((rows, width))]
    out_shape = [shape_of((rows, wide // 2), BF), shape_of((rows, width), F32)]
    scratch = []
    if last:
        out_specs += [whole((rows, width))] + [whole((rows, width // 2))] * 2 + [whole((2, width))]
        out_shape += [
            shape_of((rows, width), BF),
            shape_of((rows, width // 2), BF),
            shape_of((rows, width // 2), BF),
            shape_of((2, width), F32),
        ]
        scratch = [pltpu.VMEM((rows, width), F32)] * 3
    call = kernel_call(
        partial(contract_back_body, last),
        (steps,),
        in_specs,
        out_specs,
        out_shape,
        scratch,
        18,
        scalars=1,
        aliases={5: 1} if last else None,
    )
    return call(core, low_grad, w_contract, slope, w_expand, *rest)


def add_rows(parts):
    first, last = parts
    rows = first.shape[0]
    if rows == last.shape[0]:
        return first + last
    return jnp.concatenate([first + last[:rows], last[rows:]])


def backward_body(causal, core, *refs):
    (row_seg, key_seg, low_grad, w_out, query_in, key_in, value_in, o_in, lse_in) = refs[:9]
    if causal:
        (send_out, keep_out, bias) = refs[9:]
    else:
        (w_query, grad_part, normal_part, inverse_in, norms) = refs[9:14]
        (send_out, keep_out, grad_out, low_out, send_low, keep_low, norm_out) = refs[14:21]
        (bias, total, grad_in, normal_in) = refs[21:]
        gather_rows(((grad_part, grad_in), (normal_part, normal_in)))
    step = pl.program_id(0)
    steps = pl.num_programs(0)
    rows, width = low_grad.shape
    keys = bias.shape[1]

    @pl.when(step == 0)
    def _():
        fill_bias(bias, row_seg, key_seg, causal)
        if not causal:
            total[...] = jnp.zeros_like(total)

    o_grad = mul_nt(low_grad[...], w_out[...]).astype(BF)
    plain = head_masks()
    scaled = head_masks_scaled()
    first_lanes = lax.broadcasted_iota(jnp.int32, (1, PAIR), 1) < HEAD_DIM
    query_grads, key_grads, value_grads = [], [], []
    for pair in range(GROUP // PAIR):
        lanes = slice(pair * PAIR, (pair + 1) * PAIR)
        started = []
        for begin, size, seen in row_parts(rows, keys, causal):
            rows_at = slice(begin, begin + size)
            query = query_in[rows_at, lanes]
            grad = o_grad[rows_at, lanes]
            key = key_in[:seen, lanes]
            value = value_in[:seen, lanes]
            product = grad.astype(F32) * o_in[rows_at, lanes].astype(F32)
            head_queries = [query * scaled[head] for head in range(2)]
            head_grads = [grad * plain[head] for head in range(2)]
            scores = [mul_nt(item, key) for item in head_queries]
            prob_grads = [mul_nt(item, value) for item in head_grads]
            started.append(
                (rows_at, seen, key, product, head_queries, head_grads, scores, prob_grads)
            )
        query_parts, key_parts, value_parts = [], [], []
        for rows_at, seen, key, product, head_queries, head_grads, scores, prob_grads in started:
            probs, score_grads = [], []
            for head in range(2):
                mine = first_lanes if head == 0 else jnp.logical_not(first_lanes)
                delta = jnp.sum(jnp.where(mine, product, 0.0), -1, keepdims=True)
                lse = lse_in[rows_at, pair * 2 + head : pair * 2 + head + 1]
                prob = jnp.exp(scores[head] + bias[rows_at, :seen] - lse)
                score_grads.append((prob * (prob_grads[head] - delta)).astype(BF))
                probs.append(prob.astype(BF))
            value_parts.append(mul_tn(jnp.concatenate(probs), jnp.concatenate(head_grads)))
            stacked = jnp.concatenate(score_grads)
            key_parts.append(mul_tn(stacked, jnp.concatenate(head_queries)))
            wide = jnp.concatenate(score_grads, axis=1)
            head_keys = jnp.concatenate([key * scaled[0], key * scaled[1]])
            query_parts.append(mul_nn(wide, head_keys))
        query_grads.append(jnp.concatenate(query_parts).astype(BF))
        key_grads.append(add_rows(key_parts).astype(BF))
        value_grads.append(add_rows(value_parts).astype(BF))
    query_grad = jnp.concatenate(query_grads, axis=1)
    key_grad = jnp.concatenate(key_grads, axis=1)
    value_grad = jnp.concatenate(value_grads, axis=1)

    @pl.when(step < steps // 2)
    def _():
        send_out[0], send_out[1], send_out[2] = query_grad, key_grad, value_grad

    @pl.when(step >= steps // 2)
    def _():
        keep_out[0], keep_out[1], keep_out[2] = query_grad, key_grad, value_grad

    if causal:
        return
    total[...] += mul_nt(query_grad, w_query[...])

    @pl.when(step == steps - 1)
    def _():
        norm_out[...] = jnp.zeros_like(norm_out)
        half = width // 2
        is_low = core[0] == 0

        def block(at):
            grad, gain_term, bias_term = normalize_back(
                ALPHA * grad_in[at, :] + total[at, :],
                normal_in[at, :],
                inverse_in[at, :],
                norms[0:1, :],
            )
            norm_out[0:1, :] += gain_term
            norm_out[1:2, :] += bias_term
            grad_out[at, :] = grad
            low_out[at, :] = grad.astype(BF)
            left, right = grad[:, :half], grad[:, half:]
            keep_low[at, :] = jnp.where(is_low, left, right).astype(BF)
            send_low[at, :] = jnp.where(is_low, right, left).astype(BF)

        by_rows(rows, 128, block)


def project_back_body(items, core, send, keep, *refs):
    weights = refs[: len(items)]
    rest = refs[len(items) :]
    total = rest[-1]
    step = pl.program_id(0)
    steps = pl.num_programs(0)
    joined_weights = jnp.concatenate([weight[...] for weight in weights], axis=1)

    @pl.when(step == 0)
    def _():
        total[...] = jnp.zeros_like(total)

    for source, first in ((send, 0), (keep, steps // 2)):

        @pl.when((step >= first) & (step < first + steps // 2))
        def _():
            joined = jnp.concatenate([source[item] for item in items], axis=1)
            total[...] += mul_nt(joined, joined_weights)

    @pl.when(step == steps - 1)
    def _():
        if len(rest) == 3 and rest[0].dtype == F32:
            grad_in, out = rest[:2]

            def block(at):
                out[at, :] = (ALPHA * grad_in[at, :] + total[at, :]).astype(BF)

            by_rows(out.shape[0], 64, block)
        else:
            own, other = rest[:2]
            rows = own.shape[0]
            own[...] = total[:rows, :].astype(BF)
            other[...] = total[rows:, :].astype(BF)


def project_back(core, send, keep, items, weights, grad=None):
    count, rows, half = send.shape
    width = weights[0].shape[0]
    steps = 2 * half // GROUP
    in_specs = [
        pl.BlockSpec((count, rows, GROUP), lambda s, _: (0, 0, jnp.minimum(s, steps // 2 - 1))),
        pl.BlockSpec((count, rows, GROUP), lambda s, _: (0, 0, jnp.maximum(s - steps // 2, 0))),
    ]
    columns = pl.BlockSpec((width, GROUP), lambda s, core: (0, send_first(s, steps, core)))
    in_specs += [columns] * len(weights)
    extra = [] if grad is None else [grad]
    in_specs += [whole(item.shape) for item in extra]
    outs = [(rows, width)] if extra else [(rows // 2, width)] * 2
    call = kernel_call(
        partial(project_back_body, items),
        (steps,),
        in_specs,
        [whole(out) for out in outs],
        [shape_of(out, BF) for out in outs],
        [pltpu.VMEM((rows, width), F32)],
        0,
        scalars=1,
    )
    return call(core, send, keep, *weights, *extra)


def attention_backward(causal, core, row_seg, key_seg, low_grad, w_out, saved, extra):
    rows, width = low_grad.shape
    keys = key_seg.shape[0]
    steps = width // GROUP
    half = steps // 2

    def block(shape, spread):
        def index(s, core):
            group = send_first(s, steps, core)
            return (group, 0) if spread == 0 else (0, group)

        return pl.BlockSpec(shape, index)

    row_block = block((rows, GROUP), 1)
    key_block = block((keys, GROUP), 1)
    columns = block((width, GROUP), 1)
    in_specs = [
        whole((1, rows)),
        whole((1, keys)),
        whole((rows, width)),
        block((GROUP, width), 0),
        row_block,
        key_block,
        key_block,
        row_block,
        block((rows, PAIR), 1),
    ]
    if not causal:
        in_specs += [columns]
        in_specs += [pl.BlockSpec((rows // steps, width), lambda s, _: (s, 0))] * 2
    in_specs += [whole(item.shape) for item in extra[3:]]
    out_specs = [
        pl.BlockSpec((3, rows, GROUP), lambda s, _: (0, 0, jnp.minimum(s, half - 1))),
        pl.BlockSpec((3, rows, GROUP), lambda s, _: (0, 0, jnp.maximum(s - half, 0))),
    ]
    out_shape = [shape_of((3, rows, width // 2), BF)] * 2
    scratch = [pltpu.VMEM((rows, keys), F32)]
    if not causal:
        out_specs += [whole((rows, width))] * 2 + [whole((rows, width // 2))] * 2
        out_specs += [whole((2, width))]
        out_shape += [
            shape_of((rows, width), F32),
            shape_of((rows, width), BF),
            shape_of((rows, width // 2), BF),
            shape_of((rows, width // 2), BF),
            shape_of((2, width), F32),
        ]
        scratch += [pltpu.VMEM((rows, width), F32)] * 3
    call = kernel_call(
        partial(backward_body, causal),
        (steps,),
        in_specs,
        out_specs,
        out_shape,
        scratch,
        44,
        scalars=1,
    )
    return call(
        core,
        row_seg.reshape(1, rows),
        key_seg.reshape(1, keys),
        low_grad,
        w_out,
        *saved,
        *extra,
    )


def swap_mem(tensor):
    return lax.ppermute(tensor, "mem", [(0, 1), (1, 0)])


def tie(value, *after):
    return lax.optimization_barrier((value, after))[0]


def beside(outputs, arrays):
    return lax.optimization_barrier((outputs, arrays))


def during(outputs, *chains):
    outputs, terms = lax.optimization_barrier((outputs, [chain.terms for chain in chains]))
    for chain, items in zip(chains, terms):
        chain.terms = items
    return outputs


class Plan:
    def __init__(self, steps, row_count):
        self.steps = steps
        self.row_count = row_count
        sizes = [self.pieces(step) for step in steps]
        self.relative, self.fixed = [], []
        for k in range(row_count):
            mask = fixed = 0
            rest = row_count
            for step, size in zip(steps, sizes):
                rest //= size
                digit = k // rest % size
                if step == "group":
                    fixed = digit << 2
                elif step == "plane":
                    mask |= digit
                else:
                    mask |= digit << step
            self.relative.append(mask)
            self.fixed.append(fixed)
        self.groups = [list(range(low, row_count, 4)) for low in range(4)]

    def pieces(self, step):
        if step == "group":
            return self.row_count // 4
        return 4 if step == "plane" else 2

    def first_pieces(self):
        return 1 if self.steps[0] == "group" else self.pieces(self.steps[0])

    def block_at(self, chip, k):
        own = (chip & 3) if "group" in self.steps else chip
        return (own ^ self.relative[k]) | self.fixed[k]

    def place_of(self, chip, block):
        own = (chip & 3) if "group" in self.steps else chip
        apart = own ^ block
        place = 0
        for step in self.steps:
            size = self.pieces(step)
            if step == "group":
                digit = apart >> 2
            elif step == "plane":
                digit = apart & 3
            else:
                digit = (apart >> step) & 1
            place = place * size + digit
        return place

    def at_places(self, chip):
        own = (chip & 3) if "group" in self.steps else chip
        return (own ^ jnp.asarray(self.relative, jnp.int32)) | jnp.asarray(self.fixed, jnp.int32)

    def permute(self, tensor, mask):
        pairs = [(i, i ^ mask) for i in range(self.row_count)]
        return lax.ppermute(tensor, "row", pairs)

    def group_sum(self, tensor):
        return lax.psum_scatter(
            tensor, "row", scatter_dimension=0, tiled=True, axis_index_groups=self.groups
        )


def group_sum_joined(plan, tensors, lanes):
    count = plan.row_count // 4
    pieces, sizes = [], []
    for tensor in tensors:
        blocks = tensor.reshape(count, -1, tensor.shape[1])
        sizes.append(blocks.shape[1:])
        pieces += [blocks[:, :, at : at + lanes] for at in range(0, blocks.shape[2], lanes)]
    joined = jnp.concatenate(pieces, axis=1)
    return joined, sizes, plan.group_sum(joined)[0]


def parted(summed, sizes, lanes):
    outs, at = [], 0
    for rows, width in sizes:
        parts = []
        for _ in range(width // lanes):
            parts.append(summed[at : at + rows])
            at += rows
        outs.append(jnp.concatenate(parts, axis=1) if len(parts) > 1 else parts[0])
    return outs


class Chain:
    def __init__(self, plan, blocks):
        self.plan = plan
        self.left = list(plan.steps)
        self.launch(list(blocks))

    def launch(self, pieces):
        step = self.left.pop(0)
        if step == "group":
            self.sent = pieces
            self.terms = [self.plan.group_sum(pieces[0])]
            return
        self.sent = pieces[1:]
        masks = [1, 2, 3] if step == "plane" else [1 << step]
        got = [self.plan.permute(piece, mask) for piece, mask in zip(self.sent, masks)]
        self.terms = [pieces[0]] + got

    def hold(self, *after):
        got = self.terms[1:] if len(self.terms) > 1 else self.terms
        self.terms[-len(got) :] = tie(got, *after)

    def sum_rows(self, rows):
        total = self.terms[0][rows].astype(F32)
        for term in self.terms[1:]:
            total = total + term[rows].astype(F32)
        return total

    def merged(self):
        assert self.left.pop(0) == "group"
        return self.sum_rows(slice(None)).astype(BF)

    def advance(self):
        step = self.left[0]
        count = 1 if step == "group" else self.plan.pieces(step)
        rows = self.terms[0].shape[0] // count
        self.launch(
            [self.sum_rows(slice(k * rows, (k + 1) * rows)).astype(BF) for k in range(count)]
        )

    def result(self):
        assert not self.left
        return self.sum_rows(slice(None))


def joined_chain(chains, plan):
    half = chains[0].terms[0].shape[0] // 2
    blocks = []
    for rows in (slice(None, half), slice(half, None)):
        blocks.append(jnp.concatenate([chain.sum_rows(rows) for chain in chains], axis=1).astype(BF))
    return Chain(plan, blocks)


def swap_mem(tensor):
    return lax.ppermute(tensor, "mem", [(0, 1), (1, 0)])


def weight_grads_body(spans, sources_count, grads_count, step_table, count, chip, *refs):
    sources = refs[: 2 * sources_count]
    grads = refs[2 * sources_count : 2 * (sources_count + grads_count)]
    outs = refs[2 * (sources_count + grads_count) : -1]
    whole_grad = refs[-1]
    step = pl.program_id(0)
    _, block_rows, lanes = whole_grad.shape
    joined = max(16 // block_rows, 1)
    for entry in sorted(set(step_table)):
        steps = [at for at, which in enumerate(step_table) if which == entry]

        @pl.when((step >= steps[0]) & (step <= steps[-1]))
        def _():
            own, other = sources[2 * entry[0] : 2 * entry[0] + 2]
            own_grad, other_grad = grads[2 * entry[1] : 2 * entry[1] + 2]
            grad = mul_tn(own[...], own_grad[0]) + mul_tn(other[...], other_grad[0])
            whole_grad[...] = grad.reshape(count, block_rows, lanes)

    at_out = 0
    for begin, chunks, pieces, plan in spans:
        targets = outs[at_out : at_out + pieces]
        at_out += pieces

        @pl.when((step >= begin) & (step < begin + chunks))
        def _():
            size = count // pieces
            for part, out in enumerate(targets):
                for k in range(0, size, joined):
                    places = range(part * size + k, part * size + k + joined)
                    blocks = [whole_grad[plan.block_at(chip[0], place)] for place in places]
                    rows = slice(k * block_rows, (k + joined) * block_rows)
                    out[rows, :] = jnp.concatenate(blocks).astype(BF)


def weight_grads(chip, sources, grads, step_table, chunk, outs, travelling=()):
    tokens, width = sources[0][0].shape
    count = outs[0][1].row_count
    steps = len(step_table)
    in_specs = [whole((tokens, width))] * (2 * len(sources))
    flat = [item for pair in sources for item in pair]
    for number, pair in enumerate(grads):
        pair = [item if item.ndim == 3 else item[None] for item in pair]
        flat += pair
        across = pair[0].shape[2] // chunk
        mine = [at for at, which in enumerate(step_table) if which[1] == number]

        def index(i, _, first=mine[0], last=mine[-1], across=across):
            at = jnp.clip(i, first, last) - first
            return (at // across, 0, at % across)

        in_specs += [pl.BlockSpec((1, tokens, chunk), index)] * 2
    out_specs, out_shape, spans = [], [], []
    begin = 0
    for chunks, plan in outs:
        pieces = plan.first_pieces()

        def index(i, _, begin=begin, chunks=chunks):
            return (0, jnp.clip(i - begin, 0, chunks - 1))

        for _ in range(pieces):
            out_specs.append(pl.BlockSpec((width // pieces, chunk), index))
            out_shape.append(shape_of((width // pieces, chunk * chunks), BF))
        spans.append((begin, chunks, pieces, plan))
        begin += chunks
    call = kernel_call(
        partial(weight_grads_body, spans, len(sources), len(grads), step_table, count),
        (steps,),
        in_specs,
        out_specs,
        out_shape,
        [pltpu.VMEM((count, width // count, chunk), F32)],
        16,
        scalars=1,
    )
    results = during(call(chip.reshape(1), *flat), *travelling)
    chains, at = [], 0
    for _, _, pieces, plan in spans:
        chains.append(Chain(plan, results[at : at + pieces]))
        at += pieces
    return chains


def wide_grads_body(plans, chip, own, other, own_grad, other_grad, *outs):
    step = pl.program_id(0)
    chains = len(outs) // 2
    lanes = outs[0].shape[1]
    block_rows = outs[0].shape[0] * 2 // plans[0].row_count
    blocks = own.shape[1] // block_rows
    size = outs[0].shape[0] // block_rows
    grad = mul_tn(own[...], own_grad[...]) + mul_tn(other[...], other_grad[...])
    grad = grad.astype(BF)
    for block in range(blocks):
        for chain in range(chains):
            part = grad[block * block_rows : (block + 1) * block_rows]
            part = part[:, chain * lanes : (chain + 1) * lanes]
            place = plans[chain].place_of(chip[0], step * blocks + block)
            for half in range(2):

                @pl.when((place >= half * size) & (place < (half + 1) * size))
                def _():
                    row = pl.multiple_of((place - half * size) * block_rows, block_rows)
                    outs[2 * chain + half][pl.ds(row, block_rows), :] = part


def wide_grads(chip, own, other, own_grad, other_grad, plans):
    tokens, width = own.shape
    lanes = own_grad.shape[1]
    chunk = 512
    source = pl.BlockSpec((tokens, chunk), lambda i, _: (0, i))
    out = (width // 2, lanes // len(plans))
    call = kernel_call(
        partial(wide_grads_body, plans),
        (width // chunk,),
        [source] * 2 + [whole((tokens, lanes))] * 2,
        [whole(out)] * (2 * len(plans)),
        [shape_of(out, BF)] * (2 * len(plans)),
        [],
        20,
        scalars=1,
    )
    results = call(chip.reshape(1), own, other, own_grad, other_grad)
    return [Chain(plan, results[2 * at : 2 * at + 2]) for at, plan in enumerate(plans)]


def shards(
    row_count,
    inputs,
    memory,
    target_seg,
    memory_seg,
    self_query,
    self_key,
    self_value,
    self_out,
    cross_query,
    cross_key,
    cross_value,
    cross_out,
    expand_weight,
    contract_weight,
    norm_params,
    out_grad,
):
    core = lax.axis_index("mem").astype(jnp.int32).reshape(1)
    chip = lax.axis_index("row").astype(jnp.int32)
    upper = list(range(2, row_count.bit_length() - 1))
    plan_x = Plan([0, 1, "group"], row_count)
    plan_y = Plan([1, 0, "group"], row_count)
    group_first = Plan(["group", 0, 1], row_count)
    last_x = Plan([0, 1] + upper, row_count)
    last_y = Plan([1, 0] + upper, row_count)
    rest = Plan(upper, row_count)

    self_saved = attention_forward(
        True,
        target_seg,
        target_seg,
        inputs,
        (),
        (self_query, self_key, self_value, self_out),
        norm_params,
    )
    self_saved, (other_memory, other_seg) = beside(
        self_saved, (swap_mem(memory), swap_mem(memory_seg))
    )
    pair_seg = jnp.concatenate([memory_seg, other_seg])
    other_inputs = swap_mem(inputs)
    self_o, normal_one, inverse_one, low_one = self_saved[3], *self_saved[5:]
    cross_saved = attention_forward(
        False,
        target_seg,
        pair_seg,
        low_one,
        (normal_one, memory, other_memory),
        (cross_query, cross_key, cross_value, cross_out),
        norm_params,
    )
    cross_saved, (other_inputs, other_self_o, other_one) = beside(
        cross_saved, (other_inputs, swap_mem(self_o), swap_mem(low_one))
    )
    cross_o, normal_two, inverse_two, low_two = cross_saved[3], *cross_saved[5:]
    outputs = feed_forward(
        core, low_two, normal_two, expand_weight, contract_weight, norm_params, out_grad
    )
    outputs, (other_cross_o, other_two) = beside(outputs, (swap_mem(cross_o), swap_mem(low_two)))
    (active, slope, layer_out, grad_three, low_three, send_three, keep_three, norm_three) = outputs
    outputs = feed_backward(False, core, low_three, contract_weight, slope, expand_weight)
    (send_wide, part_two), (other_active, got_three) = beside(
        outputs, (swap_mem(active), swap_mem(send_three))
    )

    half = keep_three.shape[1]
    contract_x, contract_y = wide_grads(
        chip, active, other_active, keep_three, got_three, [plan_x, plan_y]
    )
    outputs = feed_backward(
        True,
        core,
        tie(low_three, contract_x.sent, contract_y.sent),
        contract_weight,
        slope,
        expand_weight,
        part_two,
        grad_three,
        normal_two,
        inverse_two,
        norm_params,
    )
    outputs, got_wide = beside(outputs, swap_mem(send_wide))
    (keep_wide, grad_two, low_grad_two, send_two, keep_two, norm_two) = outputs
    expand, expand_x = weight_grads(
        chip,
        [(low_two, other_two)],
        [(keep_wide, got_wide)],
        [(0, 0)] * 4,
        512,
        [(2, group_first), (2, plan_x)],
        (contract_x, contract_y),
    )
    contract_x.advance()
    contract_y.advance()
    got_two = swap_mem(send_two)

    outputs = attention_backward(
        False,
        core,
        target_seg,
        pair_seg,
        tie(low_grad_two, expand.sent, expand_x.sent, contract_x.sent, contract_y.sent),
        cross_out,
        (cross_saved[0], cross_saved[1], cross_saved[2], cross_o, cross_saved[4]),
        (cross_query, grad_two, normal_one, inverse_one, norm_params),
    )
    (send_c, keep_c, grad_one, low_grad_one, send_one, keep_one, norm_one) = during(
        outputs, contract_x, contract_y, expand_x
    )
    norm_grad = jnp.concatenate([norm_one, norm_two, norm_three])
    norm_grad = norm_grad.reshape(2, 3, norm_grad.shape[1])
    norm_half = norm_grad[core[0]] + swap_mem(norm_grad[1 - core[0]])
    got_c = swap_mem(send_c)
    got_one = swap_mem(send_one)
    contract_merged = [chain.merged() for chain in (contract_x, contract_y)]
    expand_x.advance()
    block_rows = inputs.shape[1] // row_count
    norm_blocks = norm_half.reshape(3, row_count, block_rows).transpose(1, 0, 2)
    norm_blocks = jnp.take(norm_blocks, last_y.at_places(chip), axis=0)
    norm_chain = Chain(last_y, norm_blocks.reshape((2, -1) + norm_blocks.shape[1:]).astype(BF))
    pair_memory = jnp.concatenate([memory, other_memory])
    turned_memory = jnp.concatenate([other_memory, memory])
    cross_x, cross_y = weight_grads(
        chip,
        [
            (tie(cross_o, contract_merged, expand_x.sent, norm_chain.sent), other_cross_o),
            (low_one, other_one),
            (pair_memory, turned_memory),
            (self_o, other_self_o),
        ],
        [(keep_two, got_two), (keep_c, got_c), (keep_one, got_one)],
        [(0, 0)] * 2 + [(1, 1)] * 2 + [(2, 1)] * 4 + [(3, 2)] * 2,
        256,
        [(5, last_x), (5, last_y)],
        (expand_x, expand, norm_chain),
    )
    merged = contract_merged + [expand_x.merged()]
    joined, forward_sizes, forward_sum = group_sum_joined(plan_x, merged, half // 2)
    expand.advance()
    norm_chain.advance()

    mem_own, mem_send = project_back(
        core, tie(send_c, cross_x.sent, cross_y.sent), keep_c, (1, 2), (cross_key, cross_value)
    )
    outputs = attention_backward(
        True,
        core,
        target_seg,
        target_seg,
        tie(low_grad_one, mem_own, expand.sent, joined, norm_chain.sent),
        self_out,
        (self_saved[0], self_saved[1], self_saved[2], self_o, self_saved[4]),
        (),
    )
    send_s, keep_s = during(outputs, cross_x, cross_y, expand, norm_chain)
    got_s = swap_mem(send_s)
    cross_x.advance()
    cross_y.advance()
    expand.advance()
    norm_chain.advance()
    self_chains = weight_grads(
        chip,
        [(tie(inputs, cross_x.sent, cross_y.sent, expand.sent, norm_chain.sent), other_inputs)],
        [(keep_s, got_s)],
        [(0, 0)] * 6,
        256,
        [(3, last_x), (3, last_y)],
        (cross_x, cross_y, expand),
    )
    started = [chain.sent for chain in self_chains]
    for chain in (cross_x, cross_y):
        chain.hold(started, forward_sum)
    cross_chain = joined_chain((cross_x, cross_y), rest)
    (input_grad,) = project_back(
        core,
        tie(send_s, cross_chain.sent),
        keep_s,
        (0, 1, 2),
        (self_query, self_key, self_value),
        grad_one,
    )
    for chain in self_chains + [cross_chain]:
        chain.hold(input_grad)
        chain.advance()
    self_chain = joined_chain(self_chains, rest)
    norm_chain.hold(self_chain.sent)
    norm_chain.advance()
    mem_send, forward_sum, expand.terms, cross_chain.terms = tie(
        (mem_send, forward_sum, expand.terms, cross_chain.terms), self_chain.sent
    )
    memory_grad = (mem_own.astype(F32) + swap_mem(mem_send).astype(F32)).astype(BF)
    forward_parts = [part.astype(F32) for part in parted(forward_sum, forward_sizes, half // 2)]
    contract_result = jnp.concatenate(forward_parts[:2], axis=1)
    expand_result = jnp.concatenate([expand.result(), forward_parts[2]], axis=1)
    self_chain.hold(contract_result, expand_result)
    for chain in (self_chain, cross_chain, norm_chain):
        while chain.left:
            chain.advance()
    self_sum, cross_sum = self_chain.result(), cross_chain.result()
    own_lanes = self_out.shape[1] // 2
    cross_parts = [cross_sum[:, at * own_lanes : (at + 1) * own_lanes] for at in range(5)]
    return (
        layer_out,
        input_grad,
        memory_grad,
        self_sum[:, :own_lanes],
        self_sum[:, own_lanes : 2 * own_lanes],
        self_sum[:, 2 * own_lanes :],
        cross_parts[4],
        cross_parts[1],
        cross_parts[2],
        cross_parts[3],
        cross_parts[0],
        expand_result,
        contract_result,
        norm_chain.result()[0],
    )


def solution(mesh):
    split_rows = P(("row", "mem"), None)
    split_ids = P(("row", "mem"))
    in_specs = (split_rows, split_rows, split_ids, split_ids) + (P(),) * 11 + (split_rows,)
    out_specs = (split_rows,) * 3 + (P("row", "mem"),) * 10 + (P("mem", "row"),)
    return jax.shard_map(
        partial(shards, mesh.shape["row"]),
        mesh=mesh,
        in_specs=in_specs,
        out_specs=out_specs,
        check_vma=False,
    )
```
